32 devices in a mesh: item: 2 (over core), row: 4 (over y, x), col: 4 (over z).
Axes of the slice: x: 2, y: 2, z: 4, core: 2. Of those that a mesh axis runs over, the one named last changes fastest.
Arguments:
- latents: bfloat16 [2, 2, 16, 16, 3072], P('item', None, 'row', 'col'), may hold values from -640 to 640
- prompt_rows: bfloat16 [2, 226, 3072], P('item'), may hold values from -640 to 640
- peg_weight: bfloat16 [3, 3, 3072], replicated, may hold values from -1 to 1
- modulation_weight: bfloat16 [512, 6144], P(None, 'col'), may hold values from -0.5 to 0.5
- qkv_weight: bfloat16 [3072, 3, 2048], P(('item', 'row'), None, 'col'), may hold values from -3 to 3
- text_len: int32 [2], P('item'), may hold values from 56 to 226, as said below
- timestep: int32 [2], P('item'), may hold values from 0 to 999
Outputs:
- attended: bfloat16 [2, 2, 16, 16, 2048], P('item', None, 'row', None, 'col')
The draws below stay inside these ranges and needn't reach their ends.
Inputs may be any that keep to these rules, and one draw needn't show every extreme that they name: `text_len`: one item has all 226 text tokens valid; the others have fewer.
All inputs are finite; a program needn't handle non-finite values.
Results may differ from the reference program's by a relative error of at most 0.02.
Values may be sent and summed in bfloat16 or wider, within the bound.
A program may use at most 64 MiB of HBM per device.

```python
import math
import jax
import jax.numpy as jnp
from jax import lax

D = 3072
HD = 64
TEXT = 226
TEMB = 512
H = 32
FR = 2
ITEMS = 2
GH = 16
GW = 16
NLAT = 512
N_ROW = 4


def scaled_rows(key, shape):
    first, second, third = jax.random.split(key, 3)
    base = jnp.clip(jax.random.normal(first, shape, jnp.float32), -4.0, 4.0)
    row_scale = jnp.exp(jax.random.uniform(second, shape[:-1] + (1,), jnp.float32, 0.0, math.log(10.0)))
    col_scale = jnp.exp(jax.random.uniform(third, shape[-1:], jnp.float32, 0.0, math.log(10.0)))
    return base * row_scale * col_scale


def draw_latents(key, part):
    return scaled_rows(jax.random.fold_in(key, 11), (ITEMS, FR, GH, GW, D)).astype(jnp.bfloat16)


def draw_prompt_rows(key, part):
    return scaled_rows(jax.random.fold_in(key, 23), (ITEMS, TEXT, D)).astype(jnp.bfloat16)


def draw_qkv_weight(key, part):
    first, second, third = jax.random.split(jax.random.fold_in(key, 37), 3)
    shape = (D, H * HD)
    norm_scale = 1.0 / math.sqrt(D)
    query_part = jnp.clip(jax.random.normal(first, shape, jnp.float32), -5.0, 5.0) * (1.7 * norm_scale)
    key_part = jnp.clip(jax.random.normal(second, shape, jnp.float32), -5.0, 5.0) * (1.7 * norm_scale)
    value_part = jnp.clip(jax.random.normal(third, shape, jnp.float32), -5.0, 5.0) * norm_scale
    return jnp.stack([query_part, key_part, value_part], axis=1).astype(jnp.bfloat16)


def draw_text_len(key, part):
    first, second = jax.random.split(jax.random.fold_in(key, 53))
    others = jax.random.randint(first, (ITEMS - 1,), TEXT // 4, TEXT, dtype=jnp.int32)
    lengths = jnp.concatenate([jnp.full((1,), TEXT, dtype=jnp.int32), others])
    return jax.random.permutation(second, lengths)


def shard_levels(rng, extent, shards, smallest, high):
    gain, own = 1.0, jax.random.fold_in(rng, 6)
    for axis_at, blocks in shards:
        heights = jnp.exp(jax.random.uniform(jax.random.fold_in(own, axis_at), (blocks,), jnp.float32, smallest / len(shards), high / len(shards)))
        gain = gain * jnp.repeat(heights, extent[axis_at] // blocks).reshape([-1 if axis == axis_at else 1 for axis in range(len(extent))])
    return gain


def gaussian(stream_key, extent, width, most, cuts=(), kind=jnp.bfloat16):
    entries = jax.random.normal(stream_key, extent, jnp.float32) * width
    if len(cuts) > 0:
        entries = shard_levels(stream_key, extent, cuts, -0.22, 0.18) * entries
    return jnp.clip(entries, min=-most, max=most).astype(kind)


def setup_inputs(seed: int = 0) -> dict:
    seeds = jax.random.split(jax.random.key(seed), 8)
    latents = draw_latents(jax.random.fold_in(seeds[7], 71), 0)
    prompt_rows = draw_prompt_rows(jax.random.fold_in(seeds[7], 71), 0)
    peg_weight = gaussian(seeds[2], (3, 3, D), 0.2, 1.0)
    modulation_weight = gaussian(seeds[3], (TEMB, 2 * D), (TEMB // 4) ** -0.5, 0.5, ((1, 4),))
    qkv_weight = draw_qkv_weight(jax.random.fold_in(seeds[7], 71), 0)
    text_len = draw_text_len(jax.random.fold_in(seeds[7], 71), 0)
    timestep = jax.random.randint(seeds[6], (ITEMS,), 0, 1000).astype(jnp.int32)
    return dict(latents=latents, prompt_rows=prompt_rows, peg_weight=peg_weight, modulation_weight=modulation_weight, qkv_weight=qkv_weight, text_len=text_len, timestep=timestep)


def time_angles(step, count):
    half = count // 2
    freqs = jnp.exp(-math.log(10000.0) * jnp.arange(half, dtype=jnp.float32) / half)
    angle = step.astype(jnp.float32) * freqs
    return jnp.concatenate([jnp.cos(angle), jnp.sin(angle)])

def modulate(rows, shift, scale):
    values = rows.astype(jnp.float32)
    center = lax.optimization_barrier(jnp.mean(values, axis=-1, keepdims=True))
    centered = values - center
    spread = lax.optimization_barrier(jnp.mean(centered * centered, axis=-1, keepdims=True))
    return (centered * lax.rsqrt(spread + 1e-06) * (1.0 + scale) + shift).astype(jnp.bfloat16)

def reference(latents, prompt_rows, peg_weight, modulation_weight, qkv_weight, text_len, timestep):
    flat_weight = qkv_weight.reshape(D, 3 * H * HD)
    results = []
    for item in range(ITEMS):
        frames = latents[item].astype(jnp.float32)
        padded = jnp.pad(frames, ((0, 0), (1, 1), (1, 1), (0, 0)))
        summed = frames
        for row_tap in range(3):
            for col_tap in range(3):
                summed = summed + padded[:, row_tap:row_tap + GH, col_tap:col_tap + GW, :] * peg_weight[row_tap, col_tap].astype(jnp.float32)
        convolved = summed.astype(jnp.bfloat16)
        activation = jax.nn.silu(time_angles(timestep[item], TEMB)).astype(jnp.bfloat16)
        modulation = jnp.dot(activation[None, :], modulation_weight, preferred_element_type=jnp.float32)[0]
        shift = modulation[:D]
        scale = modulation[D:]
        normed = modulate(convolved.reshape(NLAT, D), shift, scale)
        text_normed = modulate(prompt_rows[item], shift, scale)
        latent_qkv = jnp.dot(normed, flat_weight, preferred_element_type=jnp.float32).astype(jnp.bfloat16).reshape(NLAT, 3, H, HD)
        text_qkv = jnp.dot(text_normed, flat_weight, preferred_element_type=jnp.float32).astype(jnp.bfloat16).reshape(TEXT, 3, H, HD)
        key_all = jnp.concatenate([text_qkv[:, 1], latent_qkv[:, 1]], axis=0)
        value_all = jnp.concatenate([text_qkv[:, 2], latent_qkv[:, 2]], axis=0)
        positions = jnp.arange(TEXT + NLAT, dtype=jnp.int32)
        valid = (positions >= TEXT) | (positions < text_len[item])
        query_heads = jnp.transpose(latent_qkv[:, 0], (1, 0, 2))
        key_heads = jnp.transpose(key_all, (1, 0, 2))
        value_heads = jnp.transpose(value_all, (1, 0, 2))

        def one_head(triple):
            queries, key_rows, value_rows = triple
            key_float = key_rows.astype(jnp.float32)

            def one_group(block):
                scores = jnp.dot(block.astype(jnp.float32), key_float.T, precision=lax.Precision.HIGHEST) * 0.125
                scores = jnp.where(valid[None, :], scores, -jnp.inf)
                weights = jnp.exp(scores - lax.optimization_barrier(jnp.max(scores, axis=1, keepdims=True)))
                weighted = jnp.dot(weights.astype(jnp.bfloat16), value_rows, preferred_element_type=jnp.float32)
                return weighted / lax.optimization_barrier(jnp.sum(weights, axis=1, keepdims=True))
            grouped = lax.map(one_group, queries.reshape(N_ROW, NLAT // N_ROW, HD))
            return grouped.reshape(NLAT, HD)
        head_out = lax.map(one_head, (query_heads, key_heads, value_heads))
        attended = jnp.transpose(head_out, (1, 0, 2)).reshape(FR, GH, GW, H * HD).astype(jnp.bfloat16)
        results.append(attended)
    return jnp.stack(results, axis=0)
```

```python
import functools
import math

import jax
import jax.numpy as jnp
from jax import lax
from jax.experimental import pallas as pl
from jax.experimental.pallas import tpu as pltpu
from jax.sharding import PartitionSpec as P

HD = 64
MESH = pl.DeviceIdType.MESH
VMEM = pltpu.VMEM


def with_halo(block, sides, width):
    for axis, dim in sides:
        count = lax.axis_size(axis)
        forward = [(i, i + 1) for i in range(count - 1)]
        backward = [(target, source) for source, target in forward]
        low = lax.ppermute(
            lax.slice_in_dim(block, block.shape[dim] - width, None, axis=dim), axis, forward
        )
        high = lax.ppermute(lax.slice_in_dim(block, 0, width, axis=dim), axis, backward)
        block = jnp.concatenate([low, block, high], axis=dim)
    return block


def time_angles(step, count):
    half = count // 2
    freqs = jnp.exp(-math.log(10000.0) * jnp.arange(half, dtype=jnp.float32) / half)
    angle = step.astype(jnp.float32) * freqs
    return jnp.concatenate([jnp.cos(angle), jnp.sin(angle)])


def modulate(rows, shift, scale):
    values = rows.astype(jnp.float32)
    center = jnp.mean(values, axis=-1, keepdims=True)
    centered = values - center
    spread = jnp.mean(centered * centered, axis=-1, keepdims=True)
    return (centered * lax.rsqrt(spread + 1e-06) * (1.0 + scale) + shift).astype(jnp.bfloat16)


def absorb(carry, queries, key_rows, value_rows, valid):
    running_max, running_sum, weighted = carry
    count = key_rows.shape[0]
    heads = queries.shape[1]
    key_heads = key_rows.reshape(count, heads, HD)
    value_heads = value_rows.reshape(count, heads, HD)
    scores = (
        jnp.einsum("rhd,bhd->rhb", queries, key_heads, preferred_element_type=jnp.float32) * 0.125
    )
    if valid is not None:
        scores = jnp.where(valid[None, None, :], scores, -jnp.inf)
    newest = jnp.maximum(running_max, jnp.max(scores, axis=-1))
    weights = jnp.exp(scores - newest[..., None])
    shrink_by = jnp.exp(running_max - newest)
    running_sum = running_sum * shrink_by + jnp.sum(weights, axis=-1)
    weighted = weighted * shrink_by[..., None] + jnp.einsum(
        "rhb,bhd->rhd",
        weights.astype(jnp.bfloat16),
        value_heads,
        preferred_element_type=jnp.float32,
    )
    return (newest, running_sum, weighted)


def on_device_general(latents, prompt_rows, peg_weight, modulation_weight, qkv_weight, text_len, timestep):
    tile_h = latents.shape[2]
    tile_w = latents.shape[3]
    width = latents.shape[4]
    padded = with_halo(latents, (("row", 2), ("col", 3)), 1)
    summed = latents.astype(jnp.float32)
    for row_tap in range(3):
        for col_tap in range(3):
            summed = summed + padded[
                :, :, row_tap : row_tap + tile_h, col_tap : col_tap + tile_w, :
            ].astype(jnp.float32) * peg_weight[row_tap, col_tap].astype(jnp.float32)
    convolved = summed.astype(jnp.bfloat16)
    activation = jax.nn.silu(time_angles(timestep[0], modulation_weight.shape[0])).astype(
        jnp.bfloat16
    )
    own_columns = jnp.dot(
        activation[None, :], modulation_weight, preferred_element_type=jnp.float32
    )
    modulation = lax.all_gather(own_columns, "col", axis=1, tiled=True)[0]
    shift = modulation[:width]
    scale = modulation[width:]
    group_rows = lax.all_gather(modulate(convolved, shift, scale), "col", axis=3, tiled=True)
    frames = group_rows.shape[1]
    grid_w = group_rows.shape[3]
    flat_rows = group_rows.reshape(-1, width)
    row_count = flat_rows.shape[0]
    text_normed = modulate(prompt_rows[0], shift, scale)
    text_count = text_normed.shape[0]
    head_width = qkv_weight.shape[2]
    full_weight = lax.all_gather(qkv_weight, ("item", "row"), axis=0, tiled=True)
    latent_proj = jnp.einsum(
        "rd,dkc->rkc", flat_rows, full_weight, preferred_element_type=jnp.float32
    )
    text_proj = jnp.einsum(
        "rd,dkc->rkc", text_normed, full_weight, preferred_element_type=jnp.float32
    )
    latent_qkv = latent_proj.astype(jnp.bfloat16)
    text_qkv = text_proj.astype(jnp.bfloat16)
    heads = head_width // HD
    queries = latent_qkv[:, 0, :].reshape(row_count, heads, HD)
    local_keys = latent_qkv[:, 1, :]
    local_values = latent_qkv[:, 2, :]
    text_valid = jnp.arange(text_count, dtype=jnp.int32) < text_len[0]
    start_carry = (
        jnp.full((row_count, heads), -jnp.inf, jnp.float32),
        jnp.zeros((row_count, heads), jnp.float32),
        jnp.zeros((row_count, heads, HD), jnp.float32),
    )
    text_carry = absorb(start_carry, queries, text_qkv[:, 1, :], text_qkv[:, 2, :], text_valid)
    key_rows = lax.all_gather(local_keys, "row", axis=0, tiled=True)
    value_rows = lax.all_gather(local_values, "row", axis=0, tiled=True)
    total_rows = key_rows.shape[0]
    block_count = total_rows // row_count

    def one_block(state, pair):
        return (absorb(state, queries, pair[0], pair[1], None), None)

    state, unused = lax.scan(
        one_block,
        text_carry,
        (
            key_rows.reshape(block_count, row_count, head_width),
            value_rows.reshape(block_count, row_count, head_width),
        ),
    )
    running_max, running_sum, weighted = state
    attended = (weighted / running_sum[..., None]).astype(jnp.bfloat16)
    return attended.reshape(1, frames, tile_h, grid_w, head_width)


def centered_rows(values):
    center = jnp.mean(values, axis=-1, keepdims=True)
    centered = values - center
    spread = jnp.mean(centered * centered, axis=-1, keepdims=True)
    return centered * lax.rsqrt(spread + 1e-06)


def layer_kernel(
    sizes,
    len_ref,
    tile_ref,
    prompt_ref,
    act_ref,
    mod_ref,
    weight_ref,
    out_ref,
    mod_buf,
    affine,
    weights,
    text_in,
    send_x,
    grid_x,
    send_text,
    recv_text,
    own_text,
    send_part,
    recv_part,
    own_part,
    q_buf,
    k_buf,
    v_buf,
    send_out,
    recv_out,
    w_sems,
    mod_send,
    mod_recv,
    x_send,
    x_recv,
    z_send,
    z_recv,
    t_send,
    t_recv,
    p_send,
    p_recv,
    o_send,
    o_recv,
):
    rows, cols, text, padded_text, tile_w = sizes
    tokens, width = tile_ref.shape
    depth = weight_ref.shape[1]
    out_w = weight_ref.shape[2] // 3
    block = tokens * cols
    item = lax.axis_index("item")
    row = lax.axis_index("row")
    col = lax.axis_index("col")

    def row_peer(step):
        return lax.rem(row + step, rows)

    def col_peer(step):
        return lax.rem(col + step, cols)

    def remote(src, dst, send, recv, where):
        return pltpu.make_async_remote_copy(
            src_ref=src, dst_ref=dst, send_sem=send, recv_sem=recv, device_id=where, device_id_type=MESH
        )

    barrier = pltpu.get_barrier_semaphore()
    pl.semaphore_signal(barrier, inc=1, device_id={"item": 1 - item}, device_id_type=MESH)
    for step in range(1, rows):
        pl.semaphore_signal(barrier, inc=1, device_id={"row": row_peer(step)}, device_id_type=MESH)
    for step in range(1, cols):
        pl.semaphore_signal(barrier, inc=1, device_id={"col": col_peer(step)}, device_id_type=MESH)

    own_columns = jnp.dot(act_ref[...], mod_ref[...], preferred_element_type=jnp.float32)
    mod_buf[col] = own_columns[0:1, :]
    pl.semaphore_wait(barrier, rows + cols - 1)
    mod_copies = []
    for step in range(1, cols):
        copy = remote(
            mod_buf.at[col],
            mod_buf.at[col],
            mod_send.at[step - 1],
            mod_recv.at[step - 1],
            {"col": col_peer(step)},
        )
        copy.start()
        mod_copies.append(copy)
    weight_copy = remote(
        weight_ref,
        weights.at[:, pl.ds(depth, depth), :],
        w_sems.at[0],
        w_sems.at[1],
        {"item": 1 - item},
    )
    weight_copy.start()
    for dest in range(rows):
        weights[dest, 0:depth, :] = weight_ref[dest]
    tile_normal = centered_rows(tile_ref[...].astype(jnp.float32))
    for step in range(1, cols):
        remote(
            mod_buf.at[col],
            mod_buf.at[lax.rem(col - step + cols, cols)],
            mod_send.at[step - 1],
            mod_recv.at[step - 1],
            {"col": col_peer(step)},
        ).wait_recv()
    half = cols // 2
    piece = mod_buf.shape[2]
    for part in range(half):
        affine[0, :, part * piece : (part + 1) * piece] = mod_buf[part]
        affine[1, :, part * piece : (part + 1) * piece] = 1.0 + mod_buf[half + part]

    def depth_slices(dest):
        first = (item * rows + dest) * depth
        second = ((1 - item) * rows + dest) * depth
        return (pl.multiple_of(first, depth), pl.multiple_of(second, depth))

    text_in[0:tokens, :] = (tile_normal * affine[1] + affine[0]).astype(jnp.bfloat16)
    x_copies = []
    for step in range(1, rows):
        peer = row_peer(step)
        for order, start in enumerate(depth_slices(peer)):
            send_x[step - 1, :, order * depth : (order + 1) * depth] = text_in[
                0:tokens, pl.ds(start, depth)
            ]
        copy = remote(
            send_x.at[step - 1],
            grid_x.at[0, pl.ds(pl.multiple_of(row * tokens, tokens), tokens), :],
            x_send.at[step - 1],
            x_recv.at[step - 1],
            {"row": peer},
        )
        copy.start()
        x_copies.append(copy)
    own_slices = depth_slices(row)
    for order, start in enumerate(own_slices):
        grid_x[
            0, pl.ds(pl.multiple_of(row * tokens, tokens), tokens), order * depth : (order + 1) * depth
        ] = text_in[0:tokens, pl.ds(start, depth)]

    for step in range(1, rows):
        source = lax.rem(row - step + rows, rows)
        remote(
            send_x.at[step - 1],
            grid_x.at[0, pl.ds(pl.multiple_of(source * tokens, tokens), tokens), :],
            x_send.at[step - 1],
            x_recv.at[step - 1],
            {"row": row_peer(step)},
        ).wait_recv()
    z_copies = []
    for step in range(1, cols):
        copy = remote(
            grid_x.at[0], grid_x.at[step], z_send.at[step - 1], z_recv.at[step - 1], {"col": col_peer(step)}
        )
        copy.start()
        z_copies.append(copy)
    weight_copy.wait_recv()

    p_copies = []

    def latent_part(group):
        values = grid_x[group]
        for step in range(1, rows):
            peer = row_peer(step)
            send_part[group, step - 1] = jnp.dot(
                values, weights[peer], preferred_element_type=jnp.float32
            ).astype(jnp.bfloat16)
            copy = remote(
                send_part.at[group, step - 1],
                recv_part.at[group, step - 1],
                p_send.at[group, step - 1],
                p_recv.at[group, step - 1],
                {"row": peer},
            )
            copy.start()
            p_copies.append(copy)
        own_part[group] = jnp.dot(values, weights[row], preferred_element_type=jnp.float32)

    latent_part(0)

    scale_pieces = [affine[1, :, pl.ds(start, depth)] for start in own_slices]
    shift_pieces = [affine[0, :, pl.ds(start, depth)] for start in own_slices]
    for start_row in range(0, padded_text, 16):
        count = min(16, text - start_row)
        values = prompt_ref[start_row : start_row + count, :].astype(jnp.float32)
        center = jnp.mean(values, axis=-1, keepdims=True)
        centered = values - center
        spread = lax.rsqrt(jnp.mean(centered * centered, axis=-1, keepdims=True) + 1e-06)
        for order, start in enumerate(own_slices):
            part = prompt_ref[start_row : start_row + count, pl.ds(start, depth)].astype(jnp.float32)
            normed = (part - center) * spread * scale_pieces[order] + shift_pieces[order]
            if count < 16:
                normed = jnp.concatenate([normed, jnp.zeros((16 - count, depth), jnp.float32)], axis=0)
            text_in[start_row : start_row + 16, order * depth : (order + 1) * depth] = normed.astype(
                jnp.bfloat16
            )
    text_values = text_in[:, 0 : 2 * depth]
    t_copies = []
    for step in range(1, rows):
        peer = row_peer(step)
        send_text[step - 1] = jnp.dot(
            text_values, weights[peer, :, out_w:], preferred_element_type=jnp.float32
        ).astype(jnp.bfloat16)
        copy = remote(
            send_text.at[step - 1],
            recv_text.at[step - 1],
            t_send.at[step - 1],
            t_recv.at[step - 1],
            {"row": peer},
        )
        copy.start()
        t_copies.append(copy)
    own_text[...] = jnp.dot(text_values, weights[row, :, out_w:], preferred_element_type=jnp.float32)

    for group in range(1, cols):
        z_copies[group - 1].wait_recv()
        latent_part(group)

    for copy in t_copies:
        copy.wait_recv()
    total = own_text[...]
    for step in range(1, rows):
        total = total + recv_text[step - 1].astype(jnp.float32)
    k_buf[0:padded_text, :] = total[:, 0:out_w].astype(jnp.bfloat16)
    v_buf[0:padded_text, :] = total[:, out_w:].astype(jnp.bfloat16)
    for group in range(cols):
        for step in range(1, rows):
            p_copies[group * (rows - 1) + step - 1].wait_recv()
        total = own_part[group]
        for step in range(1, rows):
            total = total + recv_part[group, step - 1].astype(jnp.float32)
        rounded = total.astype(jnp.bfloat16)
        per_col = rows * tokens
        base = padded_text + group * per_col
        k_buf[base : base + per_col, :] = rounded[:, out_w : 2 * out_w]
        v_buf[base : base + per_col, :] = rounded[:, 2 * out_w :]
        for dest in range(rows):
            q_buf[dest, group * tokens : (group + 1) * tokens, :] = rounded[
                dest * tokens : (dest + 1) * tokens, 0:out_w
            ]

    at = lax.broadcasted_iota(jnp.int32, (block, block), 0)
    source = lax.broadcasted_iota(jnp.int32, (block, block), 1)
    group = source // tokens
    token = source - group * tokens
    line = token // tile_w
    place = token - line * tile_w
    owner = col - group
    owner = jnp.where(owner < 0, owner + cols, owner)
    target = (line * cols + owner) * tile_w + place
    permute = jnp.where(at == target, 1.0, 0.0).astype(jnp.bfloat16)
    keys = k_buf[...]
    vals = v_buf[...]
    position = lax.broadcasted_iota(jnp.int32, (1, keys.shape[0]), 1)
    valid = (position >= padded_text) | (position < len_ref[0])
    o_copies = []
    for step in list(range(1, rows)) + [0]:
        peer = row_peer(step)
        queries = jnp.dot(permute, q_buf[peer], preferred_element_type=jnp.float32).astype(jnp.bfloat16)
        outs = []
        for head in range(out_w // HD):
            lanes = slice(head * HD, (head + 1) * HD)
            scores = (
                lax.dot_general(
                    queries[:, lanes],
                    keys[:, lanes],
                    (((1,), (1,)), ((), ())),
                    preferred_element_type=jnp.float32,
                )
                * 0.125
            )
            scores = jnp.where(valid, scores, -jnp.inf)
            weight = jnp.exp(scores - jnp.max(scores, axis=-1, keepdims=True))
            total = jnp.sum(weight, axis=-1, keepdims=True)
            outs.append(
                jnp.dot(weight.astype(jnp.bfloat16), vals[:, lanes], preferred_element_type=jnp.float32)
                / total
            )
        result = jnp.concatenate(outs, axis=-1).astype(jnp.bfloat16)
        if step == 0:
            recv_out[row] = result
        else:
            send_out[step - 1] = result
            copy = remote(
                send_out.at[step - 1],
                recv_out.at[row],
                o_send.at[step - 1],
                o_recv.at[step - 1],
                {"row": peer},
            )
            copy.start()
            o_copies.append(copy)
    for step in range(1, rows):
        source = lax.rem(row - step + rows, rows)
        remote(
            send_out.at[step - 1],
            recv_out.at[source],
            o_send.at[step - 1],
            o_recv.at[step - 1],
            {"row": row_peer(step)},
        ).wait_recv()
    for source in range(rows):
        out_ref[:, source * out_w : (source + 1) * out_w] = recv_out[source]
    for copy in mod_copies + [weight_copy] + x_copies + z_copies + p_copies + t_copies + o_copies:
        copy.wait_send()


def on_device_fast(
    rows, cols, latents, prompt_rows, peg_weight, modulation_weight, qkv_weight, text_len, timestep
):
    frames, tile_h, tile_w, width = latents.shape[1:]
    padded = with_halo(latents, (("row", 2), ("col", 3)), 1)
    summed = latents.astype(jnp.float32)
    for row_tap in range(3):
        for col_tap in range(3):
            summed = summed + padded[
                :, :, row_tap : row_tap + tile_h, col_tap : col_tap + tile_w, :
            ].astype(jnp.float32) * peg_weight[row_tap, col_tap].astype(jnp.float32)
    tokens = frames * tile_h * tile_w
    tile = summed.astype(jnp.bfloat16).reshape(tokens, width)
    temb = modulation_weight.shape[0]
    activation = jax.nn.silu(time_angles(timestep[0], temb)).astype(jnp.bfloat16)
    activation = jnp.broadcast_to(activation[None, :], (16, temb))
    depth, parts, head_width = qkv_weight.shape
    out_w = head_width // rows
    by_dest = qkv_weight.reshape(depth, parts, rows, out_w).transpose(2, 0, 1, 3)
    by_dest = by_dest.reshape(rows, depth, parts * out_w)
    text = prompt_rows.shape[1]
    padded_text = -(-text // 16) * 16
    block = tokens * cols
    group_rows = tokens * rows
    bf16, f32 = jnp.bfloat16, jnp.float32
    dma = pltpu.SemaphoreType.DMA
    all_rows = padded_text + group_rows * cols
    attended = pl.pallas_call(
        functools.partial(layer_kernel, (rows, cols, text, padded_text, tile_w)),
        out_shape=jax.ShapeDtypeStruct((block, head_width), bf16),
        in_specs=[pl.BlockSpec(memory_space=pltpu.SMEM)] + [pl.BlockSpec(memory_space=VMEM)] * 5,
        out_specs=pl.BlockSpec(memory_space=VMEM),
        scratch_shapes=[
            VMEM((cols, 1, modulation_weight.shape[1]), f32),
            VMEM((2, 1, width), f32),
            VMEM((rows, 2 * depth, parts * out_w), bf16),
            VMEM((max(padded_text, tokens), width), bf16),
            VMEM((rows - 1, tokens, 2 * depth), bf16),
            VMEM((cols, group_rows, 2 * depth), bf16),
            VMEM((rows - 1, padded_text, 2 * out_w), bf16),
            VMEM((rows - 1, padded_text, 2 * out_w), bf16),
            VMEM((padded_text, 2 * out_w), f32),
            VMEM((cols, rows - 1, group_rows, parts * out_w), bf16),
            VMEM((cols, rows - 1, group_rows, parts * out_w), bf16),
            VMEM((cols, group_rows, parts * out_w), f32),
            VMEM((rows, block, out_w), bf16),
            VMEM((all_rows, out_w), bf16),
            VMEM((all_rows, out_w), bf16),
            VMEM((rows - 1, block, out_w), bf16),
            VMEM((rows, block, out_w), bf16),
            dma((2,)),
            dma((cols - 1,)),
            dma((cols - 1,)),
            dma((rows - 1,)),
            dma((rows - 1,)),
            dma((cols - 1,)),
            dma((cols - 1,)),
            dma((rows - 1,)),
            dma((rows - 1,)),
            dma((cols, rows - 1)),
            dma((cols, rows - 1)),
            dma((rows - 1,)),
            dma((rows - 1,)),
        ],
        compiler_params=pltpu.CompilerParams(
            collective_id=0, has_side_effects=True, vmem_limit_bytes=48 * 1024 * 1024
        ),
    )(text_len, tile, prompt_rows[0], activation, modulation_weight, by_dest)
    return attended.reshape(1, frames, tile_h, tile_w * cols, head_width)


def solution(mesh):
    in_specs = (
        P("item", None, "row", "col", None),
        P("item", None, None),
        P(),
        P(None, "col"),
        P(("item", "row"), None, "col"),
        P("item"),
        P("item"),
    )
    out_specs = P("item", None, "row", None, "col")
    rows, cols, items = mesh.shape["row"], mesh.shape["col"], mesh.shape["item"]

    def on_device(*blocks):
        group = blocks[4].shape[2] // rows
        if items == 2 and cols % 2 == 0 and group >= 128 and group % 128 == 0:
            return on_device_fast(rows, cols, *blocks)
        return on_device_general(*blocks)

    return jax.shard_map(
        on_device, mesh=mesh, in_specs=in_specs, out_specs=out_specs, check_vma=False
    )
```

```python
import functools
import math

import jax
import jax.numpy as jnp
import numpy as np
from jax import lax
from jax.experimental import pallas as pl
from jax.experimental.pallas import tpu as pltpu
from jax.sharding import PartitionSpec as P

HD = 64
MESH = pl.DeviceIdType.MESH
VMEM = pltpu.VMEM


def with_halo(block, sides, width):
    for axis, dim in sides:
        count = lax.axis_size(axis)
        forward = [(i, i + 1) for i in range(count - 1)]
        backward = [(target, source) for source, target in forward]
        low = lax.ppermute(
            lax.slice_in_dim(block, block.shape[dim] - width, None, axis=dim), axis, forward
        )
        high = lax.ppermute(lax.slice_in_dim(block, 0, width, axis=dim), axis, backward)
        block = jnp.concatenate([low, block, high], axis=dim)
    return block


def time_angles(step, count):
    half = count // 2
    freqs = jnp.exp(-math.log(10000.0) * jnp.arange(half, dtype=jnp.float32) / half)
    angle = step.astype(jnp.float32) * freqs
    return jnp.concatenate([jnp.cos(angle), jnp.sin(angle)])


def modulate(rows, shift, scale):
    values = rows.astype(jnp.float32)
    center = jnp.mean(values, axis=-1, keepdims=True)
    centered = values - center
    spread = jnp.mean(centered * centered, axis=-1, keepdims=True)
    return (centered * lax.rsqrt(spread + 1e-06) * (1.0 + scale) + shift).astype(jnp.bfloat16)


def absorb(carry, queries, key_rows, value_rows, valid):
    running_max, running_sum, weighted = carry
    count = key_rows.shape[0]
    heads = queries.shape[1]
    key_heads = key_rows.reshape(count, heads, HD)
    value_heads = value_rows.reshape(count, heads, HD)
    scores = (
        jnp.einsum("rhd,bhd->rhb", queries, key_heads, preferred_element_type=jnp.float32) * 0.125
    )
    if valid is not None:
        scores = jnp.where(valid[None, None, :], scores, -jnp.inf)
    newest = jnp.maximum(running_max, jnp.max(scores, axis=-1))
    weights = jnp.exp(scores - newest[..., None])
    shrink_by = jnp.exp(running_max - newest)
    running_sum = running_sum * shrink_by + jnp.sum(weights, axis=-1)
    weighted = weighted * shrink_by[..., None] + jnp.einsum(
        "rhb,bhd->rhd",
        weights.astype(jnp.bfloat16),
        value_heads,
        preferred_element_type=jnp.float32,
    )
    return (newest, running_sum, weighted)


def on_device_general(latents, prompt_rows, peg_weight, modulation_weight, qkv_weight, text_len, timestep):
    tile_h = latents.shape[2]
    tile_w = latents.shape[3]
    width = latents.shape[4]
    padded = with_halo(latents, (("row", 2), ("col", 3)), 1)
    summed = latents.astype(jnp.float32)
    for row_tap in range(3):
        for col_tap in range(3):
            summed = summed + padded[
                :, :, row_tap : row_tap + tile_h, col_tap : col_tap + tile_w, :
            ].astype(jnp.float32) * peg_weight[row_tap, col_tap].astype(jnp.float32)
    convolved = summed.astype(jnp.bfloat16)
    activation = jax.nn.silu(time_angles(timestep[0], modulation_weight.shape[0])).astype(
        jnp.bfloat16
    )
    own_columns = jnp.dot(
        activation[None, :], modulation_weight, preferred_element_type=jnp.float32
    )
    modulation = lax.all_gather(own_columns, "col", axis=1, tiled=True)[0]
    shift = modulation[:width]
    scale = modulation[width:]
    group_rows = lax.all_gather(modulate(convolved, shift, scale), "col", axis=3, tiled=True)
    frames = group_rows.shape[1]
    grid_w = group_rows.shape[3]
    flat_rows = group_rows.reshape(-1, width)
    row_count = flat_rows.shape[0]
    text_normed = modulate(prompt_rows[0], shift, scale)
    text_count = text_normed.shape[0]
    head_width = qkv_weight.shape[2]
    full_weight = lax.all_gather(qkv_weight, ("item", "row"), axis=0, tiled=True)
    latent_proj = jnp.einsum(
        "rd,dkc->rkc", flat_rows, full_weight, preferred_element_type=jnp.float32
    )
    text_proj = jnp.einsum(
        "rd,dkc->rkc", text_normed, full_weight, preferred_element_type=jnp.float32
    )
    latent_qkv = latent_proj.astype(jnp.bfloat16)
    text_qkv = text_proj.astype(jnp.bfloat16)
    heads = head_width // HD
    queries = latent_qkv[:, 0, :].reshape(row_count, heads, HD)
    local_keys = latent_qkv[:, 1, :]
    local_values = latent_qkv[:, 2, :]
    text_valid = jnp.arange(text_count, dtype=jnp.int32) < text_len[0]
    start_carry = (
        jnp.full((row_count, heads), -jnp.inf, jnp.float32),
        jnp.zeros((row_count, heads), jnp.float32),
        jnp.zeros((row_count, heads, HD), jnp.float32),
    )
    text_carry = absorb(start_carry, queries, text_qkv[:, 1, :], text_qkv[:, 2, :], text_valid)
    key_rows = lax.all_gather(local_keys, "row", axis=0, tiled=True)
    value_rows = lax.all_gather(local_values, "row", axis=0, tiled=True)
    total_rows = key_rows.shape[0]
    block_count = total_rows // row_count

    def one_block(state, pair):
        return (absorb(state, queries, pair[0], pair[1], None), None)

    state, unused = lax.scan(
        one_block,
        text_carry,
        (
            key_rows.reshape(block_count, row_count, head_width),
            value_rows.reshape(block_count, row_count, head_width),
        ),
    )
    running_max, running_sum, weighted = state
    attended = (weighted / running_sum[..., None]).astype(jnp.bfloat16)
    return attended.reshape(1, frames, tile_h, grid_w, head_width)


def centered_rows(values):
    center = jnp.mean(values, axis=-1, keepdims=True)
    centered = values - center
    spread = jnp.mean(centered * centered, axis=-1, keepdims=True)
    return centered * lax.rsqrt(spread + 1e-06)


SIDES = ((-1, 0), (1, 0), (0, -1), (0, 1), (-1, -1), (-1, 1), (1, -1), (1, 1))


def halo_tables(frames, tile_h, tile_w, parts):
    tokens = frames * tile_h * tile_w
    edge = frames * tile_h

    def token(f, h, w):
        return (f * tile_h + h) * tile_w + w

    pick = np.zeros((1 + parts, 64, tokens), np.float32)
    shift = np.zeros((parts, 8 * tokens, tokens + 8 * edge + 64), np.float32)
    last_h, last_w = tile_h - 1, tile_w - 1
    for at, (down, right) in enumerate(SIDES):
        h_from = last_h if down < 0 else 0
        w_from = last_w if right < 0 else 0
        for f in range(frames):
            if at < 4:
                for k in range(tile_h):
                    source = token(f, h_from, k) if down else token(f, k, w_from)
                    pick[0, at * edge + f * tile_h + k, source] = 1
            else:
                for part in range(parts):
                    pick[1 + part, (at - 4) * 16 + part * frames + f, token(f, h_from, w_from)] = 1
        for part in range(parts):
            upper = part // (parts // 2)
            for f in range(frames):
                for h in range(tile_h):
                    for w in range(tile_w):
                        y, x = h + down, w + right
                        out_y = -1 if y < 0 else (1 if y > last_h else 0)
                        out_x = -1 if x < 0 else (1 if x > last_w else 0)
                        if out_y == 0 and out_x == 0:
                            source = token(f, y, x)
                        else:
                            slot = SIDES.index((out_y, out_x))
                            if slot < 4:
                                k = x if out_y else y
                                source = tokens + slot * 2 * edge + upper * edge + f * tile_h + k
                            else:
                                source = tokens + 8 * edge + (slot - 4) * 16 + part * frames + f
                        shift[part, at * tokens + token(f, h, w), source] = 1
    return pick, shift


def layer_kernel(
    sizes,
    len_ref,
    tile_ref,
    pick_ref,
    shift_ref,
    peg_ref,
    prompt_hbm,
    act_ref,
    mod_hbm,
    weight_ref,
    out_ref,
    prompt_ref,
    mod_ref,
    side_send,
    side_in,
    corner_send,
    corner_in,
    conv,
    local_sems,
    halo_send,
    halo_recv,
    mod_buf,
    affine,
    weights,
    text_in,
    send_x,
    grid_x,
    send_text,
    recv_text,
    own_text,
    send_part,
    recv_part,
    own_part,
    q_buf,
    k_buf,
    v_buf,
    send_out,
    recv_out,
    w_sems,
    mod_send,
    mod_recv,
    x_send,
    x_recv,
    z_send,
    z_recv,
    t_send,
    t_recv,
    p_send,
    p_recv,
    o_send,
    o_recv,
):
    rows, cols, text, padded_text, tile_w = sizes
    tokens, width = tile_ref.shape
    depth = weight_ref.shape[1]
    out_w = weight_ref.shape[2] // 3
    block = tokens * cols
    item = lax.axis_index("item")
    row = lax.axis_index("row")
    col = lax.axis_index("col")

    def row_peer(step):
        return lax.rem(row + step, rows)

    def col_peer(step):
        return lax.rem(col + step, cols)

    def remote(src, dst, send, recv, where):
        return pltpu.make_async_remote_copy(
            src_ref=src, dst_ref=dst, send_sem=send, recv_sem=recv, device_id=where, device_id_type=MESH
        )

    prompt_copy = pltpu.make_async_copy(prompt_hbm, prompt_ref, local_sems.at[0])
    mod_copy = pltpu.make_async_copy(mod_hbm, mod_ref, local_sems.at[1])
    mod_copy.start()
    prompt_copy.start()
    side_in[...] = jnp.zeros_like(side_in)
    corner_in[...] = jnp.zeros_like(corner_in)

    def within(down, right):
        r, c = row + down, col + right
        return (r >= 0) & (r < rows) & (c >= 0) & (c < cols)

    barrier = pltpu.get_barrier_semaphore()
    for down, right in SIDES[4:]:

        @pl.when(within(down, right))
        def greet(down=down, right=right):
            pl.semaphore_signal(
                barrier, inc=1, device_id={"row": row + down, "col": col + right}, device_id_type=MESH
            )

    pl.semaphore_signal(barrier, inc=1, device_id={"item": 1 - item}, device_id_type=MESH)
    for step in range(1, rows):
        pl.semaphore_signal(barrier, inc=1, device_id={"row": row_peer(step)}, device_id_type=MESH)
    for step in range(1, cols):
        pl.semaphore_signal(barrier, inc=1, device_id={"col": col_peer(step)}, device_id_type=MESH)

    tile = tile_ref[...]
    wide = side_in.shape[2]
    narrow = corner_in.shape[1]
    edge = side_in.shape[1] // 2
    picked = jnp.dot(pick_ref[0, 0 : 4 * edge], tile, preferred_element_type=jnp.float32)
    for side in range(4):
        lines = picked[side * edge : (side + 1) * edge]
        side_send[side] = jnp.concatenate([lines[:, :wide], lines[:, wide:]], axis=0).astype(jnp.bfloat16)
    corners = jnp.zeros((corner_in.shape[0], narrow), jnp.float32)
    for part in range(width // narrow):
        corners = corners + jnp.dot(
            pick_ref[1 + part],
            tile[:, part * narrow : (part + 1) * narrow],
            preferred_element_type=jnp.float32,
        )
    corner_send[...] = corners.astype(jnp.bfloat16)

    def halo_copy(at, down, right):
        if at < 4:
            src, dst = side_send.at[at], side_in.at[at]
        else:
            lines = pl.ds((at - 4) * 16, 16)
            src, dst = corner_send.at[lines, :], corner_in.at[lines, :]
        return remote(
            src, dst, halo_send.at[at], halo_recv.at[at], {"row": row - down, "col": col - right}
        )

    mod_copy.wait()
    own_columns = jnp.dot(act_ref[...], mod_ref[...], preferred_element_type=jnp.float32)
    mod_buf[col] = own_columns[0:1, :]
    beside_rows = (row + rows - 1) // rows + (2 * rows - 2 - row) // rows
    beside_cols = (col + cols - 1) // cols + (2 * cols - 2 - col) // cols
    pl.semaphore_wait(barrier, rows + cols - 1 + beside_rows * beside_cols)
    for at, (down, right) in enumerate(SIDES):

        @pl.when(within(-down, -right))
        def send(at=at, down=down, right=right):
            halo_copy(at, down, right).start()

    mod_copies = []
    for step in range(1, cols):
        copy = remote(
            mod_buf.at[col],
            mod_buf.at[col],
            mod_send.at[step - 1],
            mod_recv.at[step - 1],
            {"col": col_peer(step)},
        )
        copy.start()
        mod_copies.append(copy)
    weight_copy = remote(
        weight_ref,
        weights.at[:, pl.ds(depth, depth), :],
        w_sems.at[0],
        w_sems.at[1],
        {"item": 1 - item},
    )
    weight_copy.start()
    for dest in range(rows):
        weights[dest, 0:depth, :] = weight_ref[dest]
    for at, (down, right) in enumerate(SIDES):

        @pl.when(within(down, right))
        def receive(at=at, down=down, right=right):
            halo_copy(at, down, right).wait_recv()

    for part in range(width // narrow):
        lanes = slice(part * narrow, (part + 1) * narrow)
        upper, start = divmod(part * narrow, wide)
        pieces = [tile[:, lanes]]
        for side in range(4):
            pieces.append(side_in[side, :, start : start + narrow])
        pieces.append(corner_in[...])
        moved = jnp.dot(
            shift_ref[part], jnp.concatenate(pieces, axis=0), preferred_element_type=jnp.float32
        )
        own = tile[:, lanes].astype(jnp.float32)
        taps = [peg_ref[a, :, lanes].astype(jnp.float32) for a in range(3)]
        summed = own + own * taps[1][1:2]
        for at, (down, right) in enumerate(SIDES):
            summed = summed + moved[at * tokens : (at + 1) * tokens] * taps[down + 1][right + 1 : right + 2]
        conv[:, lanes] = summed.astype(jnp.bfloat16)
    tile_normal = centered_rows(conv[...].astype(jnp.float32))
    for step in range(1, cols):
        remote(
            mod_buf.at[col],
            mod_buf.at[lax.rem(col - step + cols, cols)],
            mod_send.at[step - 1],
            mod_recv.at[step - 1],
            {"col": col_peer(step)},
        ).wait_recv()
    half = cols // 2
    piece = mod_buf.shape[2]
    for part in range(half):
        affine[0, :, part * piece : (part + 1) * piece] = mod_buf[part]
        affine[1, :, part * piece : (part + 1) * piece] = 1.0 + mod_buf[half + part]

    def depth_slices(dest):
        first = (item * rows + dest) * depth
        second = ((1 - item) * rows + dest) * depth
        return (pl.multiple_of(first, depth), pl.multiple_of(second, depth))

    text_in[0:tokens, :] = (tile_normal * affine[1] + affine[0]).astype(jnp.bfloat16)
    x_copies = []
    for step in range(1, rows):
        peer = row_peer(step)
        for order, start in enumerate(depth_slices(peer)):
            send_x[step - 1, :, order * depth : (order + 1) * depth] = text_in[
                0:tokens, pl.ds(start, depth)
            ]
        copy = remote(
            send_x.at[step - 1],
            grid_x.at[0, pl.ds(pl.multiple_of(row * tokens, tokens), tokens), :],
            x_send.at[step - 1],
            x_recv.at[step - 1],
            {"row": peer},
        )
        copy.start()
        x_copies.append(copy)
    own_slices = depth_slices(row)
    for order, start in enumerate(own_slices):
        grid_x[
            0, pl.ds(pl.multiple_of(row * tokens, tokens), tokens), order * depth : (order + 1) * depth
        ] = text_in[0:tokens, pl.ds(start, depth)]

    for step in range(1, rows):
        source = lax.rem(row - step + rows, rows)
        remote(
            send_x.at[step - 1],
            grid_x.at[0, pl.ds(pl.multiple_of(source * tokens, tokens), tokens), :],
            x_send.at[step - 1],
            x_recv.at[step - 1],
            {"row": row_peer(step)},
        ).wait_recv()
    z_copies = []
    for step in range(1, cols):
        copy = remote(
            grid_x.at[0], grid_x.at[step], z_send.at[step - 1], z_recv.at[step - 1], {"col": col_peer(step)}
        )
        copy.start()
        z_copies.append(copy)
    weight_copy.wait_recv()

    p_copies = []

    def latent_part(group):
        values = grid_x[group]
        for step in range(1, rows):
            peer = row_peer(step)
            send_part[group, step - 1] = jnp.dot(
                values, weights[peer], preferred_element_type=jnp.float32
            ).astype(jnp.bfloat16)
            copy = remote(
                send_part.at[group, step - 1],
                recv_part.at[group, step - 1],
                p_send.at[group, step - 1],
                p_recv.at[group, step - 1],
                {"row": peer},
            )
            copy.start()
            p_copies.append(copy)
        own_part[group] = jnp.dot(values, weights[row], preferred_element_type=jnp.float32)

    latent_part(0)

    prompt_copy.wait()
    scale_pieces = [affine[1, :, pl.ds(start, depth)] for start in own_slices]
    shift_pieces = [affine[0, :, pl.ds(start, depth)] for start in own_slices]
    for start_row in range(0, padded_text, 16):
        count = min(16, text - start_row)
        values = prompt_ref[start_row : start_row + count, :].astype(jnp.float32)
        center = jnp.mean(values, axis=-1, keepdims=True)
        centered = values - center
        spread = lax.rsqrt(jnp.mean(centered * centered, axis=-1, keepdims=True) + 1e-06)
        for order, start in enumerate(own_slices):
            part = prompt_ref[start_row : start_row + count, pl.ds(start, depth)].astype(jnp.float32)
            normed = (part - center) * spread * scale_pieces[order] + shift_pieces[order]
            if count < 16:
                normed = jnp.concatenate([normed, jnp.zeros((16 - count, depth), jnp.float32)], axis=0)
            text_in[start_row : start_row + 16, order * depth : (order + 1) * depth] = normed.astype(
                jnp.bfloat16
            )
    text_values = text_in[:, 0 : 2 * depth]
    t_copies = []
    for step in range(1, rows):
        peer = row_peer(step)
        send_text[step - 1] = jnp.dot(
            text_values, weights[peer, :, out_w:], preferred_element_type=jnp.float32
        ).astype(jnp.bfloat16)
        copy = remote(
            send_text.at[step - 1],
            recv_text.at[step - 1],
            t_send.at[step - 1],
            t_recv.at[step - 1],
            {"row": peer},
        )
        copy.start()
        t_copies.append(copy)
    own_text[...] = jnp.dot(text_values, weights[row, :, out_w:], preferred_element_type=jnp.float32)

    for group in range(1, cols):
        z_copies[group - 1].wait_recv()
        latent_part(group)

    for copy in t_copies:
        copy.wait_recv()
    total = own_text[...]
    for step in range(1, rows):
        total = total + recv_text[step - 1].astype(jnp.float32)
    k_buf[0:padded_text, :] = total[:, 0:out_w].astype(jnp.bfloat16)
    v_buf[0:padded_text, :] = total[:, out_w:].astype(jnp.bfloat16)
    for group in range(cols):
        for step in range(1, rows):
            p_copies[group * (rows - 1) + step - 1].wait_recv()
        total = own_part[group]
        for step in range(1, rows):
            total = total + recv_part[group, step - 1].astype(jnp.float32)
        rounded = total.astype(jnp.bfloat16)
        per_col = rows * tokens
        base = padded_text + group * per_col
        k_buf[base : base + per_col, :] = rounded[:, out_w : 2 * out_w]
        v_buf[base : base + per_col, :] = rounded[:, 2 * out_w :]
        for dest in range(rows):
            q_buf[dest, group * tokens : (group + 1) * tokens, :] = rounded[
                dest * tokens : (dest + 1) * tokens, 0:out_w
            ]

    at = lax.broadcasted_iota(jnp.int32, (block, block), 0)
    source = lax.broadcasted_iota(jnp.int32, (block, block), 1)
    group = source // tokens
    token = source - group * tokens
    line = token // tile_w
    place = token - line * tile_w
    owner = col - group
    owner = jnp.where(owner < 0, owner + cols, owner)
    target = (line * cols + owner) * tile_w + place
    permute = jnp.where(at == target, 1.0, 0.0).astype(jnp.bfloat16)
    keys = k_buf[...]
    vals = v_buf[...]
    position = lax.broadcasted_iota(jnp.int32, (1, keys.shape[0]), 1)
    valid = (position >= padded_text) | (position < len_ref[0])
    o_copies = []
    for step in list(range(1, rows)) + [0]:
        peer = row_peer(step)
        queries = jnp.dot(permute, q_buf[peer], preferred_element_type=jnp.float32).astype(jnp.bfloat16)
        outs = []
        for head in range(out_w // HD):
            lanes = slice(head * HD, (head + 1) * HD)
            scores = (
                lax.dot_general(
                    queries[:, lanes],
                    keys[:, lanes],
                    (((1,), (1,)), ((), ())),
                    preferred_element_type=jnp.float32,
                )
                * 0.125
            )
            scores = jnp.where(valid, scores, -jnp.inf)
            weight = jnp.exp(scores - jnp.max(scores, axis=-1, keepdims=True))
            total = jnp.sum(weight, axis=-1, keepdims=True)
            outs.append(
                jnp.dot(weight.astype(jnp.bfloat16), vals[:, lanes], preferred_element_type=jnp.float32)
                / total
            )
        result = jnp.concatenate(outs, axis=-1).astype(jnp.bfloat16)
        if step == 0:
            recv_out[row] = result
        else:
            send_out[step - 1] = result
            copy = remote(
                send_out.at[step - 1],
                recv_out.at[row],
                o_send.at[step - 1],
                o_recv.at[step - 1],
                {"row": peer},
            )
            copy.start()
            o_copies.append(copy)
    for step in range(1, rows):
        source = lax.rem(row - step + rows, rows)
        remote(
            send_out.at[step - 1],
            recv_out.at[source],
            o_send.at[step - 1],
            o_recv.at[step - 1],
            {"row": row_peer(step)},
        ).wait_recv()
    for source in range(rows):
        out_ref[:, source * out_w : (source + 1) * out_w] = recv_out[source]
    for at, (down, right) in enumerate(SIDES):

        @pl.when(within(-down, -right))
        def sent(at=at, down=down, right=right):
            halo_copy(at, down, right).wait_send()

    for copy in mod_copies + [weight_copy] + x_copies + z_copies + p_copies + t_copies + o_copies:
        copy.wait_send()


def on_device_fast(
    rows, cols, latents, prompt_rows, peg_weight, modulation_weight, qkv_weight, text_len, timestep
):
    frames, tile_h, tile_w, width = latents.shape[1:]
    tokens = frames * tile_h * tile_w
    tile = latents.reshape(tokens, width)
    parts = 8
    narrow = width // parts
    pick, shift = (jnp.asarray(table, jnp.bfloat16) for table in halo_tables(frames, tile_h, tile_w, parts))
    temb = modulation_weight.shape[0]
    activation = jax.nn.silu(time_angles(timestep[0], temb)).astype(jnp.bfloat16)
    activation = jnp.broadcast_to(activation[None, :], (16, temb))
    depth, kinds, head_width = qkv_weight.shape
    out_w = head_width // rows
    by_dest = qkv_weight.reshape(depth, kinds, rows, out_w).transpose(2, 0, 1, 3)
    by_dest = by_dest.reshape(rows, depth, kinds * out_w)
    text = prompt_rows.shape[1]
    padded_text = -(-text // 16) * 16
    block = tokens * cols
    group_rows = tokens * rows
    bf16, f32 = jnp.bfloat16, jnp.float32
    dma = pltpu.SemaphoreType.DMA
    all_rows = padded_text + group_rows * cols
    attended = pl.pallas_call(
        functools.partial(layer_kernel, (rows, cols, text, padded_text, tile_w)),
        out_shape=jax.ShapeDtypeStruct((block, head_width), bf16),
        in_specs=[pl.BlockSpec(memory_space=pltpu.SMEM)] + [pl.BlockSpec(memory_space=space) for space in (VMEM,) * 4 + (pltpu.HBM, VMEM, pltpu.HBM, VMEM)],
        out_specs=pl.BlockSpec(memory_space=VMEM),
        scratch_shapes=[
            VMEM((text, width), bf16),
            VMEM(modulation_weight.shape, bf16),
            VMEM((4, 16, width // 2), bf16),
            VMEM((4, 16, width // 2), bf16),
            VMEM((64, narrow), bf16),
            VMEM((64, narrow), bf16),
            VMEM((tokens, width), bf16),
            dma((2,)),
            dma((8,)),
            dma((8,)),
            VMEM((cols, 1, modulation_weight.shape[1]), f32),
            VMEM((2, 1, width), f32),
            VMEM((rows, 2 * depth, kinds * out_w), bf16),
            VMEM((max(padded_text, tokens), width), bf16),
            VMEM((rows - 1, tokens, 2 * depth), bf16),
            VMEM((cols, group_rows, 2 * depth), bf16),
            VMEM((rows - 1, padded_text, 2 * out_w), bf16),
            VMEM((rows - 1, padded_text, 2 * out_w), bf16),
            VMEM((padded_text, 2 * out_w), f32),
            VMEM((cols, rows - 1, group_rows, kinds * out_w), bf16),
            VMEM((cols, rows - 1, group_rows, kinds * out_w), bf16),
            VMEM((cols, group_rows, kinds * out_w), f32),
            VMEM((rows, block, out_w), bf16),
            VMEM((all_rows, out_w), bf16),
            VMEM((all_rows, out_w), bf16),
            VMEM((rows - 1, block, out_w), bf16),
            VMEM((rows, block, out_w), bf16),
            dma((2,)),
            dma((cols - 1,)),
            dma((cols - 1,)),
            dma((rows - 1,)),
            dma((rows - 1,)),
            dma((cols - 1,)),
            dma((cols - 1,)),
            dma((rows - 1,)),
            dma((rows - 1,)),
            dma((cols, rows - 1)),
            dma((cols, rows - 1)),
            dma((rows - 1,)),
            dma((rows - 1,)),
        ],
        compiler_params=pltpu.CompilerParams(
            collective_id=0, has_side_effects=True, vmem_limit_bytes=48 * 1024 * 1024
        ),
    )(text_len, tile, pick, shift, peg_weight, prompt_rows[0], activation, modulation_weight, by_dest)
    return attended.reshape(1, frames, tile_h, tile_w * cols, head_width)


def solution(mesh):
    in_specs = (
        P("item", None, "row", "col", None),
        P("item", None, None),
        P(),
        P(None, "col"),
        P(("item", "row"), None, "col"),
        P("item"),
        P("item"),
    )
    out_specs = P("item", None, "row", None, "col")
    rows, cols, items = mesh.shape["row"], mesh.shape["col"], mesh.shape["item"]

    def on_device(*blocks):
        group = blocks[4].shape[2] // rows
        if items == 2 and cols % 2 == 0 and group >= 128 and group % 128 == 0 and blocks[0].shape[1:4] == (2, 4, 4):
            return on_device_fast(rows, cols, *blocks)
        return on_device_general(*blocks)

    return jax.shard_map(
        on_device, mesh=mesh, in_specs=in_specs, out_specs=out_specs, check_vma=False
    )
```

```python
import functools
import math

import jax
import jax.numpy as jnp
import numpy as np
from jax import lax
from jax.experimental import pallas as pl
from jax.experimental.pallas import tpu as pltpu
from jax.sharding import PartitionSpec as P

HD = 64
MESH = pl.DeviceIdType.MESH
VMEM = pltpu.VMEM


def with_halo(block, sides, width):
    for axis, dim in sides:
        count = lax.axis_size(axis)
        forward = [(i, i + 1) for i in range(count - 1)]
        backward = [(target, source) for source, target in forward]
        low = lax.ppermute(
            lax.slice_in_dim(block, block.shape[dim] - width, None, axis=dim), axis, forward
        )
        high = lax.ppermute(lax.slice_in_dim(block, 0, width, axis=dim), axis, backward)
        block = jnp.concatenate([low, block, high], axis=dim)
    return block


def time_angles(step, count):
    half = count // 2
    freqs = jnp.exp(-math.log(10000.0) * jnp.arange(half, dtype=jnp.float32) / half)
    angle = step.astype(jnp.float32) * freqs
    return jnp.concatenate([jnp.cos(angle), jnp.sin(angle)])


def modulate(rows, shift, scale):
    values = rows.astype(jnp.float32)
    center = jnp.mean(values, axis=-1, keepdims=True)
    centered = values - center
    spread = jnp.mean(centered * centered, axis=-1, keepdims=True)
    return (centered * lax.rsqrt(spread + 1e-06) * (1.0 + scale) + shift).astype(jnp.bfloat16)


def absorb(carry, queries, key_rows, value_rows, valid):
    running_max, running_sum, weighted = carry
    count = key_rows.shape[0]
    heads = queries.shape[1]
    key_heads = key_rows.reshape(count, heads, HD)
    value_heads = value_rows.reshape(count, heads, HD)
    scores = (
        jnp.einsum("rhd,bhd->rhb", queries, key_heads, preferred_element_type=jnp.float32) * 0.125
    )
    if valid is not None:
        scores = jnp.where(valid[None, None, :], scores, -jnp.inf)
    newest = jnp.maximum(running_max, jnp.max(scores, axis=-1))
    weights = jnp.exp(scores - newest[..., None])
    shrink_by = jnp.exp(running_max - newest)
    running_sum = running_sum * shrink_by + jnp.sum(weights, axis=-1)
    weighted = weighted * shrink_by[..., None] + jnp.einsum(
        "rhb,bhd->rhd",
        weights.astype(jnp.bfloat16),
        value_heads,
        preferred_element_type=jnp.float32,
    )
    return (newest, running_sum, weighted)


def on_device_general(latents, prompt_rows, peg_weight, modulation_weight, qkv_weight, text_len, timestep):
    tile_h = latents.shape[2]
    tile_w = latents.shape[3]
    width = latents.shape[4]
    padded = with_halo(latents, (("row", 2), ("col", 3)), 1)
    summed = latents.astype(jnp.float32)
    for row_tap in range(3):
        for col_tap in range(3):
            summed = summed + padded[
                :, :, row_tap : row_tap + tile_h, col_tap : col_tap + tile_w, :
            ].astype(jnp.float32) * peg_weight[row_tap, col_tap].astype(jnp.float32)
    convolved = summed.astype(jnp.bfloat16)
    activation = jax.nn.silu(time_angles(timestep[0], modulation_weight.shape[0])).astype(
        jnp.bfloat16
    )
    own_columns = jnp.dot(
        activation[None, :], modulation_weight, preferred_element_type=jnp.float32
    )
    modulation = lax.all_gather(own_columns, "col", axis=1, tiled=True)[0]
    shift = modulation[:width]
    scale = modulation[width:]
    group_rows = lax.all_gather(modulate(convolved, shift, scale), "col", axis=3, tiled=True)
    frames = group_rows.shape[1]
    grid_w = group_rows.shape[3]
    flat_rows = group_rows.reshape(-1, width)
    row_count = flat_rows.shape[0]
    text_normed = modulate(prompt_rows[0], shift, scale)
    text_count = text_normed.shape[0]
    head_width = qkv_weight.shape[2]
    full_weight = lax.all_gather(qkv_weight, ("item", "row"), axis=0, tiled=True)
    latent_proj = jnp.einsum(
        "rd,dkc->rkc", flat_rows, full_weight, preferred_element_type=jnp.float32
    )
    text_proj = jnp.einsum(
        "rd,dkc->rkc", text_normed, full_weight, preferred_element_type=jnp.float32
    )
    latent_qkv = latent_proj.astype(jnp.bfloat16)
    text_qkv = text_proj.astype(jnp.bfloat16)
    heads = head_width // HD
    queries = latent_qkv[:, 0, :].reshape(row_count, heads, HD)
    local_keys = latent_qkv[:, 1, :]
    local_values = latent_qkv[:, 2, :]
    text_valid = jnp.arange(text_count, dtype=jnp.int32) < text_len[0]
    start_carry = (
        jnp.full((row_count, heads), -jnp.inf, jnp.float32),
        jnp.zeros((row_count, heads), jnp.float32),
        jnp.zeros((row_count, heads, HD), jnp.float32),
    )
    text_carry = absorb(start_carry, queries, text_qkv[:, 1, :], text_qkv[:, 2, :], text_valid)
    key_rows = lax.all_gather(local_keys, "row", axis=0, tiled=True)
    value_rows = lax.all_gather(local_values, "row", axis=0, tiled=True)
    total_rows = key_rows.shape[0]
    block_count = total_rows // row_count

    def one_block(state, pair):
        return (absorb(state, queries, pair[0], pair[1], None), None)

    state, unused = lax.scan(
        one_block,
        text_carry,
        (
            key_rows.reshape(block_count, row_count, head_width),
            value_rows.reshape(block_count, row_count, head_width),
        ),
    )
    running_max, running_sum, weighted = state
    attended = (weighted / running_sum[..., None]).astype(jnp.bfloat16)
    return attended.reshape(1, frames, tile_h, grid_w, head_width)


def centered_rows(values):
    center = jnp.mean(values, axis=-1, keepdims=True)
    centered = values - center
    spread = jnp.mean(centered * centered, axis=-1, keepdims=True)
    return centered * lax.rsqrt(spread + 1e-06)


SIDES = ((-1, 0), (1, 0), (0, -1), (0, 1), (-1, -1), (-1, 1), (1, -1), (1, 1))


def halo_tables(frames, tile_h, tile_w, parts):
    tokens = frames * tile_h * tile_w
    edge = frames * tile_h

    def token(f, h, w):
        return (f * tile_h + h) * tile_w + w

    pick = np.zeros((1 + parts, 64, tokens), np.float32)
    shift = np.zeros((parts, 8 * tokens, tokens + 8 * edge + 64), np.float32)
    last_h, last_w = tile_h - 1, tile_w - 1
    for at, (down, right) in enumerate(SIDES):
        h_from = last_h if down < 0 else 0
        w_from = last_w if right < 0 else 0
        for f in range(frames):
            if at < 4:
                for k in range(tile_h):
                    source = token(f, h_from, k) if down else token(f, k, w_from)
                    pick[0, at * edge + f * tile_h + k, source] = 1
            else:
                for part in range(parts):
                    pick[1 + part, (at - 4) * 16 + part * frames + f, token(f, h_from, w_from)] = 1
        for part in range(parts):
            upper = part // (parts // 2)
            for f in range(frames):
                for h in range(tile_h):
                    for w in range(tile_w):
                        y, x = h + down, w + right
                        out_y = -1 if y < 0 else (1 if y > last_h else 0)
                        out_x = -1 if x < 0 else (1 if x > last_w else 0)
                        if out_y == 0 and out_x == 0:
                            source = token(f, y, x)
                        else:
                            slot = SIDES.index((out_y, out_x))
                            if slot < 4:
                                k = x if out_y else y
                                source = tokens + slot * 2 * edge + upper * edge + f * tile_h + k
                            else:
                                source = tokens + 8 * edge + (slot - 4) * 16 + part * frames + f
                        shift[part, at * tokens + token(f, h, w), source] = 1
    return pick, shift


def layer_kernel(
    sizes,
    len_ref,
    tile_ref,
    pick_ref,
    shift_ref,
    peg_ref,
    prompt_hbm,
    act_ref,
    mod_hbm,
    weight_ref,
    out_ref,
    prompt_ref,
    mod_ref,
    side_send,
    side_in,
    corner_send,
    corner_in,
    conv,
    local_sems,
    halo_send,
    halo_recv,
    mod_buf,
    affine,
    weights,
    text_in,
    send_x,
    grid_x,
    send_text,
    recv_text,
    own_text,
    send_part,
    recv_part,
    own_part,
    q_buf,
    k_buf,
    v_buf,
    send_out,
    recv_out,
    w_sems,
    mod_send,
    mod_recv,
    x_send,
    x_recv,
    z_send,
    z_recv,
    t_send,
    t_recv,
    p_send,
    p_recv,
    o_send,
    o_recv,
):
    rows, cols, text, padded_text, tile_w = sizes
    tokens, width = tile_ref.shape
    depth = weight_ref.shape[1]
    out_w = weight_ref.shape[2] // 3
    block = tokens * cols
    item = lax.axis_index("item")
    row = lax.axis_index("row")
    col = lax.axis_index("col")

    def row_peer(step):
        return lax.rem(row + step, rows)

    def col_peer(step):
        return lax.rem(col + step, cols)

    def remote(src, dst, send, recv, where):
        return pltpu.make_async_remote_copy(
            src_ref=src, dst_ref=dst, send_sem=send, recv_sem=recv, device_id=where, device_id_type=MESH
        )

    prompt_copy = pltpu.make_async_copy(prompt_hbm, prompt_ref, local_sems.at[0])
    mod_copy = pltpu.make_async_copy(mod_hbm, mod_ref, local_sems.at[1])
    mod_copy.start()
    prompt_copy.start()
    side_in[...] = jnp.zeros_like(side_in)
    corner_in[...] = jnp.zeros_like(corner_in)

    def within(down, right):
        r, c = row + down, col + right
        return (r >= 0) & (r < rows) & (c >= 0) & (c < cols)

    barrier = pltpu.get_barrier_semaphore()
    for down, right in SIDES[4:]:

        @pl.when(within(down, right))
        def greet(down=down, right=right):
            pl.semaphore_signal(
                barrier, inc=1, device_id={"row": row + down, "col": col + right}, device_id_type=MESH
            )

    pl.semaphore_signal(barrier, inc=1, device_id={"item": 1 - item}, device_id_type=MESH)
    for step in range(1, rows):
        pl.semaphore_signal(barrier, inc=1, device_id={"row": row_peer(step)}, device_id_type=MESH)
    for step in range(1, cols):
        pl.semaphore_signal(barrier, inc=1, device_id={"col": col_peer(step)}, device_id_type=MESH)

    tile = tile_ref[...]
    wide = side_in.shape[2]
    narrow = corner_in.shape[1]
    edge = side_in.shape[1] // 2
    picked = jnp.dot(pick_ref[0, 0 : 4 * edge], tile, preferred_element_type=jnp.float32)
    for side in range(4):
        lines = picked[side * edge : (side + 1) * edge]
        side_send[side] = jnp.concatenate([lines[:, :wide], lines[:, wide:]], axis=0).astype(jnp.bfloat16)
    corners = jnp.zeros((corner_in.shape[0], narrow), jnp.float32)
    for part in range(width // narrow):
        corners = corners + jnp.dot(
            pick_ref[1 + part],
            tile[:, part * narrow : (part + 1) * narrow],
            preferred_element_type=jnp.float32,
        )
    corner_send[...] = corners.astype(jnp.bfloat16)

    def halo_copy(at, down, right):
        if at < 4:
            src, dst = side_send.at[at], side_in.at[at]
        else:
            lines = pl.ds((at - 4) * 16, 16)
            src, dst = corner_send.at[lines, :], corner_in.at[lines, :]
        return remote(
            src, dst, halo_send.at[at], halo_recv.at[at], {"row": row - down, "col": col - right}
        )

    mod_copy.wait()
    own_columns = jnp.dot(act_ref[...], mod_ref[...], preferred_element_type=jnp.float32)
    mod_buf[col] = own_columns[0:1, :]
    beside_rows = (row + rows - 1) // rows + (2 * rows - 2 - row) // rows
    beside_cols = (col + cols - 1) // cols + (2 * cols - 2 - col) // cols
    pl.semaphore_wait(barrier, rows + cols - 1 + beside_rows * beside_cols)
    for at, (down, right) in enumerate(SIDES):

        @pl.when(within(-down, -right))
        def send(at=at, down=down, right=right):
            halo_copy(at, down, right).start()

    mod_copies = []
    for step in range(1, cols):
        copy = remote(
            mod_buf.at[col],
            mod_buf.at[col],
            mod_send.at[step - 1],
            mod_recv.at[step - 1],
            {"col": col_peer(step)},
        )
        copy.start()
        mod_copies.append(copy)
    weight_copy = remote(
        weight_ref,
        weights.at[:, pl.ds(depth, depth), :],
        w_sems.at[0],
        w_sems.at[1],
        {"item": 1 - item},
    )
    weight_copy.start()
    for dest in range(rows):
        weights[dest, 0:depth, :] = weight_ref[dest]
    prompt_copy.wait()
    text_stats = []
    for start_row in range(0, padded_text, 16):
        count = min(16, text - start_row)
        values = prompt_ref[start_row : start_row + count, :].astype(jnp.float32)
        center = jnp.mean(values, axis=-1, keepdims=True)
        centered = values - center
        spread = lax.rsqrt(jnp.mean(centered * centered, axis=-1, keepdims=True) + 1e-06)
        text_stats.append((center, spread))

    for at, (down, right) in enumerate(SIDES):

        @pl.when(within(down, right))
        def receive(at=at, down=down, right=right):
            halo_copy(at, down, right).wait_recv()

    for part in range(width // narrow):
        lanes = slice(part * narrow, (part + 1) * narrow)
        upper, start = divmod(part * narrow, wide)
        pieces = [tile[:, lanes]]
        for side in range(4):
            pieces.append(side_in[side, :, start : start + narrow])
        pieces.append(corner_in[...])
        moved = jnp.dot(
            shift_ref[part], jnp.concatenate(pieces, axis=0), preferred_element_type=jnp.float32
        )
        own = tile[:, lanes].astype(jnp.float32)
        taps = [peg_ref[a, :, lanes].astype(jnp.float32) for a in range(3)]
        summed = own + own * taps[1][1:2]
        for at, (down, right) in enumerate(SIDES):
            summed = summed + moved[at * tokens : (at + 1) * tokens] * taps[down + 1][right + 1 : right + 2]
        conv[:, lanes] = summed.astype(jnp.bfloat16)
    tile_normal = centered_rows(conv[...].astype(jnp.float32))
    for step in range(1, cols):
        remote(
            mod_buf.at[col],
            mod_buf.at[lax.rem(col - step + cols, cols)],
            mod_send.at[step - 1],
            mod_recv.at[step - 1],
            {"col": col_peer(step)},
        ).wait_recv()
    half = cols // 2
    piece = mod_buf.shape[2]
    for part in range(half):
        affine[0, :, part * piece : (part + 1) * piece] = mod_buf[part]
        affine[1, :, part * piece : (part + 1) * piece] = 1.0 + mod_buf[half + part]

    def depth_slices(dest):
        first = (item * rows + dest) * depth
        second = ((1 - item) * rows + dest) * depth
        return (pl.multiple_of(first, depth), pl.multiple_of(second, depth))

    text_in[0:tokens, :] = (tile_normal * affine[1] + affine[0]).astype(jnp.bfloat16)
    x_copies = []
    for step in range(1, rows):
        peer = row_peer(step)
        for order, start in enumerate(depth_slices(peer)):
            send_x[step - 1, :, order * depth : (order + 1) * depth] = text_in[
                0:tokens, pl.ds(start, depth)
            ]
        copy = remote(
            send_x.at[step - 1],
            grid_x.at[col, pl.ds(pl.multiple_of(row * tokens, tokens), tokens), :],
            x_send.at[step - 1],
            x_recv.at[step - 1],
            {"row": peer},
        )
        copy.start()
        x_copies.append(copy)
    own_slices = depth_slices(row)
    for order, start in enumerate(own_slices):
        grid_x[
            col, pl.ds(pl.multiple_of(row * tokens, tokens), tokens), order * depth : (order + 1) * depth
        ] = text_in[0:tokens, pl.ds(start, depth)]

    weight_copy.wait_recv()

    scale_pieces = [affine[1, :, pl.ds(start, depth)] for start in own_slices]
    shift_pieces = [affine[0, :, pl.ds(start, depth)] for start in own_slices]
    for start_row in range(0, padded_text, 16):
        count = min(16, text - start_row)
        center, spread = text_stats[start_row // 16]
        for order, start in enumerate(own_slices):
            part = prompt_ref[start_row : start_row + count, pl.ds(start, depth)].astype(jnp.float32)
            normed = (part - center) * spread * scale_pieces[order] + shift_pieces[order]
            if count < 16:
                normed = jnp.concatenate([normed, jnp.zeros((16 - count, depth), jnp.float32)], axis=0)
            text_in[start_row : start_row + 16, order * depth : (order + 1) * depth] = normed.astype(
                jnp.bfloat16
            )
    text_values = text_in[:, 0 : 2 * depth]
    t_copies = []
    for step in range(1, rows):
        peer = row_peer(step)
        send_text[step - 1] = jnp.dot(
            text_values, weights[peer, :, out_w:], preferred_element_type=jnp.float32
        ).astype(jnp.bfloat16)
        copy = remote(
            send_text.at[step - 1],
            recv_text.at[step - 1],
            t_send.at[step - 1],
            t_recv.at[step - 1],
            {"row": peer},
        )
        copy.start()
        t_copies.append(copy)
    own_text[...] = jnp.dot(text_values, weights[row, :, out_w:], preferred_element_type=jnp.float32)

    for step in range(1, rows):
        source = lax.rem(row - step + rows, rows)
        remote(
            send_x.at[step - 1],
            grid_x.at[col, pl.ds(pl.multiple_of(source * tokens, tokens), tokens), :],
            x_send.at[step - 1],
            x_recv.at[step - 1],
            {"row": row_peer(step)},
        ).wait_recv()
    def z_copy(direction, distance, source):
        sign = 1 - 2 * direction
        return remote(
            grid_x.at[source],
            grid_x.at[source],
            z_send.at[direction, distance - 1],
            z_recv.at[direction, distance - 1],
            {"col": col + sign},
        )

    def passes(direction, distance):
        home = col - (distance - 1) * (1 - 2 * direction)
        return (home >= 0) & (home < cols) & (col < cols - 1 if direction == 0 else col > 0)

    def arrives(direction, distance):
        home = col - distance * (1 - 2 * direction)
        return (home >= 0) & (home < cols)

    def pass_on(distance):
        for direction in range(2):

            @pl.when(passes(direction, distance))
            def start(direction=direction):
                z_copy(direction, distance, col - (distance - 1) * (1 - 2 * direction)).start()

    pass_on(1)

    def part_copy(group, step):
        return remote(
            send_part.at[group, step - 1],
            recv_part.at[group, step - 1],
            p_send.at[group, step - 1],
            p_recv.at[group, step - 1],
            {"row": row_peer(step)},
        )

    def latent_part(group):
        values = grid_x[group]
        for step in range(1, rows):
            send_part[group, step - 1] = jnp.dot(
                values, weights[row_peer(step)], preferred_element_type=jnp.float32
            ).astype(jnp.bfloat16)
            part_copy(group, step).start()
        own_part[group] = jnp.dot(values, weights[row], preferred_element_type=jnp.float32)

    latent_part(col)
    for distance in range(1, cols):
        for direction in range(2):

            @pl.when(arrives(direction, distance))
            def landed(direction=direction, distance=distance):
                z_copy(direction, distance, col - distance * (1 - 2 * direction)).wait_recv()

        if distance < cols - 1:
            pass_on(distance + 1)
        for direction in range(2):

            @pl.when(arrives(direction, distance))
            def multiply(direction=direction, distance=distance):
                latent_part(col - distance * (1 - 2 * direction))

    for copy in t_copies:
        copy.wait_recv()
    total = own_text[...]
    for step in range(1, rows):
        total = total + recv_text[step - 1].astype(jnp.float32)
    k_buf[0:padded_text, :] = total[:, 0:out_w].astype(jnp.bfloat16)
    v_buf[0:padded_text, :] = total[:, out_w:].astype(jnp.bfloat16)
    for group in range(cols):
        for step in range(1, rows):
            part_copy(group, step).wait_recv()
        total = own_part[group]
        for step in range(1, rows):
            total = total + recv_part[group, step - 1].astype(jnp.float32)
        rounded = total.astype(jnp.bfloat16)
        per_col = rows * tokens
        base = padded_text + group * per_col
        k_buf[base : base + per_col, :] = rounded[:, out_w : 2 * out_w]
        v_buf[base : base + per_col, :] = rounded[:, 2 * out_w :]
        for dest in range(rows):
            q_buf[dest, group * tokens : (group + 1) * tokens, :] = rounded[
                dest * tokens : (dest + 1) * tokens, 0:out_w
            ]

    at = lax.broadcasted_iota(jnp.int32, (block, block), 0)
    source = lax.broadcasted_iota(jnp.int32, (block, block), 1)
    group = source // tokens
    token = source - group * tokens
    line = token // tile_w
    place = token - line * tile_w
    target = (line * cols + group) * tile_w + place
    permute = jnp.where(at == target, 1.0, 0.0).astype(jnp.bfloat16)
    keys = k_buf[...]
    vals = v_buf[...]
    position = lax.broadcasted_iota(jnp.int32, (1, keys.shape[0]), 1)
    valid = (position >= padded_text) | (position < len_ref[0])
    o_copies = []
    for step in list(range(1, rows)) + [0]:
        peer = row_peer(step)
        queries = jnp.dot(permute, q_buf[peer], preferred_element_type=jnp.float32).astype(jnp.bfloat16)
        outs = []
        for head in range(out_w // HD):
            lanes = slice(head * HD, (head + 1) * HD)
            scores = (
                lax.dot_general(
                    queries[:, lanes],
                    keys[:, lanes],
                    (((1,), (1,)), ((), ())),
                    preferred_element_type=jnp.float32,
                )
                * 0.125
            )
            scores = jnp.where(valid, scores, -jnp.inf)
            weight = jnp.exp(scores - jnp.max(scores, axis=-1, keepdims=True))
            total = jnp.sum(weight, axis=-1, keepdims=True)
            outs.append(
                jnp.dot(weight.astype(jnp.bfloat16), vals[:, lanes], preferred_element_type=jnp.float32)
                / total
            )
        result = jnp.concatenate(outs, axis=-1).astype(jnp.bfloat16)
        if step == 0:
            recv_out[row] = result
        else:
            send_out[step - 1] = result
            copy = remote(
                send_out.at[step - 1],
                recv_out.at[row],
                o_send.at[step - 1],
                o_recv.at[step - 1],
                {"row": peer},
            )
            copy.start()
            o_copies.append(copy)
    for step in range(1, rows):
        source = lax.rem(row - step + rows, rows)
        remote(
            send_out.at[step - 1],
            recv_out.at[source],
            o_send.at[step - 1],
            o_recv.at[step - 1],
            {"row": row_peer(step)},
        ).wait_recv()
    for source in range(rows):
        out_ref[:, source * out_w : (source + 1) * out_w] = recv_out[source]
    for at, (down, right) in enumerate(SIDES):

        @pl.when(within(-down, -right))
        def sent(at=at, down=down, right=right):
            halo_copy(at, down, right).wait_send()

    for direction in range(2):
        for distance in range(1, cols):

            @pl.when(passes(direction, distance))
            def passed(direction=direction, distance=distance):
                z_copy(direction, distance, col - (distance - 1) * (1 - 2 * direction)).wait_send()

    for group in range(cols):
        for step in range(1, rows):
            part_copy(group, step).wait_send()
    for copy in mod_copies + [weight_copy] + x_copies + t_copies + o_copies:
        copy.wait_send()


def on_device_fast(
    rows, cols, latents, prompt_rows, peg_weight, modulation_weight, qkv_weight, text_len, timestep
):
    frames, tile_h, tile_w, width = latents.shape[1:]
    tokens = frames * tile_h * tile_w
    tile = latents.reshape(tokens, width)
    parts = 8
    narrow = width // parts
    pick, shift = (jnp.asarray(table, jnp.bfloat16) for table in halo_tables(frames, tile_h, tile_w, parts))
    temb = modulation_weight.shape[0]
    activation = jax.nn.silu(time_angles(timestep[0], temb)).astype(jnp.bfloat16)
    activation = jnp.broadcast_to(activation[None, :], (16, temb))
    depth, kinds, head_width = qkv_weight.shape
    out_w = head_width // rows
    by_dest = qkv_weight.reshape(depth, kinds, rows, out_w).transpose(2, 0, 1, 3)
    by_dest = by_dest.reshape(rows, depth, kinds * out_w)
    text = prompt_rows.shape[1]
    padded_text = -(-text // 16) * 16
    block = tokens * cols
    group_rows = tokens * rows
    bf16, f32 = jnp.bfloat16, jnp.float32
    dma = pltpu.SemaphoreType.DMA
    all_rows = padded_text + group_rows * cols
    attended = pl.pallas_call(
        functools.partial(layer_kernel, (rows, cols, text, padded_text, tile_w)),
        out_shape=jax.ShapeDtypeStruct((block, head_width), bf16),
        in_specs=[pl.BlockSpec(memory_space=pltpu.SMEM)] + [pl.BlockSpec(memory_space=space) for space in (VMEM,) * 4 + (pltpu.HBM, VMEM, pltpu.HBM, VMEM)],
        out_specs=pl.BlockSpec(memory_space=VMEM),
        scratch_shapes=[
            VMEM((text, width), bf16),
            VMEM(modulation_weight.shape, bf16),
            VMEM((4, 16, width // 2), bf16),
            VMEM((4, 16, width // 2), bf16),
            VMEM((64, narrow), bf16),
            VMEM((64, narrow), bf16),
            VMEM((tokens, width), bf16),
            dma((2,)),
            dma((8,)),
            dma((8,)),
            VMEM((cols, 1, modulation_weight.shape[1]), f32),
            VMEM((2, 1, width), f32),
            VMEM((rows, 2 * depth, kinds * out_w), bf16),
            VMEM((max(padded_text, tokens), width), bf16),
            VMEM((rows - 1, tokens, 2 * depth), bf16),
            VMEM((cols, group_rows, 2 * depth), bf16),
            VMEM((rows - 1, padded_text, 2 * out_w), bf16),
            VMEM((rows - 1, padded_text, 2 * out_w), bf16),
            VMEM((padded_text, 2 * out_w), f32),
            VMEM((cols, rows - 1, group_rows, kinds * out_w), bf16),
            VMEM((cols, rows - 1, group_rows, kinds * out_w), bf16),
            VMEM((cols, group_rows, kinds * out_w), f32),
            VMEM((rows, block, out_w), bf16),
            VMEM((all_rows, out_w), bf16),
            VMEM((all_rows, out_w), bf16),
            VMEM((rows - 1, block, out_w), bf16),
            VMEM((rows, block, out_w), bf16),
            dma((2,)),
            dma((cols - 1,)),
            dma((cols - 1,)),
            dma((rows - 1,)),
            dma((rows - 1,)),
            dma((2, cols - 1)),
            dma((2, cols - 1)),
            dma((rows - 1,)),
            dma((rows - 1,)),
            dma((cols, rows - 1)),
            dma((cols, rows - 1)),
            dma((rows - 1,)),
            dma((rows - 1,)),
        ],
        compiler_params=pltpu.CompilerParams(
            collective_id=0, has_side_effects=True, vmem_limit_bytes=48 * 1024 * 1024
        ),
    )(text_len, tile, pick, shift, peg_weight, prompt_rows[0], activation, modulation_weight, by_dest)
    return attended.reshape(1, frames, tile_h, tile_w * cols, head_width)


def solution(mesh):
    in_specs = (
        P("item", None, "row", "col", None),
        P("item", None, None),
        P(),
        P(None, "col"),
        P(("item", "row"), None, "col"),
        P("item"),
        P("item"),
    )
    out_specs = P("item", None, "row", None, "col")
    rows, cols, items = mesh.shape["row"], mesh.shape["col"], mesh.shape["item"]

    def on_device(*blocks):
        group = blocks[4].shape[2] // rows
        if items == 2 and cols % 2 == 0 and group >= 128 and group % 128 == 0 and blocks[0].shape[1:4] == (2, 4, 4):
            return on_device_fast(rows, cols, *blocks)
        return on_device_general(*blocks)

    return jax.shard_map(
        on_device, mesh=mesh, in_specs=in_specs, out_specs=out_specs, check_vma=False
    )
```

```python
import functools
import math

import jax
import jax.numpy as jnp
import numpy as np
from jax import lax
from jax.experimental import pallas as pl
from jax.experimental.pallas import tpu as pltpu
from jax.sharding import PartitionSpec as P

HD = 64
MESH = pl.DeviceIdType.MESH
VMEM = pltpu.VMEM


def with_halo(block, sides, width):
    for axis, dim in sides:
        count = lax.axis_size(axis)
        forward = [(i, i + 1) for i in range(count - 1)]
        backward = [(target, source) for source, target in forward]
        low = lax.ppermute(
            lax.slice_in_dim(block, block.shape[dim] - width, None, axis=dim), axis, forward
        )
        high = lax.ppermute(lax.slice_in_dim(block, 0, width, axis=dim), axis, backward)
        block = jnp.concatenate([low, block, high], axis=dim)
    return block


def time_angles(step, count):
    half = count // 2
    freqs = jnp.exp(-math.log(10000.0) * jnp.arange(half, dtype=jnp.float32) / half)
    angle = step.astype(jnp.float32) * freqs
    return jnp.concatenate([jnp.cos(angle), jnp.sin(angle)])


def modulate(rows, shift, scale):
    values = rows.astype(jnp.float32)
    center = jnp.mean(values, axis=-1, keepdims=True)
    centered = values - center
    spread = jnp.mean(centered * centered, axis=-1, keepdims=True)
    return (centered * lax.rsqrt(spread + 1e-06) * (1.0 + scale) + shift).astype(jnp.bfloat16)


def absorb(carry, queries, key_rows, value_rows, valid):
    running_max, running_sum, weighted = carry
    count = key_rows.shape[0]
    heads = queries.shape[1]
    key_heads = key_rows.reshape(count, heads, HD)
    value_heads = value_rows.reshape(count, heads, HD)
    scores = (
        jnp.einsum("rhd,bhd->rhb", queries, key_heads, preferred_element_type=jnp.float32) * 0.125
    )
    if valid is not None:
        scores = jnp.where(valid[None, None, :], scores, -jnp.inf)
    newest = jnp.maximum(running_max, jnp.max(scores, axis=-1))
    weights = jnp.exp(scores - newest[..., None])
    shrink_by = jnp.exp(running_max - newest)
    running_sum = running_sum * shrink_by + jnp.sum(weights, axis=-1)
    weighted = weighted * shrink_by[..., None] + jnp.einsum(
        "rhb,bhd->rhd",
        weights.astype(jnp.bfloat16),
        value_heads,
        preferred_element_type=jnp.float32,
    )
    return (newest, running_sum, weighted)


def on_device_general(latents, prompt_rows, peg_weight, modulation_weight, qkv_weight, text_len, timestep):
    tile_h = latents.shape[2]
    tile_w = latents.shape[3]
    width = latents.shape[4]
    padded = with_halo(latents, (("row", 2), ("col", 3)), 1)
    summed = latents.astype(jnp.float32)
    for row_tap in range(3):
        for col_tap in range(3):
            summed = summed + padded[
                :, :, row_tap : row_tap + tile_h, col_tap : col_tap + tile_w, :
            ].astype(jnp.float32) * peg_weight[row_tap, col_tap].astype(jnp.float32)
    convolved = summed.astype(jnp.bfloat16)
    activation = jax.nn.silu(time_angles(timestep[0], modulation_weight.shape[0])).astype(
        jnp.bfloat16
    )
    own_columns = jnp.dot(
        activation[None, :], modulation_weight, preferred_element_type=jnp.float32
    )
    modulation = lax.all_gather(own_columns, "col", axis=1, tiled=True)[0]
    shift = modulation[:width]
    scale = modulation[width:]
    group_rows = lax.all_gather(modulate(convolved, shift, scale), "col", axis=3, tiled=True)
    frames = group_rows.shape[1]
    grid_w = group_rows.shape[3]
    flat_rows = group_rows.reshape(-1, width)
    row_count = flat_rows.shape[0]
    text_normed = modulate(prompt_rows[0], shift, scale)
    text_count = text_normed.shape[0]
    head_width = qkv_weight.shape[2]
    full_weight = lax.all_gather(qkv_weight, ("item", "row"), axis=0, tiled=True)
    latent_proj = jnp.einsum(
        "rd,dkc->rkc", flat_rows, full_weight, preferred_element_type=jnp.float32
    )
    text_proj = jnp.einsum(
        "rd,dkc->rkc", text_normed, full_weight, preferred_element_type=jnp.float32
    )
    latent_qkv = latent_proj.astype(jnp.bfloat16)
    text_qkv = text_proj.astype(jnp.bfloat16)
    heads = head_width // HD
    queries = latent_qkv[:, 0, :].reshape(row_count, heads, HD)
    local_keys = latent_qkv[:, 1, :]
    local_values = latent_qkv[:, 2, :]
    text_valid = jnp.arange(text_count, dtype=jnp.int32) < text_len[0]
    start_carry = (
        jnp.full((row_count, heads), -jnp.inf, jnp.float32),
        jnp.zeros((row_count, heads), jnp.float32),
        jnp.zeros((row_count, heads, HD), jnp.float32),
    )
    text_carry = absorb(start_carry, queries, text_qkv[:, 1, :], text_qkv[:, 2, :], text_valid)
    key_rows = lax.all_gather(local_keys, "row", axis=0, tiled=True)
    value_rows = lax.all_gather(local_values, "row", axis=0, tiled=True)
    total_rows = key_rows.shape[0]
    block_count = total_rows // row_count

    def one_block(state, pair):
        return (absorb(state, queries, pair[0], pair[1], None), None)

    state, unused = lax.scan(
        one_block,
        text_carry,
        (
            key_rows.reshape(block_count, row_count, head_width),
            value_rows.reshape(block_count, row_count, head_width),
        ),
    )
    running_max, running_sum, weighted = state
    attended = (weighted / running_sum[..., None]).astype(jnp.bfloat16)
    return attended.reshape(1, frames, tile_h, grid_w, head_width)


def centered_rows(values):
    center = jnp.mean(values, axis=-1, keepdims=True)
    centered = values - center
    spread = jnp.mean(centered * centered, axis=-1, keepdims=True)
    return centered * lax.rsqrt(spread + 1e-06)


SIDES = ((-1, 0), (1, 0), (0, -1), (0, 1), (-1, -1), (-1, 1), (1, -1), (1, 1))


def halo_tables(frames, tile_h, tile_w, parts):
    tokens = frames * tile_h * tile_w
    edge = frames * tile_h

    def token(f, h, w):
        return (f * tile_h + h) * tile_w + w

    pick = np.zeros((1 + parts, 64, tokens), np.float32)
    shift = np.zeros((parts, 8 * tokens, tokens + 8 * edge + 64), np.float32)
    last_h, last_w = tile_h - 1, tile_w - 1
    for at, (down, right) in enumerate(SIDES):
        h_from = last_h if down < 0 else 0
        w_from = last_w if right < 0 else 0
        for f in range(frames):
            if at < 4:
                for k in range(tile_h):
                    source = token(f, h_from, k) if down else token(f, k, w_from)
                    pick[0, at * edge + f * tile_h + k, source] = 1
            else:
                for part in range(parts):
                    pick[1 + part, (at - 4) * 16 + part * frames + f, token(f, h_from, w_from)] = 1
        for part in range(parts):
            upper = part // (parts // 2)
            for f in range(frames):
                for h in range(tile_h):
                    for w in range(tile_w):
                        y, x = h + down, w + right
                        out_y = -1 if y < 0 else (1 if y > last_h else 0)
                        out_x = -1 if x < 0 else (1 if x > last_w else 0)
                        if out_y == 0 and out_x == 0:
                            source = token(f, y, x)
                        else:
                            slot = SIDES.index((out_y, out_x))
                            if slot < 4:
                                k = x if out_y else y
                                source = tokens + slot * 2 * edge + upper * edge + f * tile_h + k
                            else:
                                source = tokens + 8 * edge + (slot - 4) * 16 + part * frames + f
                        shift[part, at * tokens + token(f, h, w), source] = 1
    return pick, shift


def layer_kernel(
    sizes,
    len_ref,
    tile_ref,
    pick_ref,
    shift_hbm,
    peg_ref,
    prompt_hbm,
    act_ref,
    mod_hbm,
    weight_hbm,
    out_ref,
    shift_ref,
    prompt_ref,
    mod_ref,
    side_send,
    side_in,
    corner_send,
    corner_in,
    conv,
    local_sems,
    halo_send,
    halo_recv,
    mod_buf,
    affine,
    weights,
    text_in,
    send_x,
    grid_x,
    send_text,
    recv_text,
    own_text,
    send_part,
    recv_part,
    own_part,
    q_buf,
    k_buf,
    v_buf,
    send_out,
    recv_out,
    w_sems,
    mod_send,
    mod_recv,
    x_send,
    x_recv,
    z_send,
    z_recv,
    t_send,
    t_recv,
    p_send,
    p_recv,
    o_send,
    o_recv,
):
    rows, cols, text, padded_text, tile_w = sizes
    tokens, width = tile_ref.shape
    depth = weight_hbm.shape[1]
    out_w = weight_hbm.shape[2] // rows
    block = tokens * cols
    item = lax.axis_index("item")
    row = lax.axis_index("row")
    col = lax.axis_index("col")

    def row_peer(step):
        return lax.rem(row + step, rows)

    def col_peer(step):
        return lax.rem(col + step, cols)

    def remote(src, dst, send, recv, where):
        return pltpu.make_async_remote_copy(
            src_ref=src, dst_ref=dst, send_sem=send, recv_sem=recv, device_id=where, device_id_type=MESH
        )

    prompt_copy = pltpu.make_async_copy(prompt_hbm, prompt_ref, local_sems.at[0])
    mod_copy = pltpu.make_async_copy(mod_hbm, mod_ref, local_sems.at[1])
    shift_copy = pltpu.make_async_copy(shift_hbm, shift_ref, local_sems.at[2])
    stage_copies = []
    for kind in range(3):
        for dest in range(rows):
            stage_copies.append(
                pltpu.make_async_copy(
                    weight_hbm.at[kind, :, dest * out_w : (dest + 1) * out_w],
                    weights.at[dest, 0:depth, kind * out_w : (kind + 1) * out_w],
                    local_sems.at[3 + kind * rows + dest],
                )
            )
    mod_copy.start()
    for copy in stage_copies:
        copy.start()
    prompt_copy.start()
    shift_copy.start()
    side_in[...] = jnp.zeros_like(side_in)
    corner_in[...] = jnp.zeros_like(corner_in)

    def within(down, right):
        r, c = row + down, col + right
        return (r >= 0) & (r < rows) & (c >= 0) & (c < cols)

    barrier = pltpu.get_barrier_semaphore()
    for down, right in SIDES[4:]:

        @pl.when(within(down, right))
        def greet(down=down, right=right):
            pl.semaphore_signal(
                barrier, inc=1, device_id={"row": row + down, "col": col + right}, device_id_type=MESH
            )

    pl.semaphore_signal(barrier, inc=1, device_id={"item": 1 - item}, device_id_type=MESH)
    for step in range(1, rows):
        pl.semaphore_signal(barrier, inc=1, device_id={"row": row_peer(step)}, device_id_type=MESH)
    for step in range(1, cols):
        pl.semaphore_signal(barrier, inc=1, device_id={"col": col_peer(step)}, device_id_type=MESH)

    tile = tile_ref[...]
    wide = side_in.shape[2]
    narrow = corner_in.shape[1]
    edge = side_in.shape[1] // 2
    picked = jnp.dot(pick_ref[0, 0 : 4 * edge], tile, preferred_element_type=jnp.float32)
    for side in range(4):
        lines = picked[side * edge : (side + 1) * edge]
        side_send[side] = jnp.concatenate([lines[:, :wide], lines[:, wide:]], axis=0).astype(jnp.bfloat16)
    corners = jnp.zeros((corner_in.shape[0], narrow), jnp.float32)
    for part in range(width // narrow):
        corners = corners + jnp.dot(
            pick_ref[1 + part],
            tile[:, part * narrow : (part + 1) * narrow],
            preferred_element_type=jnp.float32,
        )
    corner_send[...] = corners.astype(jnp.bfloat16)

    def halo_copy(at, down, right):
        if at < 4:
            src, dst = side_send.at[at], side_in.at[at]
        else:
            lines = pl.ds((at - 4) * 16, 16)
            src, dst = corner_send.at[lines, :], corner_in.at[lines, :]
        return remote(
            src, dst, halo_send.at[at], halo_recv.at[at], {"row": row - down, "col": col - right}
        )

    mod_copy.wait()
    own_columns = jnp.dot(act_ref[...], mod_ref[...], preferred_element_type=jnp.float32)
    mod_buf[col] = own_columns[0:1, :]
    beside_rows = (row + rows - 1) // rows + (2 * rows - 2 - row) // rows
    beside_cols = (col + cols - 1) // cols + (2 * cols - 2 - col) // cols
    pl.semaphore_wait(barrier, rows + cols - 1 + beside_rows * beside_cols)
    for at, (down, right) in enumerate(SIDES):

        @pl.when(within(-down, -right))
        def send(at=at, down=down, right=right):
            halo_copy(at, down, right).start()

    mod_copies = []
    for step in range(1, cols):
        copy = remote(
            mod_buf.at[col],
            mod_buf.at[col],
            mod_send.at[step - 1],
            mod_recv.at[step - 1],
            {"col": col_peer(step)},
        )
        copy.start()
        mod_copies.append(copy)
    for copy in stage_copies:
        copy.wait()
    weight_copy = remote(
        weights.at[:, 0:depth, :],
        weights.at[:, pl.ds(depth, depth), :],
        w_sems.at[0],
        w_sems.at[1],
        {"item": 1 - item},
    )
    weight_copy.start()
    prompt_copy.wait()
    text_stats = []
    for start_row in range(0, padded_text, 16):
        count = min(16, text - start_row)
        values = prompt_ref[start_row : start_row + count, :].astype(jnp.float32)
        center = jnp.mean(values, axis=-1, keepdims=True)
        centered = values - center
        spread = lax.rsqrt(jnp.mean(centered * centered, axis=-1, keepdims=True) + 1e-06)
        text_stats.append((center, spread))

    for at, (down, right) in enumerate(SIDES):

        @pl.when(within(down, right))
        def receive(at=at, down=down, right=right):
            halo_copy(at, down, right).wait_recv()

    shift_copy.wait()
    for part in range(width // narrow):
        lanes = slice(part * narrow, (part + 1) * narrow)
        upper, start = divmod(part * narrow, wide)
        pieces = [tile[:, lanes]]
        for side in range(4):
            pieces.append(side_in[side, :, start : start + narrow])
        pieces.append(corner_in[...])
        moved = jnp.dot(
            shift_ref[part], jnp.concatenate(pieces, axis=0), preferred_element_type=jnp.float32
        )
        own = tile[:, lanes].astype(jnp.float32)
        taps = [peg_ref[a, :, lanes].astype(jnp.float32) for a in range(3)]
        summed = own + own * taps[1][1:2]
        for at, (down, right) in enumerate(SIDES):
            summed = summed + moved[at * tokens : (at + 1) * tokens] * taps[down + 1][right + 1 : right + 2]
        conv[:, lanes] = summed.astype(jnp.bfloat16)
    tile_normal = centered_rows(conv[...].astype(jnp.float32))
    for step in range(1, cols):
        remote(
            mod_buf.at[col],
            mod_buf.at[lax.rem(col - step + cols, cols)],
            mod_send.at[step - 1],
            mod_recv.at[step - 1],
            {"col": col_peer(step)},
        ).wait_recv()
    half = cols // 2
    piece = mod_buf.shape[2]
    for part in range(half):
        affine[0, :, part * piece : (part + 1) * piece] = mod_buf[part]
        affine[1, :, part * piece : (part + 1) * piece] = 1.0 + mod_buf[half + part]

    def depth_slices(dest):
        first = (item * rows + dest) * depth
        second = ((1 - item) * rows + dest) * depth
        return (pl.multiple_of(first, depth), pl.multiple_of(second, depth))

    text_in[0:tokens, :] = (tile_normal * affine[1] + affine[0]).astype(jnp.bfloat16)
    x_copies = []
    for step in range(1, rows):
        peer = row_peer(step)
        for order, start in enumerate(depth_slices(peer)):
            send_x[step - 1, :, order * depth : (order + 1) * depth] = text_in[
                0:tokens, pl.ds(start, depth)
            ]
        copy = remote(
            send_x.at[step - 1],
            grid_x.at[col, pl.ds(pl.multiple_of(row * tokens, tokens), tokens), :],
            x_send.at[step - 1],
            x_recv.at[step - 1],
            {"row": peer},
        )
        copy.start()
        x_copies.append(copy)
    own_slices = depth_slices(row)
    for order, start in enumerate(own_slices):
        grid_x[
            col, pl.ds(pl.multiple_of(row * tokens, tokens), tokens), order * depth : (order + 1) * depth
        ] = text_in[0:tokens, pl.ds(start, depth)]

    weight_copy.wait_recv()

    scale_pieces = [affine[1, :, pl.ds(start, depth)] for start in own_slices]
    shift_pieces = [affine[0, :, pl.ds(start, depth)] for start in own_slices]
    for start_row in range(0, padded_text, 16):
        count = min(16, text - start_row)
        center, spread = text_stats[start_row // 16]
        for order, start in enumerate(own_slices):
            part = prompt_ref[start_row : start_row + count, pl.ds(start, depth)].astype(jnp.float32)
            normed = (part - center) * spread * scale_pieces[order] + shift_pieces[order]
            if count < 16:
                normed = jnp.concatenate([normed, jnp.zeros((16 - count, depth), jnp.float32)], axis=0)
            text_in[start_row : start_row + 16, order * depth : (order + 1) * depth] = normed.astype(
                jnp.bfloat16
            )
    text_values = text_in[:, 0 : 2 * depth]
    t_copies = []
    for step in range(1, rows):
        peer = row_peer(step)
        send_text[step - 1] = jnp.dot(
            text_values, weights[peer, :, out_w:], preferred_element_type=jnp.float32
        ).astype(jnp.bfloat16)
        copy = remote(
            send_text.at[step - 1],
            recv_text.at[step - 1],
            t_send.at[step - 1],
            t_recv.at[step - 1],
            {"row": peer},
        )
        copy.start()
        t_copies.append(copy)
    own_text[...] = jnp.dot(text_values, weights[row, :, out_w:], preferred_element_type=jnp.float32)

    for step in range(1, rows):
        source = lax.rem(row - step + rows, rows)
        remote(
            send_x.at[step - 1],
            grid_x.at[col, pl.ds(pl.multiple_of(source * tokens, tokens), tokens), :],
            x_send.at[step - 1],
            x_recv.at[step - 1],
            {"row": row_peer(step)},
        ).wait_recv()
    def z_copy(direction, distance, source):
        sign = 1 - 2 * direction
        return remote(
            grid_x.at[source],
            grid_x.at[source],
            z_send.at[direction, distance - 1],
            z_recv.at[direction, distance - 1],
            {"col": col + sign},
        )

    def passes(direction, distance):
        home = col - (distance - 1) * (1 - 2 * direction)
        return (home >= 0) & (home < cols) & (col < cols - 1 if direction == 0 else col > 0)

    def arrives(direction, distance):
        home = col - distance * (1 - 2 * direction)
        return (home >= 0) & (home < cols)

    def pass_on(distance):
        for direction in range(2):

            @pl.when(passes(direction, distance))
            def start(direction=direction):
                z_copy(direction, distance, col - (distance - 1) * (1 - 2 * direction)).start()

    pass_on(1)

    def part_copy(group, step):
        return remote(
            send_part.at[group, step - 1],
            recv_part.at[group, step - 1],
            p_send.at[group, step - 1],
            p_recv.at[group, step - 1],
            {"row": row_peer(step)},
        )

    def latent_part(group):
        values = grid_x[group]
        for step in range(1, rows):
            send_part[group, step - 1] = jnp.dot(
                values, weights[row_peer(step)], preferred_element_type=jnp.float32
            ).astype(jnp.bfloat16)
            part_copy(group, step).start()
        own_part[group] = jnp.dot(values, weights[row], preferred_element_type=jnp.float32)

    latent_part(col)
    for distance in range(1, cols):
        for direction in range(2):

            @pl.when(arrives(direction, distance))
            def landed(direction=direction, distance=distance):
                z_copy(direction, distance, col - distance * (1 - 2 * direction)).wait_recv()

        if distance < cols - 1:
            pass_on(distance + 1)
        for direction in range(2):

            @pl.when(arrives(direction, distance))
            def multiply(direction=direction, distance=distance):
                latent_part(col - distance * (1 - 2 * direction))

    for copy in t_copies:
        copy.wait_recv()
    total = own_text[...]
    for step in range(1, rows):
        total = total + recv_text[step - 1].astype(jnp.float32)
    k_buf[0:padded_text, :] = total[:, 0:out_w].astype(jnp.bfloat16)
    v_buf[0:padded_text, :] = total[:, out_w:].astype(jnp.bfloat16)
    for group in range(cols):
        for step in range(1, rows):
            part_copy(group, step).wait_recv()
        total = own_part[group]
        for step in range(1, rows):
            total = total + recv_part[group, step - 1].astype(jnp.float32)
        rounded = total.astype(jnp.bfloat16)
        per_col = rows * tokens
        base = padded_text + group * per_col
        k_buf[base : base + per_col, :] = rounded[:, out_w : 2 * out_w]
        v_buf[base : base + per_col, :] = rounded[:, 2 * out_w :]
        for dest in range(rows):
            q_buf[dest, group * tokens : (group + 1) * tokens, :] = rounded[
                dest * tokens : (dest + 1) * tokens, 0:out_w
            ]

    at = lax.broadcasted_iota(jnp.int32, (block, block), 0)
    source = lax.broadcasted_iota(jnp.int32, (block, block), 1)
    group = source // tokens
    token = source - group * tokens
    line = token // tile_w
    place = token - line * tile_w
    target = (line * cols + group) * tile_w + place
    permute = jnp.where(at == target, 1.0, 0.0).astype(jnp.bfloat16)
    keys = k_buf[...]
    vals = v_buf[...]
    position = lax.broadcasted_iota(jnp.int32, (1, keys.shape[0]), 1)
    valid = (position >= padded_text) | (position < len_ref[0])
    o_copies = []
    for step in list(range(1, rows)) + [0]:
        peer = row_peer(step)
        queries = jnp.dot(permute, q_buf[peer], preferred_element_type=jnp.float32).astype(jnp.bfloat16)
        outs = []
        for head in range(out_w // HD):
            lanes = slice(head * HD, (head + 1) * HD)
            scores = (
                lax.dot_general(
                    queries[:, lanes],
                    keys[:, lanes],
                    (((1,), (1,)), ((), ())),
                    preferred_element_type=jnp.float32,
                )
                * 0.125
            )
            scores = jnp.where(valid, scores, -jnp.inf)
            weight = jnp.exp(scores - jnp.max(scores, axis=-1, keepdims=True))
            total = jnp.sum(weight, axis=-1, keepdims=True)
            outs.append(
                jnp.dot(weight.astype(jnp.bfloat16), vals[:, lanes], preferred_element_type=jnp.float32)
                / total
            )
        result = jnp.concatenate(outs, axis=-1).astype(jnp.bfloat16)
        if step == 0:
            recv_out[row] = result
        else:
            send_out[step - 1] = result
            copy = remote(
                send_out.at[step - 1],
                recv_out.at[row],
                o_send.at[step - 1],
                o_recv.at[step - 1],
                {"row": peer},
            )
            copy.start()
            o_copies.append(copy)
    for step in range(1, rows):
        source = lax.rem(row - step + rows, rows)
        remote(
            send_out.at[step - 1],
            recv_out.at[source],
            o_send.at[step - 1],
            o_recv.at[step - 1],
            {"row": row_peer(step)},
        ).wait_recv()
    for source in range(rows):
        out_ref[:, source * out_w : (source + 1) * out_w] = recv_out[source]
    for at, (down, right) in enumerate(SIDES):

        @pl.when(within(-down, -right))
        def sent(at=at, down=down, right=right):
            halo_copy(at, down, right).wait_send()

    for direction in range(2):
        for distance in range(1, cols):

            @pl.when(passes(direction, distance))
            def passed(direction=direction, distance=distance):
                z_copy(direction, distance, col - (distance - 1) * (1 - 2 * direction)).wait_send()

    for group in range(cols):
        for step in range(1, rows):
            part_copy(group, step).wait_send()
    for copy in mod_copies + [weight_copy] + x_copies + t_copies + o_copies:
        copy.wait_send()


def on_device_fast(
    rows, cols, latents, prompt_rows, peg_weight, modulation_weight, qkv_weight, text_len, timestep
):
    frames, tile_h, tile_w, width = latents.shape[1:]
    tokens = frames * tile_h * tile_w
    tile = latents.reshape(tokens, width)
    parts = 8
    narrow = width // parts
    pick, shift = (jnp.asarray(table, jnp.bfloat16) for table in halo_tables(frames, tile_h, tile_w, parts))
    temb = modulation_weight.shape[0]
    activation = jax.nn.silu(time_angles(timestep[0], temb)).astype(jnp.bfloat16)
    activation = jnp.broadcast_to(activation[None, :], (16, temb))
    depth, kinds, head_width = qkv_weight.shape
    out_w = head_width // rows
    by_kind = qkv_weight.transpose(1, 0, 2)
    text = prompt_rows.shape[1]
    padded_text = -(-text // 16) * 16
    block = tokens * cols
    group_rows = tokens * rows
    bf16, f32 = jnp.bfloat16, jnp.float32
    dma = pltpu.SemaphoreType.DMA
    all_rows = padded_text + group_rows * cols
    attended = pl.pallas_call(
        functools.partial(layer_kernel, (rows, cols, text, padded_text, tile_w)),
        out_shape=jax.ShapeDtypeStruct((block, head_width), bf16),
        in_specs=[pl.BlockSpec(memory_space=pltpu.SMEM)] + [pl.BlockSpec(memory_space=space) for space in (VMEM, VMEM, pltpu.HBM, VMEM, pltpu.HBM, VMEM, pltpu.HBM, pltpu.HBM)],
        out_specs=pl.BlockSpec(memory_space=VMEM),
        scratch_shapes=[
            VMEM(shift.shape, bf16),
            VMEM((text, width), bf16),
            VMEM(modulation_weight.shape, bf16),
            VMEM((4, 16, width // 2), bf16),
            VMEM((4, 16, width // 2), bf16),
            VMEM((64, narrow), bf16),
            VMEM((64, narrow), bf16),
            VMEM((tokens, width), bf16),
            dma((3 + 3 * rows,)),
            dma((8,)),
            dma((8,)),
            VMEM((cols, 1, modulation_weight.shape[1]), f32),
            VMEM((2, 1, width), f32),
            VMEM((rows, 2 * depth, kinds * out_w), bf16),
            VMEM((max(padded_text, tokens), width), bf16),
            VMEM((rows - 1, tokens, 2 * depth), bf16),
            VMEM((cols, group_rows, 2 * depth), bf16),
            VMEM((rows - 1, padded_text, 2 * out_w), bf16),
            VMEM((rows - 1, padded_text, 2 * out_w), bf16),
            VMEM((padded_text, 2 * out_w), f32),
            VMEM((cols, rows - 1, group_rows, kinds * out_w), bf16),
            VMEM((cols, rows - 1, group_rows, kinds * out_w), bf16),
            VMEM((cols, group_rows, kinds * out_w), f32),
            VMEM((rows, block, out_w), bf16),
            VMEM((all_rows, out_w), bf16),
            VMEM((all_rows, out_w), bf16),
            VMEM((rows - 1, block, out_w), bf16),
            VMEM((rows, block, out_w), bf16),
            dma((2,)),
            dma((cols - 1,)),
            dma((cols - 1,)),
            dma((rows - 1,)),
            dma((rows - 1,)),
            dma((2, cols - 1)),
            dma((2, cols - 1)),
            dma((rows - 1,)),
            dma((rows - 1,)),
            dma((cols, rows - 1)),
            dma((cols, rows - 1)),
            dma((rows - 1,)),
            dma((rows - 1,)),
        ],
        compiler_params=pltpu.CompilerParams(
            collective_id=0, has_side_effects=True, vmem_limit_bytes=58 * 1024 * 1024
        ),
    )(text_len, tile, pick, shift, peg_weight, prompt_rows[0], activation, modulation_weight, by_kind)
    return attended.reshape(1, frames, tile_h, tile_w * cols, head_width)


def solution(mesh):
    in_specs = (
        P("item", None, "row", "col", None),
        P("item", None, None),
        P(),
        P(None, "col"),
        P(("item", "row"), None, "col"),
        P("item"),
        P("item"),
    )
    out_specs = P("item", None, "row", None, "col")
    rows, cols, items = mesh.shape["row"], mesh.shape["col"], mesh.shape["item"]

    def on_device(*blocks):
        group = blocks[4].shape[2] // rows
        if items == 2 and cols % 2 == 0 and group >= 128 and group % 128 == 0 and blocks[0].shape[1:4] == (2, 4, 4):
            return on_device_fast(rows, cols, *blocks)
        return on_device_general(*blocks)

    return jax.shard_map(
        on_device, mesh=mesh, in_specs=in_specs, out_specs=out_specs, check_vma=False
    )
```

```python
import functools
import math

import jax
import jax.numpy as jnp
import numpy as np
from jax import lax
from jax.experimental import pallas as pl
from jax.experimental.pallas import tpu as pltpu
from jax.sharding import PartitionSpec as P

HD = 64
MESH = pl.DeviceIdType.MESH
VMEM = pltpu.VMEM


def with_halo(block, sides, width):
    for axis, dim in sides:
        count = lax.axis_size(axis)
        forward = [(i, i + 1) for i in range(count - 1)]
        backward = [(target, source) for source, target in forward]
        low = lax.ppermute(
            lax.slice_in_dim(block, block.shape[dim] - width, None, axis=dim), axis, forward
        )
        high = lax.ppermute(lax.slice_in_dim(block, 0, width, axis=dim), axis, backward)
        block = jnp.concatenate([low, block, high], axis=dim)
    return block


def time_angles(step, count):
    half = count // 2
    freqs = jnp.exp(-math.log(10000.0) * jnp.arange(half, dtype=jnp.float32) / half)
    angle = step.astype(jnp.float32) * freqs
    return jnp.concatenate([jnp.cos(angle), jnp.sin(angle)])


def modulate(rows, shift, scale):
    values = rows.astype(jnp.float32)
    center = jnp.mean(values, axis=-1, keepdims=True)
    centered = values - center
    spread = jnp.mean(centered * centered, axis=-1, keepdims=True)
    return (centered * lax.rsqrt(spread + 1e-06) * (1.0 + scale) + shift).astype(jnp.bfloat16)


def absorb(carry, queries, key_rows, value_rows, valid):
    running_max, running_sum, weighted = carry
    count = key_rows.shape[0]
    heads = queries.shape[1]
    key_heads = key_rows.reshape(count, heads, HD)
    value_heads = value_rows.reshape(count, heads, HD)
    scores = (
        jnp.einsum("rhd,bhd->rhb", queries, key_heads, preferred_element_type=jnp.float32) * 0.125
    )
    if valid is not None:
        scores = jnp.where(valid[None, None, :], scores, -jnp.inf)
    newest = jnp.maximum(running_max, jnp.max(scores, axis=-1))
    weights = jnp.exp(scores - newest[..., None])
    shrink_by = jnp.exp(running_max - newest)
    running_sum = running_sum * shrink_by + jnp.sum(weights, axis=-1)
    weighted = weighted * shrink_by[..., None] + jnp.einsum(
        "rhb,bhd->rhd",
        weights.astype(jnp.bfloat16),
        value_heads,
        preferred_element_type=jnp.float32,
    )
    return (newest, running_sum, weighted)


def on_device_general(latents, prompt_rows, peg_weight, modulation_weight, qkv_weight, text_len, timestep):
    tile_h = latents.shape[2]
    tile_w = latents.shape[3]
    width = latents.shape[4]
    padded = with_halo(latents, (("row", 2), ("col", 3)), 1)
    summed = latents.astype(jnp.float32)
    for row_tap in range(3):
        for col_tap in range(3):
            summed = summed + padded[
                :, :, row_tap : row_tap + tile_h, col_tap : col_tap + tile_w, :
            ].astype(jnp.float32) * peg_weight[row_tap, col_tap].astype(jnp.float32)
    convolved = summed.astype(jnp.bfloat16)
    activation = jax.nn.silu(time_angles(timestep[0], modulation_weight.shape[0])).astype(
        jnp.bfloat16
    )
    own_columns = jnp.dot(
        activation[None, :], modulation_weight, preferred_element_type=jnp.float32
    )
    modulation = lax.all_gather(own_columns, "col", axis=1, tiled=True)[0]
    shift = modulation[:width]
    scale = modulation[width:]
    group_rows = lax.all_gather(modulate(convolved, shift, scale), "col", axis=3, tiled=True)
    frames = group_rows.shape[1]
    grid_w = group_rows.shape[3]
    flat_rows = group_rows.reshape(-1, width)
    row_count = flat_rows.shape[0]
    text_normed = modulate(prompt_rows[0], shift, scale)
    text_count = text_normed.shape[0]
    head_width = qkv_weight.shape[2]
    full_weight = lax.all_gather(qkv_weight, ("item", "row"), axis=0, tiled=True)
    latent_proj = jnp.einsum(
        "rd,dkc->rkc", flat_rows, full_weight, preferred_element_type=jnp.float32
    )
    text_proj = jnp.einsum(
        "rd,dkc->rkc", text_normed, full_weight, preferred_element_type=jnp.float32
    )
    latent_qkv = latent_proj.astype(jnp.bfloat16)
    text_qkv = text_proj.astype(jnp.bfloat16)
    heads = head_width // HD
    queries = latent_qkv[:, 0, :].reshape(row_count, heads, HD)
    local_keys = latent_qkv[:, 1, :]
    local_values = latent_qkv[:, 2, :]
    text_valid = jnp.arange(text_count, dtype=jnp.int32) < text_len[0]
    start_carry = (
        jnp.full((row_count, heads), -jnp.inf, jnp.float32),
        jnp.zeros((row_count, heads), jnp.float32),
        jnp.zeros((row_count, heads, HD), jnp.float32),
    )
    text_carry = absorb(start_carry, queries, text_qkv[:, 1, :], text_qkv[:, 2, :], text_valid)
    key_rows = lax.all_gather(local_keys, "row", axis=0, tiled=True)
    value_rows = lax.all_gather(local_values, "row", axis=0, tiled=True)
    total_rows = key_rows.shape[0]
    block_count = total_rows // row_count

    def one_block(state, pair):
        return (absorb(state, queries, pair[0], pair[1], None), None)

    state, unused = lax.scan(
        one_block,
        text_carry,
        (
            key_rows.reshape(block_count, row_count, head_width),
            value_rows.reshape(block_count, row_count, head_width),
        ),
    )
    running_max, running_sum, weighted = state
    attended = (weighted / running_sum[..., None]).astype(jnp.bfloat16)
    return attended.reshape(1, frames, tile_h, grid_w, head_width)


def centered_rows(values):
    center = jnp.mean(values, axis=-1, keepdims=True)
    centered = values - center
    spread = jnp.mean(centered * centered, axis=-1, keepdims=True)
    return centered * lax.rsqrt(spread + 1e-06)


SIDES = ((-1, 0), (1, 0), (0, -1), (0, 1), (-1, -1), (-1, 1), (1, -1), (1, 1))


def halo_tables(frames, tile_h, tile_w, parts):
    tokens = frames * tile_h * tile_w
    edge = frames * tile_h

    def token(f, h, w):
        return (f * tile_h + h) * tile_w + w

    pick = np.zeros((1 + parts, 64, tokens), np.float32)
    shift = np.zeros((parts, 8 * tokens, tokens + 8 * edge + 64), np.float32)
    last_h, last_w = tile_h - 1, tile_w - 1
    for at, (down, right) in enumerate(SIDES):
        h_from = last_h if down < 0 else 0
        w_from = last_w if right < 0 else 0
        for f in range(frames):
            if at < 4:
                for k in range(tile_h):
                    source = token(f, h_from, k) if down else token(f, k, w_from)
                    pick[0, at * edge + f * tile_h + k, source] = 1
            else:
                for part in range(parts):
                    pick[1 + part, (at - 4) * 16 + part * frames + f, token(f, h_from, w_from)] = 1
        for part in range(parts):
            upper = part // (parts // 2)
            for f in range(frames):
                for h in range(tile_h):
                    for w in range(tile_w):
                        y, x = h + down, w + right
                        out_y = -1 if y < 0 else (1 if y > last_h else 0)
                        out_x = -1 if x < 0 else (1 if x > last_w else 0)
                        if out_y == 0 and out_x == 0:
                            source = token(f, y, x)
                        else:
                            slot = SIDES.index((out_y, out_x))
                            if slot < 4:
                                k = x if out_y else y
                                source = tokens + slot * 2 * edge + upper * edge + f * tile_h + k
                            else:
                                source = tokens + 8 * edge + (slot - 4) * 16 + part * frames + f
                        shift[part, at * tokens + token(f, h, w), source] = 1
    return pick, shift


def layer_kernel(
    sizes,
    len_ref,
    tile_ref,
    pick_ref,
    shift_hbm,
    peg_ref,
    prompt_hbm,
    act_ref,
    mod_hbm,
    weight_hbm,
    out_ref,
    shift_ref,
    prompt_ref,
    mod_ref,
    side_send,
    side_in,
    corner_send,
    corner_in,
    conv,
    local_sems,
    halo_send,
    halo_recv,
    mod_buf,
    affine,
    weights,
    text_in,
    send_x,
    grid_x,
    tile_buf,
    own_text,
    text_first,
    text_first_in,
    text_hold,
    text_second,
    text_second_in,
    own_part,
    part_first,
    part_first_in,
    part_hold,
    part_second,
    part_second_in,
    q_buf,
    k_buf,
    v_buf,
    send_out,
    recv_out,
    w_sems,
    mod_send,
    mod_recv,
    x_send,
    x_recv,
    z_send,
    z_recv,
    t_sems,
    p_sems,
    o_send,
    o_recv,
):
    rows, cols, text, padded_text, tile_w = sizes
    tokens, width = tile_buf.shape
    depth = weight_hbm.shape[1]
    out_w = weight_hbm.shape[2] // rows
    block = tokens * cols
    item = lax.axis_index("item")
    row = lax.axis_index("row")
    col = lax.axis_index("col")

    def row_peer(step):
        return lax.rem(row + step, rows)

    def col_peer(step):
        return lax.rem(col + step, cols)

    def remote(src, dst, send, recv, where):
        return pltpu.make_async_remote_copy(
            src_ref=src, dst_ref=dst, send_sem=send, recv_sem=recv, device_id=where, device_id_type=MESH
        )

    prompt_copy = pltpu.make_async_copy(prompt_hbm, prompt_ref, local_sems.at[0])
    mod_copy = pltpu.make_async_copy(mod_hbm, mod_ref, local_sems.at[1])
    shift_copy = pltpu.make_async_copy(shift_hbm, shift_ref, local_sems.at[2])
    stage_copies = []
    for kind in range(3):
        for dest in range(rows):
            stage_copies.append(
                pltpu.make_async_copy(
                    weight_hbm.at[kind, :, dest * out_w : (dest + 1) * out_w],
                    weights.at[dest, 0:depth, kind * out_w : (kind + 1) * out_w],
                    local_sems.at[3 + kind * rows + dest],
                )
            )
    mod_copy.start()
    for copy in stage_copies:
        copy.start()
    prompt_copy.start()
    shift_copy.start()
    side_in[...] = jnp.zeros_like(side_in)
    corner_in[...] = jnp.zeros_like(corner_in)

    def within(down, right):
        r, c = row + down, col + right
        return (r >= 0) & (r < rows) & (c >= 0) & (c < cols)

    near = (row + 1 - 2 * lax.rem(row, 2), row + 2 - 4 * lax.div(row, 2))
    across = 3 - row

    def first_copy(group, way, sems, first, first_in):
        return remote(
            first.at[group, way],
            first_in.at[group, way],
            sems.at[0, group, way],
            sems.at[1, group, way],
            {"row": near[way]},
        )

    def second_copy(group, way, sems, second, second_in):
        return remote(
            second.at[group, way],
            second_in.at[group, way],
            sems.at[2, group, way],
            sems.at[3, group, way],
            {"row": near[1 - way]},
        )

    def scatter_start(group, values, lane, own, first, first_in, hold, second, second_in, sems):
        def product(dest):
            return jnp.dot(values, weights[dest, :, lane:], preferred_element_type=jnp.float32)

        half = values.shape[0] // 2
        far = product(across)
        for way in range(2):
            first[group, way, 1] = far[way * half : (way + 1) * half].astype(jnp.bfloat16)
        for way in range(2):
            part = product(near[way])
            first[group, way, 0] = part[way * half : (way + 1) * half].astype(jnp.bfloat16)
            hold[group, 1 - way] = part[(1 - way) * half : (2 - way) * half]
            first_copy(group, way, sems, first, first_in).start()
        own[group] = product(row)

    def scatter_pass(group, own, first, first_in, hold, second, second_in, sems):
        half = hold.shape[2]
        for way in range(2):
            first_copy(group, way, sems, first, first_in).wait_recv()
            second[group, way] = (
                hold[group, way] + first_in[group, way, 1].astype(jnp.float32)
            ).astype(jnp.bfloat16)
            second_copy(group, way, sems, second, second_in).start()
            lines = slice(way * half, (way + 1) * half)
            own[group, lines] = own[group, lines] + first_in[group, way, 0].astype(jnp.float32)

    def scatter_end(group, own, first, first_in, hold, second, second_in, sems):
        sums = []
        half = hold.shape[2]
        for way in range(2):
            second_copy(group, way, sems, second, second_in).wait_recv()
            sums.append(
                own[group, way * half : (way + 1) * half] + second_in[group, way].astype(jnp.float32)
            )
        return jnp.concatenate(sums, axis=0).astype(jnp.bfloat16)

    text_state = (own_text, text_first, text_first_in, text_hold, text_second, text_second_in, t_sems)
    part_state = (own_part, part_first, part_first_in, part_hold, part_second, part_second_in, p_sems)

    barrier = pltpu.get_barrier_semaphore()
    for down, right in SIDES[4:]:

        @pl.when(within(down, right))
        def greet(down=down, right=right):
            pl.semaphore_signal(
                barrier, inc=1, device_id={"row": row + down, "col": col + right}, device_id_type=MESH
            )

    pl.semaphore_signal(barrier, inc=1, device_id={"item": 1 - item}, device_id_type=MESH)
    for step in range(1, rows):
        pl.semaphore_signal(barrier, inc=1, device_id={"row": row_peer(step)}, device_id_type=MESH)
    for step in range(1, cols):
        pl.semaphore_signal(barrier, inc=1, device_id={"col": col_peer(step)}, device_id_type=MESH)

    pieces = [
        tile_ref[0, f, h].astype(jnp.float32)
        for f in range(tile_ref.shape[1])
        for h in range(tile_ref.shape[2])
    ]
    tile_buf[...] = jnp.concatenate(pieces, axis=0).astype(jnp.bfloat16)
    tile = tile_buf[...]
    wide = side_in.shape[2]
    narrow = corner_in.shape[1]
    edge = side_in.shape[1] // 2
    picked = jnp.dot(pick_ref[0, 0 : 4 * edge], tile, preferred_element_type=jnp.float32)
    for side in range(4):
        lines = picked[side * edge : (side + 1) * edge]
        side_send[side] = jnp.concatenate([lines[:, :wide], lines[:, wide:]], axis=0).astype(jnp.bfloat16)
    corners = jnp.zeros((corner_in.shape[0], narrow), jnp.float32)
    for part in range(width // narrow):
        corners = corners + jnp.dot(
            pick_ref[1 + part],
            tile[:, part * narrow : (part + 1) * narrow],
            preferred_element_type=jnp.float32,
        )
    corner_send[...] = corners.astype(jnp.bfloat16)

    def halo_copy(at, down, right):
        if at < 4:
            src, dst = side_send.at[at], side_in.at[at]
        else:
            lines = pl.ds((at - 4) * 16, 16)
            src, dst = corner_send.at[lines, :], corner_in.at[lines, :]
        return remote(
            src, dst, halo_send.at[at], halo_recv.at[at], {"row": row - down, "col": col - right}
        )

    mod_copy.wait()
    own_columns = jnp.dot(act_ref[...], mod_ref[...], preferred_element_type=jnp.float32)
    mod_buf[col] = own_columns[0:1, :]
    beside_rows = (row + rows - 1) // rows + (2 * rows - 2 - row) // rows
    beside_cols = (col + cols - 1) // cols + (2 * cols - 2 - col) // cols
    pl.semaphore_wait(barrier, rows + cols - 1 + beside_rows * beside_cols)
    for at, (down, right) in enumerate(SIDES):

        @pl.when(within(-down, -right))
        def send(at=at, down=down, right=right):
            halo_copy(at, down, right).start()

    mod_copies = []
    for step in range(1, cols):
        copy = remote(
            mod_buf.at[col],
            mod_buf.at[col],
            mod_send.at[step - 1],
            mod_recv.at[step - 1],
            {"col": col_peer(step)},
        )
        copy.start()
        mod_copies.append(copy)
    for copy in stage_copies:
        copy.wait()
    weight_copy = remote(
        weights.at[:, 0:depth, :],
        weights.at[:, pl.ds(depth, depth), :],
        w_sems.at[0],
        w_sems.at[1],
        {"item": 1 - item},
    )
    weight_copy.start()
    prompt_copy.wait()
    text_stats = []
    for start_row in range(0, padded_text, 16):
        count = min(16, text - start_row)
        if count <= 0:
            continue
        values = prompt_ref[start_row : start_row + count, :].astype(jnp.float32)
        center = jnp.mean(values, axis=-1, keepdims=True)
        centered = values - center
        spread = lax.rsqrt(jnp.mean(centered * centered, axis=-1, keepdims=True) + 1e-06)
        text_stats.append((center, spread))

    for at, (down, right) in enumerate(SIDES):

        @pl.when(within(down, right))
        def receive(at=at, down=down, right=right):
            halo_copy(at, down, right).wait_recv()

    shift_copy.wait()
    for part in range(width // narrow):
        lanes = slice(part * narrow, (part + 1) * narrow)
        upper, start = divmod(part * narrow, wide)
        pieces = [tile[:, lanes]]
        for side in range(4):
            pieces.append(side_in[side, :, start : start + narrow])
        pieces.append(corner_in[...])
        moved = jnp.dot(
            shift_ref[part], jnp.concatenate(pieces, axis=0), preferred_element_type=jnp.float32
        )
        own = tile[:, lanes].astype(jnp.float32)
        taps = [peg_ref[a, :, lanes].astype(jnp.float32) for a in range(3)]
        summed = own + own * taps[1][1:2]
        for at, (down, right) in enumerate(SIDES):
            summed = summed + moved[at * tokens : (at + 1) * tokens] * taps[down + 1][right + 1 : right + 2]
        conv[:, lanes] = summed.astype(jnp.bfloat16)
    tile_normal = centered_rows(conv[...].astype(jnp.float32))
    for step in range(1, cols):
        remote(
            mod_buf.at[col],
            mod_buf.at[lax.rem(col - step + cols, cols)],
            mod_send.at[step - 1],
            mod_recv.at[step - 1],
            {"col": col_peer(step)},
        ).wait_recv()
    half = cols // 2
    piece = mod_buf.shape[2]
    for part in range(half):
        affine[0, :, part * piece : (part + 1) * piece] = mod_buf[part]
        affine[1, :, part * piece : (part + 1) * piece] = 1.0 + mod_buf[half + part]

    def depth_slices(dest):
        first = (item * rows + dest) * depth
        second = ((1 - item) * rows + dest) * depth
        return (pl.multiple_of(first, depth), pl.multiple_of(second, depth))

    text_in[0:tokens, :] = (tile_normal * affine[1] + affine[0]).astype(jnp.bfloat16)
    x_copies = []
    for step in range(1, rows):
        peer = row_peer(step)
        for order, start in enumerate(depth_slices(peer)):
            send_x[step - 1, :, order * depth : (order + 1) * depth] = text_in[
                0:tokens, pl.ds(start, depth)
            ]
        copy = remote(
            send_x.at[step - 1],
            grid_x.at[col, pl.ds(pl.multiple_of(row * tokens, tokens), tokens), :],
            x_send.at[step - 1],
            x_recv.at[step - 1],
            {"row": peer},
        )
        copy.start()
        x_copies.append(copy)
    own_slices = depth_slices(row)
    for order, start in enumerate(own_slices):
        grid_x[
            col, pl.ds(pl.multiple_of(row * tokens, tokens), tokens), order * depth : (order + 1) * depth
        ] = text_in[0:tokens, pl.ds(start, depth)]

    weight_copy.wait_recv()

    scale_pieces = [affine[1, :, pl.ds(start, depth)] for start in own_slices]
    shift_pieces = [affine[0, :, pl.ds(start, depth)] for start in own_slices]
    for start_row in range(0, padded_text, 16):
        count = min(16, text - start_row)
        if count <= 0:
            text_in[start_row : start_row + 16, 0 : 2 * depth] = jnp.zeros((16, 2 * depth), jnp.bfloat16)
            continue
        center, spread = text_stats[start_row // 16]
        for order, start in enumerate(own_slices):
            part = prompt_ref[start_row : start_row + count, pl.ds(start, depth)].astype(jnp.float32)
            normed = (part - center) * spread * scale_pieces[order] + shift_pieces[order]
            if count < 16:
                normed = jnp.concatenate([normed, jnp.zeros((16 - count, depth), jnp.float32)], axis=0)
            text_in[start_row : start_row + 16, order * depth : (order + 1) * depth] = normed.astype(
                jnp.bfloat16
            )
    text_values = text_in[:, 0 : 2 * depth]
    scatter_start(0, text_values, out_w, *text_state)

    for step in range(1, rows):
        source = lax.rem(row - step + rows, rows)
        remote(
            send_x.at[step - 1],
            grid_x.at[col, pl.ds(pl.multiple_of(source * tokens, tokens), tokens), :],
            x_send.at[step - 1],
            x_recv.at[step - 1],
            {"row": row_peer(step)},
        ).wait_recv()
    def z_copy(direction, distance, source):
        sign = 1 - 2 * direction
        return remote(
            grid_x.at[source],
            grid_x.at[source],
            z_send.at[direction, distance - 1],
            z_recv.at[direction, distance - 1],
            {"col": col + sign},
        )

    def passes(direction, distance):
        home = col - (distance - 1) * (1 - 2 * direction)
        return (home >= 0) & (home < cols) & (col < cols - 1 if direction == 0 else col > 0)

    def arrives(direction, distance):
        home = col - distance * (1 - 2 * direction)
        return (home >= 0) & (home < cols)

    def pass_on(distance):
        for direction in range(2):

            @pl.when(passes(direction, distance))
            def start(direction=direction):
                z_copy(direction, distance, col - (distance - 1) * (1 - 2 * direction)).start()

    pass_on(1)

    def pass_sums(distance):
        for direction in range(2):

            @pl.when(arrives(direction, distance))
            def forward(direction=direction):
                scatter_pass(col - distance * (1 - 2 * direction), *part_state)

    scatter_start(col, grid_x[col], 0, *part_state)
    scatter_pass(0, *text_state)
    for distance in range(1, cols):
        if distance == 1:
            scatter_pass(col, *part_state)
        else:
            pass_sums(distance - 1)
        for direction in range(2):

            @pl.when(arrives(direction, distance))
            def landed(direction=direction, distance=distance):
                z_copy(direction, distance, col - distance * (1 - 2 * direction)).wait_recv()

        if distance < cols - 1:
            pass_on(distance + 1)
        for direction in range(2):

            @pl.when(arrives(direction, distance))
            def multiply(direction=direction, distance=distance):
                group = col - distance * (1 - 2 * direction)
                scatter_start(group, grid_x[group], 0, *part_state)

    pass_sums(cols - 1)

    rounded = scatter_end(0, *text_state)
    k_buf[0:padded_text, :] = rounded[:, 0:out_w]
    v_buf[0:padded_text, :] = rounded[:, out_w:]
    for group in range(cols):
        rounded = scatter_end(group, *part_state)
        per_col = rows * tokens
        base = padded_text + group * per_col
        k_buf[base : base + per_col, :] = rounded[:, out_w : 2 * out_w]
        v_buf[base : base + per_col, :] = rounded[:, 2 * out_w :]
        for dest in range(rows):
            q_buf[dest, group * tokens : (group + 1) * tokens, :] = rounded[
                dest * tokens : (dest + 1) * tokens, 0:out_w
            ]

    at = lax.broadcasted_iota(jnp.int32, (block, block), 0)
    source = lax.broadcasted_iota(jnp.int32, (block, block), 1)
    group = source // tokens
    token = source - group * tokens
    line = token // tile_w
    place = token - line * tile_w
    target = (line * cols + group) * tile_w + place
    permute = jnp.where(at == target, 1.0, 0.0).astype(jnp.bfloat16)
    keys = k_buf[...]
    vals = v_buf[...]
    position = lax.broadcasted_iota(jnp.int32, (1, keys.shape[0]), 1)
    valid = (position >= padded_text) | (position < len_ref[0])
    o_copies = []
    for step in list(range(1, rows)) + [0]:
        peer = row_peer(step)
        queries = jnp.dot(permute, q_buf[peer], preferred_element_type=jnp.float32).astype(jnp.bfloat16)
        outs = []
        for head in range(out_w // HD):
            lanes = slice(head * HD, (head + 1) * HD)
            scores = (
                lax.dot_general(
                    queries[:, lanes],
                    keys[:, lanes],
                    (((1,), (1,)), ((), ())),
                    preferred_element_type=jnp.float32,
                )
                * 0.125
            )
            scores = jnp.where(valid, scores, -jnp.inf)
            weight = jnp.exp(scores - jnp.max(scores, axis=-1, keepdims=True))
            total = jnp.sum(weight, axis=-1, keepdims=True)
            outs.append(
                jnp.dot(weight.astype(jnp.bfloat16), vals[:, lanes], preferred_element_type=jnp.float32)
                / total
            )
        result = jnp.concatenate(outs, axis=-1).astype(jnp.bfloat16)
        if step == 0:
            recv_out[row] = result
        else:
            send_out[step - 1] = result
            copy = remote(
                send_out.at[step - 1],
                recv_out.at[row],
                o_send.at[step - 1],
                o_recv.at[step - 1],
                {"row": peer},
            )
            copy.start()
            o_copies.append(copy)
    for step in range(1, rows):
        source = lax.rem(row - step + rows, rows)
        remote(
            send_out.at[step - 1],
            recv_out.at[source],
            o_send.at[step - 1],
            o_recv.at[step - 1],
            {"row": row_peer(step)},
        ).wait_recv()
    for source in range(rows):
        out_ref[:, source * out_w : (source + 1) * out_w] = recv_out[source]
    for at, (down, right) in enumerate(SIDES):

        @pl.when(within(-down, -right))
        def sent(at=at, down=down, right=right):
            halo_copy(at, down, right).wait_send()

    for direction in range(2):
        for distance in range(1, cols):

            @pl.when(passes(direction, distance))
            def passed(direction=direction, distance=distance):
                z_copy(direction, distance, col - (distance - 1) * (1 - 2 * direction)).wait_send()

    for count, state in ((1, text_state), (cols, part_state)):
        own, first, first_in, hold, second, second_in, sems = state
        for group in range(count):
            for way in range(2):
                first_copy(group, way, sems, first, first_in).wait_send()
                second_copy(group, way, sems, second, second_in).wait_send()
    for copy in mod_copies + [weight_copy] + x_copies + o_copies:
        copy.wait_send()


def on_device_fast(
    rows, cols, latents, prompt_rows, peg_weight, modulation_weight, qkv_weight, text_len, timestep
):
    frames, tile_h, tile_w, width = latents.shape[1:]
    tokens = frames * tile_h * tile_w
    parts = 8
    narrow = width // parts
    pick, shift = (jnp.asarray(table, jnp.bfloat16) for table in halo_tables(frames, tile_h, tile_w, parts))
    temb = modulation_weight.shape[0]
    activation = jax.nn.silu(time_angles(timestep[0], temb)).astype(jnp.bfloat16)
    activation = jnp.broadcast_to(activation[None, :], (16, temb))
    depth, kinds, head_width = qkv_weight.shape
    out_w = head_width // rows
    by_kind = qkv_weight.transpose(1, 0, 2)
    text = prompt_rows.shape[1]
    padded_text = -(-text // 32) * 32
    block = tokens * cols
    group_rows = tokens * rows
    bf16, f32 = jnp.bfloat16, jnp.float32
    dma = pltpu.SemaphoreType.DMA
    all_rows = padded_text + group_rows * cols
    attended = pl.pallas_call(
        functools.partial(layer_kernel, (rows, cols, text, padded_text, tile_w)),
        out_shape=jax.ShapeDtypeStruct((block, head_width), bf16),
        in_specs=[pl.BlockSpec(memory_space=pltpu.SMEM)] + [pl.BlockSpec(memory_space=space) for space in (VMEM, VMEM, pltpu.HBM, VMEM, pltpu.HBM, VMEM, pltpu.HBM, pltpu.HBM)],
        out_specs=pl.BlockSpec(memory_space=VMEM),
        scratch_shapes=[
            VMEM(shift.shape, bf16),
            VMEM((text, width), bf16),
            VMEM(modulation_weight.shape, bf16),
            VMEM((4, 16, width // 2), bf16),
            VMEM((4, 16, width // 2), bf16),
            VMEM((64, narrow), bf16),
            VMEM((64, narrow), bf16),
            VMEM((tokens, width), bf16),
            dma((3 + 3 * rows,)),
            dma((8,)),
            dma((8,)),
            VMEM((cols, 1, modulation_weight.shape[1]), f32),
            VMEM((2, 1, width), f32),
            VMEM((rows, 2 * depth, kinds * out_w), bf16),
            VMEM((max(padded_text, tokens), width), bf16),
            VMEM((rows - 1, tokens, 2 * depth), bf16),
            VMEM((cols, group_rows, 2 * depth), bf16),
            VMEM((tokens, width), bf16),
            VMEM((1, padded_text, 2 * out_w), f32),
            VMEM((1, 2, 2, padded_text // 2, 2 * out_w), bf16),
            VMEM((1, 2, 2, padded_text // 2, 2 * out_w), bf16),
            VMEM((1, 2, padded_text // 2, 2 * out_w), f32),
            VMEM((1, 2, padded_text // 2, 2 * out_w), bf16),
            VMEM((1, 2, padded_text // 2, 2 * out_w), bf16),
            VMEM((cols, group_rows, kinds * out_w), f32),
            VMEM((cols, 2, 2, group_rows // 2, kinds * out_w), bf16),
            VMEM((cols, 2, 2, group_rows // 2, kinds * out_w), bf16),
            VMEM((cols, 2, group_rows // 2, kinds * out_w), f32),
            VMEM((cols, 2, group_rows // 2, kinds * out_w), bf16),
            VMEM((cols, 2, group_rows // 2, kinds * out_w), bf16),
            VMEM((rows, block, out_w), bf16),
            VMEM((all_rows, out_w), bf16),
            VMEM((all_rows, out_w), bf16),
            VMEM((rows - 1, block, out_w), bf16),
            VMEM((rows, block, out_w), bf16),
            dma((2,)),
            dma((cols - 1,)),
            dma((cols - 1,)),
            dma((rows - 1,)),
            dma((rows - 1,)),
            dma((2, cols - 1)),
            dma((2, cols - 1)),
            dma((4, 1, 2)),
            dma((4, cols, 2)),
            dma((rows - 1,)),
            dma((rows - 1,)),
        ],
        compiler_params=pltpu.CompilerParams(
            collective_id=0, has_side_effects=True, vmem_limit_bytes=58 * 1024 * 1024
        ),
    )(text_len, latents, pick, shift, peg_weight, prompt_rows[0], activation, modulation_weight, by_kind)
    return attended.reshape(1, frames, tile_h, tile_w * cols, head_width)


def solution(mesh):
    in_specs = (
        P("item", None, "row", "col", None),
        P("item", None, None),
        P(),
        P(None, "col"),
        P(("item", "row"), None, "col"),
        P("item"),
        P("item"),
    )
    out_specs = P("item", None, "row", None, "col")
    rows, cols, items = mesh.shape["row"], mesh.shape["col"], mesh.shape["item"]

    def on_device(*blocks):
        group = blocks[4].shape[2] // rows
        if items == 2 and rows == 4 and cols % 2 == 0 and group >= 128 and group % 128 == 0 and blocks[0].shape[1:4] == (2, 4, 4):
            return on_device_fast(rows, cols, *blocks)
        return on_device_general(*blocks)

    return jax.shard_map(
        on_device, mesh=mesh, in_specs=in_specs, out_specs=out_specs, check_vma=False
    )
```

```python
import functools
import math

import jax
import jax.numpy as jnp
import numpy as np
from jax import lax
from jax.experimental import pallas as pl
from jax.experimental.pallas import tpu as pltpu
from jax.sharding import PartitionSpec as P

HD = 64
MESH = pl.DeviceIdType.MESH
VMEM = pltpu.VMEM


def with_halo(block, sides, width):
    for axis, dim in sides:
        count = lax.axis_size(axis)
        forward = [(i, i + 1) for i in range(count - 1)]
        backward = [(target, source) for source, target in forward]
        low = lax.ppermute(
            lax.slice_in_dim(block, block.shape[dim] - width, None, axis=dim), axis, forward
        )
        high = lax.ppermute(lax.slice_in_dim(block, 0, width, axis=dim), axis, backward)
        block = jnp.concatenate([low, block, high], axis=dim)
    return block


def time_angles(step, count):
    half = count // 2
    freqs = jnp.exp(-math.log(10000.0) * jnp.arange(half, dtype=jnp.float32) / half)
    angle = step.astype(jnp.float32) * freqs
    return jnp.concatenate([jnp.cos(angle), jnp.sin(angle)])


def modulate(rows, shift, scale):
    values = rows.astype(jnp.float32)
    center = jnp.mean(values, axis=-1, keepdims=True)
    centered = values - center
    spread = jnp.mean(centered * centered, axis=-1, keepdims=True)
    return (centered * lax.rsqrt(spread + 1e-06) * (1.0 + scale) + shift).astype(jnp.bfloat16)


def absorb(carry, queries, key_rows, value_rows, valid):
    running_max, running_sum, weighted = carry
    count = key_rows.shape[0]
    heads = queries.shape[1]
    key_heads = key_rows.reshape(count, heads, HD)
    value_heads = value_rows.reshape(count, heads, HD)
    scores = (
        jnp.einsum("rhd,bhd->rhb", queries, key_heads, preferred_element_type=jnp.float32) * 0.125
    )
    if valid is not None:
        scores = jnp.where(valid[None, None, :], scores, -jnp.inf)
    newest = jnp.maximum(running_max, jnp.max(scores, axis=-1))
    weights = jnp.exp(scores - newest[..., None])
    shrink_by = jnp.exp(running_max - newest)
    running_sum = running_sum * shrink_by + jnp.sum(weights, axis=-1)
    weighted = weighted * shrink_by[..., None] + jnp.einsum(
        "rhb,bhd->rhd",
        weights.astype(jnp.bfloat16),
        value_heads,
        preferred_element_type=jnp.float32,
    )
    return (newest, running_sum, weighted)


def on_device_general(latents, prompt_rows, peg_weight, modulation_weight, qkv_weight, text_len, timestep):
    tile_h = latents.shape[2]
    tile_w = latents.shape[3]
    width = latents.shape[4]
    padded = with_halo(latents, (("row", 2), ("col", 3)), 1)
    summed = latents.astype(jnp.float32)
    for row_tap in range(3):
        for col_tap in range(3):
            summed = summed + padded[
                :, :, row_tap : row_tap + tile_h, col_tap : col_tap + tile_w, :
            ].astype(jnp.float32) * peg_weight[row_tap, col_tap].astype(jnp.float32)
    convolved = summed.astype(jnp.bfloat16)
    activation = jax.nn.silu(time_angles(timestep[0], modulation_weight.shape[0])).astype(
        jnp.bfloat16
    )
    own_columns = jnp.dot(
        activation[None, :], modulation_weight, preferred_element_type=jnp.float32
    )
    modulation = lax.all_gather(own_columns, "col", axis=1, tiled=True)[0]
    shift = modulation[:width]
    scale = modulation[width:]
    group_rows = lax.all_gather(modulate(convolved, shift, scale), "col", axis=3, tiled=True)
    frames = group_rows.shape[1]
    grid_w = group_rows.shape[3]
    flat_rows = group_rows.reshape(-1, width)
    row_count = flat_rows.shape[0]
    text_normed = modulate(prompt_rows[0], shift, scale)
    text_count = text_normed.shape[0]
    head_width = qkv_weight.shape[2]
    full_weight = lax.all_gather(qkv_weight, ("item", "row"), axis=0, tiled=True)
    latent_proj = jnp.einsum(
        "rd,dkc->rkc", flat_rows, full_weight, preferred_element_type=jnp.float32
    )
    text_proj = jnp.einsum(
        "rd,dkc->rkc", text_normed, full_weight, preferred_element_type=jnp.float32
    )
    latent_qkv = latent_proj.astype(jnp.bfloat16)
    text_qkv = text_proj.astype(jnp.bfloat16)
    heads = head_width // HD
    queries = latent_qkv[:, 0, :].reshape(row_count, heads, HD)
    local_keys = latent_qkv[:, 1, :]
    local_values = latent_qkv[:, 2, :]
    text_valid = jnp.arange(text_count, dtype=jnp.int32) < text_len[0]
    start_carry = (
        jnp.full((row_count, heads), -jnp.inf, jnp.float32),
        jnp.zeros((row_count, heads), jnp.float32),
        jnp.zeros((row_count, heads, HD), jnp.float32),
    )
    text_carry = absorb(start_carry, queries, text_qkv[:, 1, :], text_qkv[:, 2, :], text_valid)
    key_rows = lax.all_gather(local_keys, "row", axis=0, tiled=True)
    value_rows = lax.all_gather(local_values, "row", axis=0, tiled=True)
    total_rows = key_rows.shape[0]
    block_count = total_rows // row_count

    def one_block(state, pair):
        return (absorb(state, queries, pair[0], pair[1], None), None)

    state, unused = lax.scan(
        one_block,
        text_carry,
        (
            key_rows.reshape(block_count, row_count, head_width),
            value_rows.reshape(block_count, row_count, head_width),
        ),
    )
    running_max, running_sum, weighted = state
    attended = (weighted / running_sum[..., None]).astype(jnp.bfloat16)
    return attended.reshape(1, frames, tile_h, grid_w, head_width)


def centered_rows(values):
    center = jnp.mean(values, axis=-1, keepdims=True)
    centered = values - center
    spread = jnp.mean(centered * centered, axis=-1, keepdims=True)
    return centered * lax.rsqrt(spread + 1e-06)


SIDES = ((-1, 0), (1, 0), (0, -1), (0, 1), (-1, -1), (-1, 1), (1, -1), (1, 1))


def halo_tables(frames, tile_h, tile_w, parts):
    tokens = frames * tile_h * tile_w
    edge = frames * tile_h

    def token(f, h, w):
        return (f * tile_h + h) * tile_w + w

    pick = np.zeros((1 + parts, 64, tokens), np.float32)
    shift = np.zeros((parts, 8 * tokens, tokens + 8 * edge + 64), np.float32)
    last_h, last_w = tile_h - 1, tile_w - 1
    for at, (down, right) in enumerate(SIDES):
        h_from = last_h if down < 0 else 0
        w_from = last_w if right < 0 else 0
        for f in range(frames):
            if at < 4:
                for k in range(tile_h):
                    source = token(f, h_from, k) if down else token(f, k, w_from)
                    pick[0, at * edge + f * tile_h + k, source] = 1
            else:
                for part in range(parts):
                    pick[1 + part, (at - 4) * 16 + part * frames + f, token(f, h_from, w_from)] = 1
        for part in range(parts):
            upper = part // (parts // 2)
            for f in range(frames):
                for h in range(tile_h):
                    for w in range(tile_w):
                        y, x = h + down, w + right
                        out_y = -1 if y < 0 else (1 if y > last_h else 0)
                        out_x = -1 if x < 0 else (1 if x > last_w else 0)
                        if out_y == 0 and out_x == 0:
                            source = token(f, y, x)
                        else:
                            slot = SIDES.index((out_y, out_x))
                            if slot < 4:
                                k = x if out_y else y
                                source = tokens + slot * 2 * edge + upper * edge + f * tile_h + k
                            else:
                                source = tokens + 8 * edge + (slot - 4) * 16 + part * frames + f
                        shift[part, at * tokens + token(f, h, w), source] = 1
    return pick, shift


def layer_kernel(
    sizes,
    len_ref,
    tile_ref,
    pick_ref,
    shift_hbm,
    peg_ref,
    prompt_hbm,
    act_ref,
    mod_hbm,
    weight_hbm,
    out_ref,
    shift_ref,
    prompt_ref,
    mod_ref,
    side_send,
    side_in,
    corner_send,
    corner_in,
    conv,
    local_sems,
    halo_send,
    halo_recv,
    mod_buf,
    affine,
    weights,
    text_in,
    send_x,
    grid_x,
    send_text,
    recv_text,
    tile_buf,
    own_text,
    send_part,
    recv_part,
    own_part,
    q_buf,
    k_buf,
    v_buf,
    send_out,
    recv_out,
    w_sems,
    mod_send,
    mod_recv,
    x_send,
    x_recv,
    z_send,
    z_recv,
    t_send,
    t_recv,
    p_send,
    p_recv,
    o_send,
    o_recv,
):
    rows, cols, text, padded_text, tile_w = sizes
    tokens, width = tile_buf.shape
    depth = weight_hbm.shape[1]
    out_w = weight_hbm.shape[2] // rows
    block = tokens * cols
    item = lax.axis_index("item")
    row = lax.axis_index("row")
    col = lax.axis_index("col")

    def row_peer(step):
        return lax.rem(row + step, rows)

    def col_peer(step):
        return lax.rem(col + step, cols)

    def remote(src, dst, send, recv, where):
        return pltpu.make_async_remote_copy(
            src_ref=src, dst_ref=dst, send_sem=send, recv_sem=recv, device_id=where, device_id_type=MESH
        )

    prompt_copy = pltpu.make_async_copy(prompt_hbm, prompt_ref, local_sems.at[0])
    mod_copy = pltpu.make_async_copy(mod_hbm, mod_ref, local_sems.at[1])
    shift_copy = pltpu.make_async_copy(shift_hbm, shift_ref, local_sems.at[2])
    stage_copies = []
    for kind in range(3):
        for dest in range(rows):
            stage_copies.append(
                pltpu.make_async_copy(
                    weight_hbm.at[kind, :, dest * out_w : (dest + 1) * out_w],
                    weights.at[dest, 0:depth, kind * out_w : (kind + 1) * out_w],
                    local_sems.at[3 + kind * rows + dest],
                )
            )
    mod_copy.start()
    for copy in stage_copies:
        copy.start()
    prompt_copy.start()
    shift_copy.start()
    side_in[...] = jnp.zeros_like(side_in)
    corner_in[...] = jnp.zeros_like(corner_in)

    def within(down, right):
        r, c = row + down, col + right
        return (r >= 0) & (r < rows) & (c >= 0) & (c < cols)

    barrier = pltpu.get_barrier_semaphore()
    for down, right in SIDES[4:]:

        @pl.when(within(down, right))
        def greet(down=down, right=right):
            pl.semaphore_signal(
                barrier, inc=1, device_id={"row": row + down, "col": col + right}, device_id_type=MESH
            )

    pl.semaphore_signal(barrier, inc=1, device_id={"item": 1 - item}, device_id_type=MESH)
    for step in range(1, rows):
        pl.semaphore_signal(barrier, inc=1, device_id={"row": row_peer(step)}, device_id_type=MESH)
    for step in range(1, cols):
        pl.semaphore_signal(barrier, inc=1, device_id={"col": col_peer(step)}, device_id_type=MESH)

    pieces = [
        tile_ref[0, f, h].astype(jnp.float32)
        for f in range(tile_ref.shape[1])
        for h in range(tile_ref.shape[2])
    ]
    tile_buf[...] = jnp.concatenate(pieces, axis=0).astype(jnp.bfloat16)
    tile = tile_buf[...]
    wide = side_in.shape[2]
    narrow = corner_in.shape[1]
    edge = side_in.shape[1] // 2
    picked = jnp.dot(pick_ref[0, 0 : 4 * edge], tile, preferred_element_type=jnp.float32)
    for side in range(4):
        lines = picked[side * edge : (side + 1) * edge]
        side_send[side] = jnp.concatenate([lines[:, :wide], lines[:, wide:]], axis=0).astype(jnp.bfloat16)
    corners = jnp.zeros((corner_in.shape[0], narrow), jnp.float32)
    for part in range(width // narrow):
        corners = corners + jnp.dot(
            pick_ref[1 + part],
            tile[:, part * narrow : (part + 1) * narrow],
            preferred_element_type=jnp.float32,
        )
    corner_send[...] = corners.astype(jnp.bfloat16)

    def halo_copy(at, down, right):
        if at < 4:
            src, dst = side_send.at[at], side_in.at[at]
        else:
            lines = pl.ds((at - 4) * 16, 16)
            src, dst = corner_send.at[lines, :], corner_in.at[lines, :]
        return remote(
            src, dst, halo_send.at[at], halo_recv.at[at], {"row": row - down, "col": col - right}
        )

    mod_copy.wait()
    own_columns = jnp.dot(act_ref[...], mod_ref[...], preferred_element_type=jnp.float32)
    mod_buf[col] = own_columns[0:1, :]
    beside_rows = (row + rows - 1) // rows + (2 * rows - 2 - row) // rows
    beside_cols = (col + cols - 1) // cols + (2 * cols - 2 - col) // cols
    pl.semaphore_wait(barrier, rows + cols - 1 + beside_rows * beside_cols)
    for at, (down, right) in enumerate(SIDES):

        @pl.when(within(-down, -right))
        def send(at=at, down=down, right=right):
            halo_copy(at, down, right).start()

    mod_copies = []
    for step in range(1, cols):
        copy = remote(
            mod_buf.at[col],
            mod_buf.at[col],
            mod_send.at[step - 1],
            mod_recv.at[step - 1],
            {"col": col_peer(step)},
        )
        copy.start()
        mod_copies.append(copy)
    for copy in stage_copies:
        copy.wait()
    weight_copy = remote(
        weights.at[:, 0:depth, :],
        weights.at[:, pl.ds(depth, depth), :],
        w_sems.at[0],
        w_sems.at[1],
        {"item": 1 - item},
    )
    weight_copy.start()
    for at, (down, right) in enumerate(SIDES):

        @pl.when(within(down, right))
        def receive(at=at, down=down, right=right):
            halo_copy(at, down, right).wait_recv()

    shift_copy.wait()
    for part in range(width // narrow):
        lanes = slice(part * narrow, (part + 1) * narrow)
        upper, start = divmod(part * narrow, wide)
        pieces = [tile[:, lanes]]
        for side in range(4):
            pieces.append(side_in[side, :, start : start + narrow])
        pieces.append(corner_in[...])
        moved = jnp.dot(
            shift_ref[part], jnp.concatenate(pieces, axis=0), preferred_element_type=jnp.float32
        )
        own = tile[:, lanes].astype(jnp.float32)
        taps = [peg_ref[a, :, lanes].astype(jnp.float32) for a in range(3)]
        summed = own + own * taps[1][1:2]
        for at, (down, right) in enumerate(SIDES):
            summed = summed + moved[at * tokens : (at + 1) * tokens] * taps[down + 1][right + 1 : right + 2]
        conv[:, lanes] = summed.astype(jnp.bfloat16)
    tile_normal = centered_rows(conv[...].astype(jnp.float32))
    for step in range(1, cols):
        remote(
            mod_buf.at[col],
            mod_buf.at[lax.rem(col - step + cols, cols)],
            mod_send.at[step - 1],
            mod_recv.at[step - 1],
            {"col": col_peer(step)},
        ).wait_recv()
    half = cols // 2
    piece = mod_buf.shape[2]
    for part in range(half):
        affine[0, :, part * piece : (part + 1) * piece] = mod_buf[part]
        affine[1, :, part * piece : (part + 1) * piece] = 1.0 + mod_buf[half + part]

    def depth_slices(dest):
        first = (item * rows + dest) * depth
        second = ((1 - item) * rows + dest) * depth
        return (pl.multiple_of(first, depth), pl.multiple_of(second, depth))

    text_in[0:tokens, :] = (tile_normal * affine[1] + affine[0]).astype(jnp.bfloat16)
    x_copies = []
    for step in range(1, rows):
        peer = row_peer(step)
        for order, start in enumerate(depth_slices(peer)):
            send_x[step - 1, :, order * depth : (order + 1) * depth] = text_in[
                0:tokens, pl.ds(start, depth)
            ]
        copy = remote(
            send_x.at[step - 1],
            grid_x.at[col, pl.ds(pl.multiple_of(row * tokens, tokens), tokens), :],
            x_send.at[step - 1],
            x_recv.at[step - 1],
            {"row": peer},
        )
        copy.start()
        x_copies.append(copy)
    own_slices = depth_slices(row)
    for order, start in enumerate(own_slices):
        grid_x[
            col, pl.ds(pl.multiple_of(row * tokens, tokens), tokens), order * depth : (order + 1) * depth
        ] = text_in[0:tokens, pl.ds(start, depth)]

    for step in range(1, rows):
        source = lax.rem(row - step + rows, rows)
        remote(
            send_x.at[step - 1],
            grid_x.at[col, pl.ds(pl.multiple_of(source * tokens, tokens), tokens), :],
            x_send.at[step - 1],
            x_recv.at[step - 1],
            {"row": row_peer(step)},
        ).wait_recv()
    def z_copy(direction, distance, source):
        sign = 1 - 2 * direction
        return remote(
            grid_x.at[source],
            grid_x.at[source],
            z_send.at[direction, distance - 1],
            z_recv.at[direction, distance - 1],
            {"col": col + sign},
        )

    def passes(direction, distance):
        home = col - (distance - 1) * (1 - 2 * direction)
        return (home >= 0) & (home < cols) & (col < cols - 1 if direction == 0 else col > 0)

    def arrives(direction, distance):
        home = col - distance * (1 - 2 * direction)
        return (home >= 0) & (home < cols)

    def pass_on(distance):
        for direction in range(2):

            @pl.when(passes(direction, distance))
            def start(direction=direction):
                z_copy(direction, distance, col - (distance - 1) * (1 - 2 * direction)).start()

    pass_on(1)

    def part_copy(group, step):
        return remote(
            send_part.at[group, step - 1],
            recv_part.at[group, step - 1],
            p_send.at[group, step - 1],
            p_recv.at[group, step - 1],
            {"row": row_peer(step)},
        )

    def latent_part(group):
        values = grid_x[group]
        for step in range(1, rows):
            send_part[group, step - 1] = jnp.dot(
                values, weights[row_peer(step)], preferred_element_type=jnp.float32
            ).astype(jnp.bfloat16)
            part_copy(group, step).start()
        own_part[group] = jnp.dot(values, weights[row], preferred_element_type=jnp.float32)

    t_copies = []

    def text_part():
        prompt_copy.wait()
        scale_pieces = [affine[1, :, pl.ds(start, depth)] for start in own_slices]
        shift_pieces = [affine[0, :, pl.ds(start, depth)] for start in own_slices]
        edges = list(range(0, text - text % 16, 64)) + [text - text % 16, text]
        for first, last in zip(edges[:-1], edges[1:]):
            if first == last:
                continue
            values = prompt_ref[first:last, :].astype(jnp.float32)
            center = jnp.mean(values, axis=-1, keepdims=True)
            centered = values - center
            spread = lax.rsqrt(jnp.mean(centered * centered, axis=-1, keepdims=True) + 1e-06)
            for order, start in enumerate(own_slices):
                part = prompt_ref[first:last, pl.ds(start, depth)].astype(jnp.float32)
                normed = (part - center) * spread * scale_pieces[order] + shift_pieces[order]
                fill = -(last - first) % 16
                if fill > 0:
                    normed = jnp.concatenate([normed, jnp.zeros((fill, depth), jnp.float32)], axis=0)
                text_in[first : last + fill, order * depth : (order + 1) * depth] = normed.astype(jnp.bfloat16)
        filled = -(-text // 16) * 16
        if filled < padded_text:
            text_in[filled:padded_text, 0 : 2 * depth] = jnp.zeros(
                (padded_text - filled, 2 * depth), jnp.bfloat16
            )
        text_values = text_in[0:padded_text, 0 : 2 * depth]
        for step in range(1, rows):
            peer = row_peer(step)
            send_text[step - 1] = jnp.dot(
                text_values, weights[peer, :, out_w:], preferred_element_type=jnp.float32
            ).astype(jnp.bfloat16)
            copy = remote(
                send_text.at[step - 1],
                recv_text.at[step - 1],
                t_send.at[step - 1],
                t_recv.at[step - 1],
                {"row": peer},
            )
            copy.start()
            t_copies.append(copy)
        own_text[...] = jnp.dot(text_values, weights[row, :, out_w:], preferred_element_type=jnp.float32)

    weight_copy.wait_recv()
    latent_part(col)
    for distance in range(1, cols):
        for direction in range(2):

            @pl.when(arrives(direction, distance))
            def landed(direction=direction, distance=distance):
                z_copy(direction, distance, col - distance * (1 - 2 * direction)).wait_recv()

        if distance < cols - 1:
            pass_on(distance + 1)
        for direction in range(2):

            @pl.when(arrives(direction, distance))
            def multiply(direction=direction, distance=distance):
                latent_part(col - distance * (1 - 2 * direction))

        if distance == 1:
            text_part()

    for copy in t_copies:
        copy.wait_recv()
    total = own_text[...]
    for step in range(1, rows):
        total = total + recv_text[step - 1].astype(jnp.float32)
    k_buf[0:padded_text, :] = total[:, 0:out_w].astype(jnp.bfloat16)
    v_buf[0:padded_text, :] = total[:, out_w:].astype(jnp.bfloat16)
    for group in range(cols):
        for step in range(1, rows):
            part_copy(group, step).wait_recv()
        total = own_part[group]
        for step in range(1, rows):
            total = total + recv_part[group, step - 1].astype(jnp.float32)
        rounded = total.astype(jnp.bfloat16)
        per_col = rows * tokens
        base = padded_text + group * per_col
        k_buf[base : base + per_col, :] = rounded[:, out_w : 2 * out_w]
        v_buf[base : base + per_col, :] = rounded[:, 2 * out_w :]
        for dest in range(rows):
            q_buf[dest, group * tokens : (group + 1) * tokens, :] = rounded[
                dest * tokens : (dest + 1) * tokens, 0:out_w
            ]

    at = lax.broadcasted_iota(jnp.int32, (block, block), 0)
    source = lax.broadcasted_iota(jnp.int32, (block, block), 1)
    group = source // tokens
    token = source - group * tokens
    line = token // tile_w
    place = token - line * tile_w
    target = (line * cols + group) * tile_w + place
    permute = jnp.where(at == target, 0.125, 0.0).astype(jnp.bfloat16)
    keys = k_buf[...]
    vals = v_buf[...]
    position = lax.broadcasted_iota(jnp.int32, (1, keys.shape[0]), 1)
    valid = (position >= padded_text) | (position < len_ref[0])
    head_of = lax.broadcasted_iota(jnp.int32, (1, out_w), 1) // HD
    heads = out_w // HD
    o_copies = []
    for step in list(range(1, rows)) + [0]:
        peer = row_peer(step)
        queries = jnp.dot(permute, q_buf[peer], preferred_element_type=jnp.float32)
        by_head = [jnp.where(head_of == head, queries, 0.0) for head in range(heads)]
        stacked = jnp.concatenate(by_head, axis=0).astype(jnp.bfloat16)
        scores = lax.dot_general(
            stacked, keys, (((1,), (1,)), ((), ())), preferred_element_type=jnp.float32
        )
        scores = jnp.where(valid, scores, -jnp.inf)
        weight = jnp.exp(scores - jnp.max(scores, axis=-1, keepdims=True))
        total = jnp.sum(weight, axis=-1, keepdims=True)
        mixed = jnp.dot(weight.astype(jnp.bfloat16), vals, preferred_element_type=jnp.float32) / total
        result = mixed[0:block]
        for head in range(1, heads):
            result = jnp.where(head_of == head, mixed[head * block : (head + 1) * block], result)
        result = result.astype(jnp.bfloat16)
        if step == 0:
            recv_out[row] = result
        else:
            send_out[step - 1] = result
            copy = remote(
                send_out.at[step - 1],
                recv_out.at[row],
                o_send.at[step - 1],
                o_recv.at[step - 1],
                {"row": peer},
            )
            copy.start()
            o_copies.append(copy)
    for step in range(1, rows):
        source = lax.rem(row - step + rows, rows)
        remote(
            send_out.at[step - 1],
            recv_out.at[source],
            o_send.at[step - 1],
            o_recv.at[step - 1],
            {"row": row_peer(step)},
        ).wait_recv()
    for source in range(rows):
        out_ref[:, source * out_w : (source + 1) * out_w] = recv_out[source]
    for at, (down, right) in enumerate(SIDES):

        @pl.when(within(-down, -right))
        def sent(at=at, down=down, right=right):
            halo_copy(at, down, right).wait_send()

    for direction in range(2):
        for distance in range(1, cols):

            @pl.when(passes(direction, distance))
            def passed(direction=direction, distance=distance):
                z_copy(direction, distance, col - (distance - 1) * (1 - 2 * direction)).wait_send()

    for group in range(cols):
        for step in range(1, rows):
            part_copy(group, step).wait_send()
    for copy in mod_copies + [weight_copy] + x_copies + t_copies + o_copies:
        copy.wait_send()


def on_device_fast(
    rows, cols, latents, prompt_rows, peg_weight, modulation_weight, qkv_weight, text_len, timestep
):
    frames, tile_h, tile_w, width = latents.shape[1:]
    tokens = frames * tile_h * tile_w
    parts = 8
    narrow = width // parts
    pick, shift = (jnp.asarray(table, jnp.bfloat16) for table in halo_tables(frames, tile_h, tile_w, parts))
    temb = modulation_weight.shape[0]
    activation = jax.nn.silu(time_angles(timestep[0], temb)).astype(jnp.bfloat16)
    activation = jnp.broadcast_to(activation[None, :], (16, temb))
    depth, kinds, head_width = qkv_weight.shape
    out_w = head_width // rows
    by_kind = qkv_weight.transpose(1, 0, 2)
    text = prompt_rows.shape[1]
    padded_text = -(-text // 128) * 128
    block = tokens * cols
    group_rows = tokens * rows
    bf16, f32 = jnp.bfloat16, jnp.float32
    dma = pltpu.SemaphoreType.DMA
    all_rows = padded_text + group_rows * cols
    attended = pl.pallas_call(
        functools.partial(layer_kernel, (rows, cols, text, padded_text, tile_w)),
        out_shape=jax.ShapeDtypeStruct((block, head_width), bf16),
        in_specs=[pl.BlockSpec(memory_space=pltpu.SMEM)] + [pl.BlockSpec(memory_space=space) for space in (VMEM, VMEM, pltpu.HBM, VMEM, pltpu.HBM, VMEM, pltpu.HBM, pltpu.HBM)],
        out_specs=pl.BlockSpec(memory_space=VMEM),
        scratch_shapes=[
            VMEM(shift.shape, bf16),
            VMEM((text, width), bf16),
            VMEM(modulation_weight.shape, bf16),
            VMEM((4, 16, width // 2), bf16),
            VMEM((4, 16, width // 2), bf16),
            VMEM((64, narrow), bf16),
            VMEM((64, narrow), bf16),
            VMEM((tokens, width), bf16),
            dma((3 + 3 * rows,)),
            dma((8,)),
            dma((8,)),
            VMEM((cols, 1, modulation_weight.shape[1]), f32),
            VMEM((2, 1, width), f32),
            VMEM((rows, 2 * depth, kinds * out_w), bf16),
            VMEM((max(padded_text, tokens), width), bf16),
            VMEM((rows - 1, tokens, 2 * depth), bf16),
            VMEM((cols, group_rows, 2 * depth), bf16),
            VMEM((rows - 1, padded_text, 2 * out_w), bf16),
            VMEM((rows - 1, padded_text, 2 * out_w), bf16),
            VMEM((tokens, width), bf16),
            VMEM((padded_text, 2 * out_w), f32),
            VMEM((cols, rows - 1, group_rows, kinds * out_w), bf16),
            VMEM((cols, rows - 1, group_rows, kinds * out_w), bf16),
            VMEM((cols, group_rows, kinds * out_w), f32),
            VMEM((rows, block, out_w), bf16),
            VMEM((all_rows, out_w), bf16),
            VMEM((all_rows, out_w), bf16),
            VMEM((rows - 1, block, out_w), bf16),
            VMEM((rows, block, out_w), bf16),
            dma((2,)),
            dma((cols - 1,)),
            dma((cols - 1,)),
            dma((rows - 1,)),
            dma((rows - 1,)),
            dma((2, cols - 1)),
            dma((2, cols - 1)),
            dma((rows - 1,)),
            dma((rows - 1,)),
            dma((cols, rows - 1)),
            dma((cols, rows - 1)),
            dma((rows - 1,)),
            dma((rows - 1,)),
        ],
        compiler_params=pltpu.CompilerParams(
            collective_id=0, has_side_effects=True, vmem_limit_bytes=52 * 1024 * 1024
        ),
    )(text_len, latents, pick, shift, peg_weight, prompt_rows[0], activation, modulation_weight, by_kind)
    return attended.reshape(1, frames, tile_h, tile_w * cols, head_width)


def solution(mesh):
    in_specs = (
        P("item", None, "row", "col", None),
        P("item", None, None),
        P(),
        P(None, "col"),
        P(("item", "row"), None, "col"),
        P("item"),
        P("item"),
    )
    out_specs = P("item", None, "row", None, "col")
    rows, cols, items = mesh.shape["row"], mesh.shape["col"], mesh.shape["item"]

    def on_device(*blocks):
        group = blocks[4].shape[2] // rows
        if items == 2 and cols % 2 == 0 and group >= 128 and group % 128 == 0 and blocks[0].shape[1:4] == (2, 4, 4):
            return on_device_fast(rows, cols, *blocks)
        return on_device_general(*blocks)

    return jax.shard_map(
        on_device, mesh=mesh, in_specs=in_specs, out_specs=out_specs, check_vma=False
    )
```

```python
import functools
import math

import jax
import jax.numpy as jnp
import numpy as np
from jax import lax
from jax.experimental import pallas as pl
from jax.experimental.pallas import tpu as pltpu
from jax.sharding import PartitionSpec as P

HD = 64
MESH = pl.DeviceIdType.MESH
VMEM = pltpu.VMEM


def with_halo(block, sides, width):
    for axis, dim in sides:
        count = lax.axis_size(axis)
        forward = [(i, i + 1) for i in range(count - 1)]
        backward = [(target, source) for source, target in forward]
        low = lax.ppermute(
            lax.slice_in_dim(block, block.shape[dim] - width, None, axis=dim), axis, forward
        )
        high = lax.ppermute(lax.slice_in_dim(block, 0, width, axis=dim), axis, backward)
        block = jnp.concatenate([low, block, high], axis=dim)
    return block


def time_angles(step, count):
    half = count // 2
    freqs = jnp.exp(-math.log(10000.0) * jnp.arange(half, dtype=jnp.float32) / half)
    angle = step.astype(jnp.float32) * freqs
    return jnp.concatenate([jnp.cos(angle), jnp.sin(angle)])


def modulate(rows, shift, scale):
    values = rows.astype(jnp.float32)
    center = jnp.mean(values, axis=-1, keepdims=True)
    centered = values - center
    spread = jnp.mean(centered * centered, axis=-1, keepdims=True)
    return (centered * lax.rsqrt(spread + 1e-06) * (1.0 + scale) + shift).astype(jnp.bfloat16)


def absorb(carry, queries, key_rows, value_rows, valid):
    running_max, running_sum, weighted = carry
    count = key_rows.shape[0]
    heads = queries.shape[1]
    key_heads = key_rows.reshape(count, heads, HD)
    value_heads = value_rows.reshape(count, heads, HD)
    scores = (
        jnp.einsum("rhd,bhd->rhb", queries, key_heads, preferred_element_type=jnp.float32) * 0.125
    )
    if valid is not None:
        scores = jnp.where(valid[None, None, :], scores, -jnp.inf)
    newest = jnp.maximum(running_max, jnp.max(scores, axis=-1))
    weights = jnp.exp(scores - newest[..., None])
    shrink_by = jnp.exp(running_max - newest)
    running_sum = running_sum * shrink_by + jnp.sum(weights, axis=-1)
    weighted = weighted * shrink_by[..., None] + jnp.einsum(
        "rhb,bhd->rhd",
        weights.astype(jnp.bfloat16),
        value_heads,
        preferred_element_type=jnp.float32,
    )
    return (newest, running_sum, weighted)


def on_device_general(latents, prompt_rows, peg_weight, modulation_weight, qkv_weight, text_len, timestep):
    tile_h = latents.shape[2]
    tile_w = latents.shape[3]
    width = latents.shape[4]
    padded = with_halo(latents, (("row", 2), ("col", 3)), 1)
    summed = latents.astype(jnp.float32)
    for row_tap in range(3):
        for col_tap in range(3):
            summed = summed + padded[
                :, :, row_tap : row_tap + tile_h, col_tap : col_tap + tile_w, :
            ].astype(jnp.float32) * peg_weight[row_tap, col_tap].astype(jnp.float32)
    convolved = summed.astype(jnp.bfloat16)
    activation = jax.nn.silu(time_angles(timestep[0], modulation_weight.shape[0])).astype(
        jnp.bfloat16
    )
    own_columns = jnp.dot(
        activation[None, :], modulation_weight, preferred_element_type=jnp.float32
    )
    modulation = lax.all_gather(own_columns, "col", axis=1, tiled=True)[0]
    shift = modulation[:width]
    scale = modulation[width:]
    group_rows = lax.all_gather(modulate(convolved, shift, scale), "col", axis=3, tiled=True)
    frames = group_rows.shape[1]
    grid_w = group_rows.shape[3]
    flat_rows = group_rows.reshape(-1, width)
    row_count = flat_rows.shape[0]
    text_normed = modulate(prompt_rows[0], shift, scale)
    text_count = text_normed.shape[0]
    head_width = qkv_weight.shape[2]
    full_weight = lax.all_gather(qkv_weight, ("item", "row"), axis=0, tiled=True)
    latent_proj = jnp.einsum(
        "rd,dkc->rkc", flat_rows, full_weight, preferred_element_type=jnp.float32
    )
    text_proj = jnp.einsum(
        "rd,dkc->rkc", text_normed, full_weight, preferred_element_type=jnp.float32
    )
    latent_qkv = latent_proj.astype(jnp.bfloat16)
    text_qkv = text_proj.astype(jnp.bfloat16)
    heads = head_width // HD
    queries = latent_qkv[:, 0, :].reshape(row_count, heads, HD)
    local_keys = latent_qkv[:, 1, :]
    local_values = latent_qkv[:, 2, :]
    text_valid = jnp.arange(text_count, dtype=jnp.int32) < text_len[0]
    start_carry = (
        jnp.full((row_count, heads), -jnp.inf, jnp.float32),
        jnp.zeros((row_count, heads), jnp.float32),
        jnp.zeros((row_count, heads, HD), jnp.float32),
    )
    text_carry = absorb(start_carry, queries, text_qkv[:, 1, :], text_qkv[:, 2, :], text_valid)
    key_rows = lax.all_gather(local_keys, "row", axis=0, tiled=True)
    value_rows = lax.all_gather(local_values, "row", axis=0, tiled=True)
    total_rows = key_rows.shape[0]
    block_count = total_rows // row_count

    def one_block(state, pair):
        return (absorb(state, queries, pair[0], pair[1], None), None)

    state, unused = lax.scan(
        one_block,
        text_carry,
        (
            key_rows.reshape(block_count, row_count, head_width),
            value_rows.reshape(block_count, row_count, head_width),
        ),
    )
    running_max, running_sum, weighted = state
    attended = (weighted / running_sum[..., None]).astype(jnp.bfloat16)
    return attended.reshape(1, frames, tile_h, grid_w, head_width)


def centered_rows(values):
    center = jnp.mean(values, axis=-1, keepdims=True)
    centered = values - center
    spread = jnp.mean(centered * centered, axis=-1, keepdims=True)
    return centered * lax.rsqrt(spread + 1e-06)


SIDES = ((-1, 0), (1, 0), (0, -1), (0, 1), (-1, -1), (-1, 1), (1, -1), (1, 1))


def halo_tables(frames, tile_h, tile_w, parts):
    tokens = frames * tile_h * tile_w
    edge = frames * tile_h

    def token(f, h, w):
        return (f * tile_h + h) * tile_w + w

    pick = np.zeros((1 + parts, 64, tokens), np.float32)
    shift = np.zeros((parts, 8 * tokens, tokens + 8 * edge + 64), np.float32)
    last_h, last_w = tile_h - 1, tile_w - 1
    for at, (down, right) in enumerate(SIDES):
        h_from = last_h if down < 0 else 0
        w_from = last_w if right < 0 else 0
        for f in range(frames):
            if at < 4:
                for k in range(tile_h):
                    source = token(f, h_from, k) if down else token(f, k, w_from)
                    pick[0, at * edge + f * tile_h + k, source] = 1
            else:
                for part in range(parts):
                    pick[1 + part, (at - 4) * 16 + part * frames + f, token(f, h_from, w_from)] = 1
        for part in range(parts):
            upper = part // (parts // 2)
            for f in range(frames):
                for h in range(tile_h):
                    for w in range(tile_w):
                        y, x = h + down, w + right
                        out_y = -1 if y < 0 else (1 if y > last_h else 0)
                        out_x = -1 if x < 0 else (1 if x > last_w else 0)
                        if out_y == 0 and out_x == 0:
                            source = token(f, y, x)
                        else:
                            slot = SIDES.index((out_y, out_x))
                            if slot < 4:
                                k = x if out_y else y
                                source = tokens + slot * 2 * edge + upper * edge + f * tile_h + k
                            else:
                                source = tokens + 8 * edge + (slot - 4) * 16 + part * frames + f
                        shift[part, at * tokens + token(f, h, w), source] = 1
    return pick, shift


def layer_kernel(
    sizes,
    len_ref,
    tile_ref,
    pick_ref,
    shift_hbm,
    peg_ref,
    prompt_hbm,
    act_ref,
    mod_hbm,
    weight_hbm,
    out_ref,
    shift_ref,
    prompt_ref,
    mod_ref,
    side_send,
    side_in,
    corner_send,
    corner_in,
    conv,
    local_sems,
    halo_send,
    halo_recv,
    mod_buf,
    affine,
    weights,
    text_in,
    send_x,
    grid_x,
    tile_buf,
    own_text,
    text_first,
    text_first_in,
    text_hold,
    text_second,
    text_second_in,
    own_part,
    part_first,
    part_first_in,
    part_hold,
    part_second,
    part_second_in,
    q_buf,
    k_buf,
    v_buf,
    send_out,
    recv_out,
    w_sems,
    mod_send,
    mod_recv,
    x_send,
    x_recv,
    z_send,
    z_recv,
    t_sems,
    p_sems,
    o_send,
    o_recv,
):
    rows, cols, text, padded_text, tile_w = sizes
    tokens, width = tile_buf.shape
    depth = weight_hbm.shape[1]
    out_w = weight_hbm.shape[2] // rows
    block = tokens * cols
    item = lax.axis_index("item")
    row = lax.axis_index("row")
    col = lax.axis_index("col")

    def row_peer(step):
        return lax.rem(row + step, rows)

    def col_peer(step):
        return lax.rem(col + step, cols)

    def remote(src, dst, send, recv, where):
        return pltpu.make_async_remote_copy(
            src_ref=src, dst_ref=dst, send_sem=send, recv_sem=recv, device_id=where, device_id_type=MESH
        )

    prompt_copy = pltpu.make_async_copy(prompt_hbm, prompt_ref, local_sems.at[0])
    mod_copy = pltpu.make_async_copy(mod_hbm, mod_ref, local_sems.at[1])
    shift_copy = pltpu.make_async_copy(shift_hbm, shift_ref, local_sems.at[2])
    stage_copies = []
    for kind in range(3):
        for dest in range(rows):
            stage_copies.append(
                pltpu.make_async_copy(
                    weight_hbm.at[kind, :, dest * out_w : (dest + 1) * out_w],
                    weights.at[dest, 0:depth, kind * out_w : (kind + 1) * out_w],
                    local_sems.at[3 + kind * rows + dest],
                )
            )
    mod_copy.start()
    for copy in stage_copies:
        copy.start()
    prompt_copy.start()
    shift_copy.start()
    side_in[...] = jnp.zeros_like(side_in)
    corner_in[...] = jnp.zeros_like(corner_in)

    def within(down, right):
        r, c = row + down, col + right
        return (r >= 0) & (r < rows) & (c >= 0) & (c < cols)

    near = (row + 1 - 2 * lax.rem(row, 2), row + 2 - 4 * lax.div(row, 2))
    across = 3 - row

    def first_copy(group, way, sems, first, first_in):
        return remote(
            first.at[group, way],
            first_in.at[group, way],
            sems.at[0, group, way],
            sems.at[1, group, way],
            {"row": near[way]},
        )

    def second_copy(group, way, sems, second, second_in):
        return remote(
            second.at[group, way],
            second_in.at[group, way],
            sems.at[2, group, way],
            sems.at[3, group, way],
            {"row": near[1 - way]},
        )

    def scatter_start(group, values, lane, own, first, first_in, hold, second, second_in, sems):
        def product(dest):
            return jnp.dot(values, weights[dest, :, lane:], preferred_element_type=jnp.float32)

        half = values.shape[0] // 2
        far = product(across)
        for way in range(2):
            first[group, way, 1] = far[way * half : (way + 1) * half].astype(jnp.bfloat16)
        for way in range(2):
            part = product(near[way])
            first[group, way, 0] = part[way * half : (way + 1) * half].astype(jnp.bfloat16)
            hold[group, 1 - way] = part[(1 - way) * half : (2 - way) * half]
            first_copy(group, way, sems, first, first_in).start()
        own[group] = product(row)

    def scatter_pass(group, own, first, first_in, hold, second, second_in, sems):
        half = hold.shape[2]
        for way in range(2):
            first_copy(group, way, sems, first, first_in).wait_recv()
            second[group, way] = (
                hold[group, way] + first_in[group, way, 1].astype(jnp.float32)
            ).astype(jnp.bfloat16)
            second_copy(group, way, sems, second, second_in).start()
            lines = slice(way * half, (way + 1) * half)
            own[group, lines] = own[group, lines] + first_in[group, way, 0].astype(jnp.float32)

    def scatter_end(group, own, first, first_in, hold, second, second_in, sems):
        sums = []
        half = hold.shape[2]
        for way in range(2):
            second_copy(group, way, sems, second, second_in).wait_recv()
            sums.append(
                own[group, way * half : (way + 1) * half] + second_in[group, way].astype(jnp.float32)
            )
        return jnp.concatenate(sums, axis=0).astype(jnp.bfloat16)

    text_state = (own_text, text_first, text_first_in, text_hold, text_second, text_second_in, t_sems)
    part_state = (own_part, part_first, part_first_in, part_hold, part_second, part_second_in, p_sems)

    barrier = pltpu.get_barrier_semaphore()
    for down, right in SIDES[4:]:

        @pl.when(within(down, right))
        def greet(down=down, right=right):
            pl.semaphore_signal(
                barrier, inc=1, device_id={"row": row + down, "col": col + right}, device_id_type=MESH
            )

    pl.semaphore_signal(barrier, inc=1, device_id={"item": 1 - item}, device_id_type=MESH)
    for step in range(1, rows):
        pl.semaphore_signal(barrier, inc=1, device_id={"row": row_peer(step)}, device_id_type=MESH)
    for step in range(1, cols):
        pl.semaphore_signal(barrier, inc=1, device_id={"col": col_peer(step)}, device_id_type=MESH)

    pieces = [
        tile_ref[0, f, h].astype(jnp.float32)
        for f in range(tile_ref.shape[1])
        for h in range(tile_ref.shape[2])
    ]
    tile_buf[...] = jnp.concatenate(pieces, axis=0).astype(jnp.bfloat16)
    tile = tile_buf[...]
    wide = side_in.shape[2]
    narrow = corner_in.shape[1]
    edge = side_in.shape[1] // 2
    picked = jnp.dot(pick_ref[0, 0 : 4 * edge], tile, preferred_element_type=jnp.float32)
    for side in range(4):
        lines = picked[side * edge : (side + 1) * edge]
        side_send[side] = jnp.concatenate([lines[:, :wide], lines[:, wide:]], axis=0).astype(jnp.bfloat16)
    corners = jnp.zeros((corner_in.shape[0], narrow), jnp.float32)
    for part in range(width // narrow):
        corners = corners + jnp.dot(
            pick_ref[1 + part],
            tile[:, part * narrow : (part + 1) * narrow],
            preferred_element_type=jnp.float32,
        )
    corner_send[...] = corners.astype(jnp.bfloat16)

    def halo_copy(at, down, right):
        if at < 4:
            src, dst = side_send.at[at], side_in.at[at]
        else:
            lines = pl.ds((at - 4) * 16, 16)
            src, dst = corner_send.at[lines, :], corner_in.at[lines, :]
        return remote(
            src, dst, halo_send.at[at], halo_recv.at[at], {"row": row - down, "col": col - right}
        )

    mod_copy.wait()
    own_columns = jnp.dot(act_ref[...], mod_ref[...], preferred_element_type=jnp.float32)
    mod_buf[col] = own_columns[0:1, :]
    beside_rows = (row + rows - 1) // rows + (2 * rows - 2 - row) // rows
    beside_cols = (col + cols - 1) // cols + (2 * cols - 2 - col) // cols
    pl.semaphore_wait(barrier, rows + cols - 1 + beside_rows * beside_cols)
    for at, (down, right) in enumerate(SIDES):

        @pl.when(within(-down, -right))
        def send(at=at, down=down, right=right):
            halo_copy(at, down, right).start()

    mod_copies = []
    for step in range(1, cols):
        copy = remote(
            mod_buf.at[col],
            mod_buf.at[col],
            mod_send.at[step - 1],
            mod_recv.at[step - 1],
            {"col": col_peer(step)},
        )
        copy.start()
        mod_copies.append(copy)
    for copy in stage_copies:
        copy.wait()
    weight_copy = remote(
        weights.at[:, 0:depth, :],
        weights.at[:, pl.ds(depth, depth), :],
        w_sems.at[0],
        w_sems.at[1],
        {"item": 1 - item},
    )
    weight_copy.start()
    prompt_copy.wait()
    text_stats = []
    for start_row in range(0, padded_text, 16):
        count = min(16, text - start_row)
        if count <= 0:
            continue
        values = prompt_ref[start_row : start_row + count, :].astype(jnp.float32)
        center = jnp.mean(values, axis=-1, keepdims=True)
        centered = values - center
        spread = lax.rsqrt(jnp.mean(centered * centered, axis=-1, keepdims=True) + 1e-06)
        text_stats.append((center, spread))

    for at, (down, right) in enumerate(SIDES):

        @pl.when(within(down, right))
        def receive(at=at, down=down, right=right):
            halo_copy(at, down, right).wait_recv()

    shift_copy.wait()
    for part in range(width // narrow):
        lanes = slice(part * narrow, (part + 1) * narrow)
        upper, start = divmod(part * narrow, wide)
        pieces = [tile[:, lanes]]
        for side in range(4):
            pieces.append(side_in[side, :, start : start + narrow])
        pieces.append(corner_in[...])
        moved = jnp.dot(
            shift_ref[part], jnp.concatenate(pieces, axis=0), preferred_element_type=jnp.float32
        )
        own = tile[:, lanes].astype(jnp.float32)
        taps = [peg_ref[a, :, lanes].astype(jnp.float32) for a in range(3)]
        summed = own + own * taps[1][1:2]
        for at, (down, right) in enumerate(SIDES):
            summed = summed + moved[at * tokens : (at + 1) * tokens] * taps[down + 1][right + 1 : right + 2]
        conv[:, lanes] = summed.astype(jnp.bfloat16)
    tile_normal = centered_rows(conv[...].astype(jnp.float32))
    for step in range(1, cols):
        remote(
            mod_buf.at[col],
            mod_buf.at[lax.rem(col - step + cols, cols)],
            mod_send.at[step - 1],
            mod_recv.at[step - 1],
            {"col": col_peer(step)},
        ).wait_recv()
    half = cols // 2
    piece = mod_buf.shape[2]
    for part in range(half):
        affine[0, :, part * piece : (part + 1) * piece] = mod_buf[part]
        affine[1, :, part * piece : (part + 1) * piece] = 1.0 + mod_buf[half + part]

    def depth_slices(dest):
        first = (item * rows + dest) * depth
        second = ((1 - item) * rows + dest) * depth
        return (pl.multiple_of(first, depth), pl.multiple_of(second, depth))

    text_in[0:tokens, :] = (tile_normal * affine[1] + affine[0]).astype(jnp.bfloat16)
    x_copies = []
    for step in range(1, rows):
        peer = row_peer(step)
        for order, start in enumerate(depth_slices(peer)):
            send_x[step - 1, :, order * depth : (order + 1) * depth] = text_in[
                0:tokens, pl.ds(start, depth)
            ]
        copy = remote(
            send_x.at[step - 1],
            grid_x.at[col, pl.ds(pl.multiple_of(row * tokens, tokens), tokens), :],
            x_send.at[step - 1],
            x_recv.at[step - 1],
            {"row": peer},
        )
        copy.start()
        x_copies.append(copy)
    own_slices = depth_slices(row)
    for order, start in enumerate(own_slices):
        grid_x[
            col, pl.ds(pl.multiple_of(row * tokens, tokens), tokens), order * depth : (order + 1) * depth
        ] = text_in[0:tokens, pl.ds(start, depth)]

    weight_copy.wait_recv()

    scale_pieces = [affine[1, :, pl.ds(start, depth)] for start in own_slices]
    shift_pieces = [affine[0, :, pl.ds(start, depth)] for start in own_slices]
    for start_row in range(0, padded_text, 16):
        count = min(16, text - start_row)
        if count <= 0:
            text_in[start_row : start_row + 16, 0 : 2 * depth] = jnp.zeros((16, 2 * depth), jnp.bfloat16)
            continue
        center, spread = text_stats[start_row // 16]
        for order, start in enumerate(own_slices):
            part = prompt_ref[start_row : start_row + count, pl.ds(start, depth)].astype(jnp.float32)
            normed = (part - center) * spread * scale_pieces[order] + shift_pieces[order]
            if count < 16:
                normed = jnp.concatenate([normed, jnp.zeros((16 - count, depth), jnp.float32)], axis=0)
            text_in[start_row : start_row + 16, order * depth : (order + 1) * depth] = normed.astype(
                jnp.bfloat16
            )
    text_values = text_in[:, 0 : 2 * depth]
    scatter_start(0, text_values, out_w, *text_state)

    for step in range(1, rows):
        source = lax.rem(row - step + rows, rows)
        remote(
            send_x.at[step - 1],
            grid_x.at[col, pl.ds(pl.multiple_of(source * tokens, tokens), tokens), :],
            x_send.at[step - 1],
            x_recv.at[step - 1],
            {"row": row_peer(step)},
        ).wait_recv()
    def z_copy(direction, distance, source):
        sign = 1 - 2 * direction
        return remote(
            grid_x.at[source],
            grid_x.at[source],
            z_send.at[direction, distance - 1],
            z_recv.at[direction, distance - 1],
            {"col": col + sign * max(1, distance - 1)},
        )

    def passes(direction, distance):
        sign = 1 - 2 * direction
        home = col - min(distance - 1, 1) * sign
        target = col + max(1, distance - 1) * sign
        return (home >= 0) & (home < cols) & (target >= 0) & (target < cols)

    def arrives(direction, distance):
        home = col - distance * (1 - 2 * direction)
        return (home >= 0) & (home < cols)

    def pass_on(distance):
        for direction in range(2):

            @pl.when(passes(direction, distance))
            def start(direction=direction):
                z_copy(direction, distance, col - min(distance - 1, 1) * (1 - 2 * direction)).start()

    pass_on(1)

    def pass_sums(distance):
        for direction in range(2):

            @pl.when(arrives(direction, distance))
            def forward(direction=direction):
                scatter_pass(col - distance * (1 - 2 * direction), *part_state)

    scatter_start(col, grid_x[col], 0, *part_state)
    for distance in range(1, cols):
        for direction in range(2):

            @pl.when(arrives(direction, distance))
            def landed(direction=direction, distance=distance):
                z_copy(direction, distance, col - distance * (1 - 2 * direction)).wait_recv()

        if distance == 1:
            pass_on(2)
            pass_on(3)
            scatter_pass(0, *text_state)
            scatter_pass(col, *part_state)
        for direction in range(2):

            @pl.when(arrives(direction, distance))
            def multiply(direction=direction, distance=distance):
                group = col - distance * (1 - 2 * direction)
                scatter_start(group, grid_x[group], 0, *part_state)

        if distance > 1:
            pass_sums(distance - 1)

    pass_sums(cols - 1)

    rounded = scatter_end(0, *text_state)
    k_buf[0:padded_text, :] = rounded[:, 0:out_w]
    v_buf[0:padded_text, :] = rounded[:, out_w:]
    for group in range(cols):
        rounded = scatter_end(group, *part_state)
        per_col = rows * tokens
        base = padded_text + group * per_col
        k_buf[base : base + per_col, :] = rounded[:, out_w : 2 * out_w]
        v_buf[base : base + per_col, :] = rounded[:, 2 * out_w :]
        for dest in range(rows):
            q_buf[dest, group * tokens : (group + 1) * tokens, :] = rounded[
                dest * tokens : (dest + 1) * tokens, 0:out_w
            ]

    at = lax.broadcasted_iota(jnp.int32, (block, block), 0)
    source = lax.broadcasted_iota(jnp.int32, (block, block), 1)
    group = source // tokens
    token = source - group * tokens
    line = token // tile_w
    place = token - line * tile_w
    target = (line * cols + group) * tile_w + place
    permute = jnp.where(at == target, 0.125, 0.0).astype(jnp.bfloat16)
    keys = k_buf[...]
    vals = v_buf[...]
    position = lax.broadcasted_iota(jnp.int32, (1, keys.shape[0]), 1)
    valid = (position >= padded_text) | (position < len_ref[0])
    head_of = lax.broadcasted_iota(jnp.int32, (1, out_w), 1) // HD
    heads = out_w // HD
    o_copies = []
    for step in list(range(1, rows)) + [0]:
        peer = row_peer(step)
        queries = jnp.dot(permute, q_buf[peer], preferred_element_type=jnp.float32)
        by_head = [jnp.where(head_of == head, queries, 0.0) for head in range(heads)]
        stacked = jnp.concatenate(by_head, axis=0).astype(jnp.bfloat16)
        scores = lax.dot_general(
            stacked, keys, (((1,), (1,)), ((), ())), preferred_element_type=jnp.float32
        )
        scores = jnp.where(valid, scores, -jnp.inf)
        weight = jnp.exp(scores - jnp.max(scores, axis=-1, keepdims=True))
        total = jnp.sum(weight, axis=-1, keepdims=True)
        mixed = jnp.dot(weight.astype(jnp.bfloat16), vals, preferred_element_type=jnp.float32) / total
        result = mixed[0:block]
        for head in range(1, heads):
            result = jnp.where(head_of == head, mixed[head * block : (head + 1) * block], result)
        result = result.astype(jnp.bfloat16)
        if step == 0:
            recv_out[row] = result
        else:
            send_out[step - 1] = result
            copy = remote(
                send_out.at[step - 1],
                recv_out.at[row],
                o_send.at[step - 1],
                o_recv.at[step - 1],
                {"row": peer},
            )
            copy.start()
            o_copies.append(copy)
    for step in range(1, rows):
        source = lax.rem(row - step + rows, rows)
        remote(
            send_out.at[step - 1],
            recv_out.at[source],
            o_send.at[step - 1],
            o_recv.at[step - 1],
            {"row": row_peer(step)},
        ).wait_recv()
    for source in range(rows):
        out_ref[:, source * out_w : (source + 1) * out_w] = recv_out[source]
    for at, (down, right) in enumerate(SIDES):

        @pl.when(within(-down, -right))
        def sent(at=at, down=down, right=right):
            halo_copy(at, down, right).wait_send()

    for direction in range(2):
        for distance in range(1, cols):

            @pl.when(passes(direction, distance))
            def passed(direction=direction, distance=distance):
                z_copy(direction, distance, col - min(distance - 1, 1) * (1 - 2 * direction)).wait_send()

    for count, state in ((1, text_state), (cols, part_state)):
        own, first, first_in, hold, second, second_in, sems = state
        for group in range(count):
            for way in range(2):
                first_copy(group, way, sems, first, first_in).wait_send()
                second_copy(group, way, sems, second, second_in).wait_send()
    for copy in mod_copies + [weight_copy] + x_copies + o_copies:
        copy.wait_send()


def on_device_fast(
    rows, cols, latents, prompt_rows, peg_weight, modulation_weight, qkv_weight, text_len, timestep
):
    frames, tile_h, tile_w, width = latents.shape[1:]
    tokens = frames * tile_h * tile_w
    parts = 8
    narrow = width // parts
    pick, shift = (jnp.asarray(table, jnp.bfloat16) for table in halo_tables(frames, tile_h, tile_w, parts))
    temb = modulation_weight.shape[0]
    activation = jax.nn.silu(time_angles(timestep[0], temb)).astype(jnp.bfloat16)
    activation = jnp.broadcast_to(activation[None, :], (16, temb))
    depth, kinds, head_width = qkv_weight.shape
    out_w = head_width // rows
    by_kind = qkv_weight.transpose(1, 0, 2)
    text = prompt_rows.shape[1]
    padded_text = -(-text // 32) * 32
    block = tokens * cols
    group_rows = tokens * rows
    bf16, f32 = jnp.bfloat16, jnp.float32
    dma = pltpu.SemaphoreType.DMA
    all_rows = padded_text + group_rows * cols
    attended = pl.pallas_call(
        functools.partial(layer_kernel, (rows, cols, text, padded_text, tile_w)),
        out_shape=jax.ShapeDtypeStruct((block, head_width), bf16),
        in_specs=[pl.BlockSpec(memory_space=pltpu.SMEM)] + [pl.BlockSpec(memory_space=space) for space in (VMEM, VMEM, pltpu.HBM, VMEM, pltpu.HBM, VMEM, pltpu.HBM, pltpu.HBM)],
        out_specs=pl.BlockSpec(memory_space=VMEM),
        scratch_shapes=[
            VMEM(shift.shape, bf16),
            VMEM((text, width), bf16),
            VMEM(modulation_weight.shape, bf16),
            VMEM((4, 16, width // 2), bf16),
            VMEM((4, 16, width // 2), bf16),
            VMEM((64, narrow), bf16),
            VMEM((64, narrow), bf16),
            VMEM((tokens, width), bf16),
            dma((3 + 3 * rows,)),
            dma((8,)),
            dma((8,)),
            VMEM((cols, 1, modulation_weight.shape[1]), f32),
            VMEM((2, 1, width), f32),
            VMEM((rows, 2 * depth, kinds * out_w), bf16),
            VMEM((max(padded_text, tokens), width), bf16),
            VMEM((rows - 1, tokens, 2 * depth), bf16),
            VMEM((cols, group_rows, 2 * depth), bf16),
            VMEM((tokens, width), bf16),
            VMEM((1, padded_text, 2 * out_w), f32),
            VMEM((1, 2, 2, padded_text // 2, 2 * out_w), bf16),
            VMEM((1, 2, 2, padded_text // 2, 2 * out_w), bf16),
            VMEM((1, 2, padded_text // 2, 2 * out_w), f32),
            VMEM((1, 2, padded_text // 2, 2 * out_w), bf16),
            VMEM((1, 2, padded_text // 2, 2 * out_w), bf16),
            VMEM((cols, group_rows, kinds * out_w), f32),
            VMEM((cols, 2, 2, group_rows // 2, kinds * out_w), bf16),
            VMEM((cols, 2, 2, group_rows // 2, kinds * out_w), bf16),
            VMEM((cols, 2, group_rows // 2, kinds * out_w), f32),
            VMEM((cols, 2, group_rows // 2, kinds * out_w), bf16),
            VMEM((cols, 2, group_rows // 2, kinds * out_w), bf16),
            VMEM((rows, block, out_w), bf16),
            VMEM((all_rows, out_w), bf16),
            VMEM((all_rows, out_w), bf16),
            VMEM((rows - 1, block, out_w), bf16),
            VMEM((rows, block, out_w), bf16),
            dma((2,)),
            dma((cols - 1,)),
            dma((cols - 1,)),
            dma((rows - 1,)),
            dma((rows - 1,)),
            dma((2, cols - 1)),
            dma((2, cols - 1)),
            dma((4, 1, 2)),
            dma((4, cols, 2)),
            dma((rows - 1,)),
            dma((rows - 1,)),
        ],
        compiler_params=pltpu.CompilerParams(
            collective_id=0, has_side_effects=True, vmem_limit_bytes=58 * 1024 * 1024
        ),
    )(text_len, latents, pick, shift, peg_weight, prompt_rows[0], activation, modulation_weight, by_kind)
    return attended.reshape(1, frames, tile_h, tile_w * cols, head_width)


def solution(mesh):
    in_specs = (
        P("item", None, "row", "col", None),
        P("item", None, None),
        P(),
        P(None, "col"),
        P(("item", "row"), None, "col"),
        P("item"),
        P("item"),
    )
    out_specs = P("item", None, "row", None, "col")
    rows, cols, items = mesh.shape["row"], mesh.shape["col"], mesh.shape["item"]

    def on_device(*blocks):
        group = blocks[4].shape[2] // rows
        if items == 2 and rows == 4 and cols == 4 and group >= 128 and group % 128 == 0 and blocks[0].shape[1:4] == (2, 4, 4):
            return on_device_fast(rows, cols, *blocks)
        return on_device_general(*blocks)

    return jax.shard_map(
        on_device, mesh=mesh, in_specs=in_specs, out_specs=out_specs, check_vma=False
    )
```

```python
import functools
import math

import jax
import jax.numpy as jnp
import numpy as np
from jax import lax
from jax.experimental import pallas as pl
from jax.experimental.pallas import tpu as pltpu
from jax.sharding import PartitionSpec as P

HD = 64
MESH = pl.DeviceIdType.MESH
VMEM = pltpu.VMEM


def with_halo(block, sides, width):
    for axis, dim in sides:
        count = lax.axis_size(axis)
        forward = [(i, i + 1) for i in range(count - 1)]
        backward = [(target, source) for source, target in forward]
        low = lax.ppermute(
            lax.slice_in_dim(block, block.shape[dim] - width, None, axis=dim), axis, forward
        )
        high = lax.ppermute(lax.slice_in_dim(block, 0, width, axis=dim), axis, backward)
        block = jnp.concatenate([low, block, high], axis=dim)
    return block


def time_angles(step, count):
    half = count // 2
    freqs = jnp.exp(-math.log(10000.0) * jnp.arange(half, dtype=jnp.float32) / half)
    angle = step.astype(jnp.float32) * freqs
    return jnp.concatenate([jnp.cos(angle), jnp.sin(angle)])


def modulate(rows, shift, scale):
    values = rows.astype(jnp.float32)
    center = jnp.mean(values, axis=-1, keepdims=True)
    centered = values - center
    spread = jnp.mean(centered * centered, axis=-1, keepdims=True)
    return (centered * lax.rsqrt(spread + 1e-06) * (1.0 + scale) + shift).astype(jnp.bfloat16)


def absorb(carry, queries, key_rows, value_rows, valid):
    running_max, running_sum, weighted = carry
    count = key_rows.shape[0]
    heads = queries.shape[1]
    key_heads = key_rows.reshape(count, heads, HD)
    value_heads = value_rows.reshape(count, heads, HD)
    scores = (
        jnp.einsum("rhd,bhd->rhb", queries, key_heads, preferred_element_type=jnp.float32) * 0.125
    )
    if valid is not None:
        scores = jnp.where(valid[None, None, :], scores, -jnp.inf)
    newest = jnp.maximum(running_max, jnp.max(scores, axis=-1))
    weights = jnp.exp(scores - newest[..., None])
    shrink_by = jnp.exp(running_max - newest)
    running_sum = running_sum * shrink_by + jnp.sum(weights, axis=-1)
    weighted = weighted * shrink_by[..., None] + jnp.einsum(
        "rhb,bhd->rhd",
        weights.astype(jnp.bfloat16),
        value_heads,
        preferred_element_type=jnp.float32,
    )
    return (newest, running_sum, weighted)


def on_device_general(latents, prompt_rows, peg_weight, modulation_weight, qkv_weight, text_len, timestep):
    tile_h = latents.shape[2]
    tile_w = latents.shape[3]
    width = latents.shape[4]
    padded = with_halo(latents, (("row", 2), ("col", 3)), 1)
    summed = latents.astype(jnp.float32)
    for row_tap in range(3):
        for col_tap in range(3):
            summed = summed + padded[
                :, :, row_tap : row_tap + tile_h, col_tap : col_tap + tile_w, :
            ].astype(jnp.float32) * peg_weight[row_tap, col_tap].astype(jnp.float32)
    convolved = summed.astype(jnp.bfloat16)
    activation = jax.nn.silu(time_angles(timestep[0], modulation_weight.shape[0])).astype(
        jnp.bfloat16
    )
    own_columns = jnp.dot(
        activation[None, :], modulation_weight, preferred_element_type=jnp.float32
    )
    modulation = lax.all_gather(own_columns, "col", axis=1, tiled=True)[0]
    shift = modulation[:width]
    scale = modulation[width:]
    group_rows = lax.all_gather(modulate(convolved, shift, scale), "col", axis=3, tiled=True)
    frames = group_rows.shape[1]
    grid_w = group_rows.shape[3]
    flat_rows = group_rows.reshape(-1, width)
    row_count = flat_rows.shape[0]
    text_normed = modulate(prompt_rows[0], shift, scale)
    text_count = text_normed.shape[0]
    head_width = qkv_weight.shape[2]
    full_weight = lax.all_gather(qkv_weight, ("item", "row"), axis=0, tiled=True)
    latent_proj = jnp.einsum(
        "rd,dkc->rkc", flat_rows, full_weight, preferred_element_type=jnp.float32
    )
    text_proj = jnp.einsum(
        "rd,dkc->rkc", text_normed, full_weight, preferred_element_type=jnp.float32
    )
    latent_qkv = latent_proj.astype(jnp.bfloat16)
    text_qkv = text_proj.astype(jnp.bfloat16)
    heads = head_width // HD
    queries = latent_qkv[:, 0, :].reshape(row_count, heads, HD)
    local_keys = latent_qkv[:, 1, :]
    local_values = latent_qkv[:, 2, :]
    text_valid = jnp.arange(text_count, dtype=jnp.int32) < text_len[0]
    start_carry = (
        jnp.full((row_count, heads), -jnp.inf, jnp.float32),
        jnp.zeros((row_count, heads), jnp.float32),
        jnp.zeros((row_count, heads, HD), jnp.float32),
    )
    text_carry = absorb(start_carry, queries, text_qkv[:, 1, :], text_qkv[:, 2, :], text_valid)
    key_rows = lax.all_gather(local_keys, "row", axis=0, tiled=True)
    value_rows = lax.all_gather(local_values, "row", axis=0, tiled=True)
    total_rows = key_rows.shape[0]
    block_count = total_rows // row_count

    def one_block(state, pair):
        return (absorb(state, queries, pair[0], pair[1], None), None)

    state, unused = lax.scan(
        one_block,
        text_carry,
        (
            key_rows.reshape(block_count, row_count, head_width),
            value_rows.reshape(block_count, row_count, head_width),
        ),
    )
    running_max, running_sum, weighted = state
    attended = (weighted / running_sum[..., None]).astype(jnp.bfloat16)
    return attended.reshape(1, frames, tile_h, grid_w, head_width)


def centered_rows(values):
    center = jnp.mean(values, axis=-1, keepdims=True)
    centered = values - center
    spread = jnp.mean(centered * centered, axis=-1, keepdims=True)
    return centered * lax.rsqrt(spread + 1e-06)


SIDES = ((-1, 0), (1, 0), (0, -1), (0, 1), (-1, -1), (-1, 1), (1, -1), (1, 1))


def halo_tables(frames, tile_h, tile_w, parts):
    tokens = frames * tile_h * tile_w
    edge = frames * tile_h

    def token(f, h, w):
        return (f * tile_h + h) * tile_w + w

    pick = np.zeros((1 + parts, 64, tokens), np.float32)
    shift = np.zeros((parts, 8 * tokens, tokens + 8 * edge + 64), np.float32)
    last_h, last_w = tile_h - 1, tile_w - 1
    for at, (down, right) in enumerate(SIDES):
        h_from = last_h if down < 0 else 0
        w_from = last_w if right < 0 else 0
        for f in range(frames):
            if at < 4:
                for k in range(tile_h):
                    source = token(f, h_from, k) if down else token(f, k, w_from)
                    pick[0, at * edge + f * tile_h + k, source] = 1
            else:
                for part in range(parts):
                    pick[1 + part, (at - 4) * 16 + part * frames + f, token(f, h_from, w_from)] = 1
        for part in range(parts):
            upper = part // (parts // 2)
            for f in range(frames):
                for h in range(tile_h):
                    for w in range(tile_w):
                        y, x = h + down, w + right
                        out_y = -1 if y < 0 else (1 if y > last_h else 0)
                        out_x = -1 if x < 0 else (1 if x > last_w else 0)
                        if out_y == 0 and out_x == 0:
                            source = token(f, y, x)
                        else:
                            slot = SIDES.index((out_y, out_x))
                            if slot < 4:
                                k = x if out_y else y
                                source = tokens + slot * 2 * edge + upper * edge + f * tile_h + k
                            else:
                                source = tokens + 8 * edge + (slot - 4) * 16 + part * frames + f
                        shift[part, at * tokens + token(f, h, w), source] = 1
    return pick, shift


def layer_kernel(
    sizes,
    len_ref,
    tile_ref,
    pick_ref,
    shift_hbm,
    peg_ref,
    prompt_hbm,
    act_ref,
    mod_hbm,
    weight_hbm,
    out_ref,
    shift_ref,
    prompt_ref,
    mod_ref,
    side_send,
    side_in,
    corner_send,
    corner_in,
    conv,
    local_sems,
    halo_send,
    halo_recv,
    mod_buf,
    affine,
    weights,
    text_in,
    send_x,
    grid_x,
    tile_buf,
    own_text,
    text_first,
    text_first_in,
    text_hold,
    text_second,
    text_second_in,
    own_part,
    part_first,
    part_first_in,
    part_hold,
    part_second,
    part_second_in,
    q_buf,
    k_buf,
    v_buf,
    send_out,
    recv_out,
    w_sems,
    mod_send,
    mod_recv,
    x_send,
    x_recv,
    z_send,
    z_recv,
    t_sems,
    p_sems,
    o_send,
    o_recv,
):
    rows, cols, text, padded_text, tile_w = sizes
    tokens, width = tile_buf.shape
    depth = weight_hbm.shape[1]
    out_w = weight_hbm.shape[2] // rows
    block = tokens * cols
    item = lax.axis_index("item")
    row = lax.axis_index("row")
    col = lax.axis_index("col")

    def row_peer(step):
        return lax.rem(row + step, rows)

    def col_peer(step):
        return lax.rem(col + step, cols)

    def remote(src, dst, send, recv, where):
        return pltpu.make_async_remote_copy(
            src_ref=src, dst_ref=dst, send_sem=send, recv_sem=recv, device_id=where, device_id_type=MESH
        )

    prompt_copy = pltpu.make_async_copy(prompt_hbm, prompt_ref, local_sems.at[0])
    mod_copy = pltpu.make_async_copy(mod_hbm, mod_ref, local_sems.at[1])
    shift_copy = pltpu.make_async_copy(shift_hbm, shift_ref, local_sems.at[2])
    stage_copies = []
    for kind in range(3):
        for dest in range(rows):
            stage_copies.append(
                pltpu.make_async_copy(
                    weight_hbm.at[kind, :, dest * out_w : (dest + 1) * out_w],
                    weights.at[dest, 0:depth, kind * out_w : (kind + 1) * out_w],
                    local_sems.at[3 + kind * rows + dest],
                )
            )
    mod_copy.start()
    for copy in stage_copies:
        copy.start()
    prompt_copy.start()
    shift_copy.start()
    side_in[...] = jnp.zeros_like(side_in)
    corner_in[...] = jnp.zeros_like(corner_in)

    def within(down, right):
        r, c = row + down, col + right
        return (r >= 0) & (r < rows) & (c >= 0) & (c < cols)

    near = (row + 1 - 2 * lax.rem(row, 2), row + 2 - 4 * lax.div(row, 2))
    across = 3 - row

    def first_copy(group, way, sems, first, first_in):
        return remote(
            first.at[group, way],
            first_in.at[group, way],
            sems.at[0, group, way],
            sems.at[1, group, way],
            {"row": near[way]},
        )

    def second_copy(group, way, sems, second, second_in):
        return remote(
            second.at[group, way],
            second_in.at[group, way],
            sems.at[2, group, way],
            sems.at[3, group, way],
            {"row": near[1 - way]},
        )

    def scatter_start(group, values, lane, own, first, first_in, hold, second, second_in, sems):
        def product(dest):
            return jnp.dot(values, weights[dest, :, lane:], preferred_element_type=jnp.float32)

        half = values.shape[0] // 2
        far = product(across)
        for way in range(2):
            first[group, way, 1] = far[way * half : (way + 1) * half].astype(jnp.bfloat16)
        for way in range(2):
            part = product(near[way])
            first[group, way, 0] = part[way * half : (way + 1) * half].astype(jnp.bfloat16)
            hold[group, 1 - way] = part[(1 - way) * half : (2 - way) * half]
            first_copy(group, way, sems, first, first_in).start()
        own[group] = product(row)

    def scatter_pass(group, own, first, first_in, hold, second, second_in, sems):
        half = hold.shape[2]
        for way in range(2):
            first_copy(group, way, sems, first, first_in).wait_recv()
            second[group, way] = (
                hold[group, way] + first_in[group, way, 1].astype(jnp.float32)
            ).astype(jnp.bfloat16)
            second_copy(group, way, sems, second, second_in).start()
            lines = slice(way * half, (way + 1) * half)
            own[group, lines] = own[group, lines] + first_in[group, way, 0].astype(jnp.float32)

    def scatter_end(group, own, first, first_in, hold, second, second_in, sems):
        sums = []
        half = hold.shape[2]
        for way in range(2):
            second_copy(group, way, sems, second, second_in).wait_recv()
            sums.append(
                own[group, way * half : (way + 1) * half] + second_in[group, way].astype(jnp.float32)
            )
        return jnp.concatenate(sums, axis=0).astype(jnp.bfloat16)

    text_state = (own_text, text_first, text_first_in, text_hold, text_second, text_second_in, t_sems)
    part_state = (own_part, part_first, part_first_in, part_hold, part_second, part_second_in, p_sems)

    barrier = pltpu.get_barrier_semaphore()
    for down, right in SIDES[4:]:

        @pl.when(within(down, right))
        def greet(down=down, right=right):
            pl.semaphore_signal(
                barrier, inc=1, device_id={"row": row + down, "col": col + right}, device_id_type=MESH
            )

    pl.semaphore_signal(barrier, inc=1, device_id={"item": 1 - item}, device_id_type=MESH)
    for step in range(1, rows):
        pl.semaphore_signal(barrier, inc=1, device_id={"row": row_peer(step)}, device_id_type=MESH)
    for step in range(1, cols):
        pl.semaphore_signal(barrier, inc=1, device_id={"col": col_peer(step)}, device_id_type=MESH)

    pieces = [
        tile_ref[0, f, h].astype(jnp.float32)
        for f in range(tile_ref.shape[1])
        for h in range(tile_ref.shape[2])
    ]
    tile_buf[...] = jnp.concatenate(pieces, axis=0).astype(jnp.bfloat16)
    tile = tile_buf[...]
    wide = side_in.shape[2]
    narrow = corner_in.shape[1]
    edge = side_in.shape[1] // 2
    picked = jnp.dot(pick_ref[0, 0 : 4 * edge], tile, preferred_element_type=jnp.float32)
    for side in range(4):
        lines = picked[side * edge : (side + 1) * edge]
        side_send[side] = jnp.concatenate([lines[:, :wide], lines[:, wide:]], axis=0).astype(jnp.bfloat16)
    corners = jnp.zeros((corner_in.shape[0], narrow), jnp.float32)
    for part in range(width // narrow):
        corners = corners + jnp.dot(
            pick_ref[1 + part],
            tile[:, part * narrow : (part + 1) * narrow],
            preferred_element_type=jnp.float32,
        )
    corner_send[...] = corners.astype(jnp.bfloat16)

    def halo_copy(at, down, right):
        if at < 4:
            src, dst = side_send.at[at], side_in.at[at]
        else:
            lines = pl.ds((at - 4) * 16, 16)
            src, dst = corner_send.at[lines, :], corner_in.at[lines, :]
        return remote(
            src, dst, halo_send.at[at], halo_recv.at[at], {"row": row - down, "col": col - right}
        )

    mod_copy.wait()
    own_columns = jnp.dot(act_ref[...], mod_ref[...], preferred_element_type=jnp.float32)
    mod_buf[col] = own_columns[0:1, :]
    beside_rows = (row + rows - 1) // rows + (2 * rows - 2 - row) // rows
    beside_cols = (col + cols - 1) // cols + (2 * cols - 2 - col) // cols
    pl.semaphore_wait(barrier, rows + cols - 1 + beside_rows * beside_cols)
    for at, (down, right) in enumerate(SIDES):

        @pl.when(within(-down, -right))
        def send(at=at, down=down, right=right):
            halo_copy(at, down, right).start()

    mod_copies = []
    for step in range(1, cols):
        copy = remote(
            mod_buf.at[col],
            mod_buf.at[col],
            mod_send.at[step - 1],
            mod_recv.at[step - 1],
            {"col": col_peer(step)},
        )
        copy.start()
        mod_copies.append(copy)
    for copy in stage_copies:
        copy.wait()
    weight_copy = remote(
        weights.at[:, 0:depth, :],
        weights.at[:, pl.ds(depth, depth), :],
        w_sems.at[0],
        w_sems.at[1],
        {"item": 1 - item},
    )
    weight_copy.start()
    for at, (down, right) in enumerate(SIDES):

        @pl.when(within(down, right))
        def receive(at=at, down=down, right=right):
            halo_copy(at, down, right).wait_recv()

    shift_copy.wait()
    for part in range(width // narrow):
        lanes = slice(part * narrow, (part + 1) * narrow)
        upper, start = divmod(part * narrow, wide)
        pieces = [tile[:, lanes]]
        for side in range(4):
            pieces.append(side_in[side, :, start : start + narrow])
        pieces.append(corner_in[...])
        moved = jnp.dot(
            shift_ref[part], jnp.concatenate(pieces, axis=0), preferred_element_type=jnp.float32
        )
        own = tile[:, lanes].astype(jnp.float32)
        taps = [peg_ref[a, :, lanes].astype(jnp.float32) for a in range(3)]
        summed = own + own * taps[1][1:2]
        for at, (down, right) in enumerate(SIDES):
            summed = summed + moved[at * tokens : (at + 1) * tokens] * taps[down + 1][right + 1 : right + 2]
        conv[:, lanes] = summed.astype(jnp.bfloat16)
    tile_normal = centered_rows(conv[...].astype(jnp.float32))
    for step in range(1, cols):
        remote(
            mod_buf.at[col],
            mod_buf.at[lax.rem(col - step + cols, cols)],
            mod_send.at[step - 1],
            mod_recv.at[step - 1],
            {"col": col_peer(step)},
        ).wait_recv()
    half = cols // 2
    piece = mod_buf.shape[2]
    for part in range(half):
        affine[0, :, part * piece : (part + 1) * piece] = mod_buf[part]
        affine[1, :, part * piece : (part + 1) * piece] = 1.0 + mod_buf[half + part]

    def depth_slices(dest):
        first = (item * rows + dest) * depth
        second = ((1 - item) * rows + dest) * depth
        return (pl.multiple_of(first, depth), pl.multiple_of(second, depth))

    text_in[0:tokens, :] = (tile_normal * affine[1] + affine[0]).astype(jnp.bfloat16)
    x_copies = []
    for step in range(1, rows):
        peer = row_peer(step)
        for order, start in enumerate(depth_slices(peer)):
            send_x[step - 1, :, order * depth : (order + 1) * depth] = text_in[
                0:tokens, pl.ds(start, depth)
            ]
        copy = remote(
            send_x.at[step - 1],
            grid_x.at[col, pl.ds(pl.multiple_of(row * tokens, tokens), tokens), :],
            x_send.at[step - 1],
            x_recv.at[step - 1],
            {"row": peer},
        )
        copy.start()
        x_copies.append(copy)
    own_slices = depth_slices(row)
    for order, start in enumerate(own_slices):
        grid_x[
            col, pl.ds(pl.multiple_of(row * tokens, tokens), tokens), order * depth : (order + 1) * depth
        ] = text_in[0:tokens, pl.ds(start, depth)]

    for step in range(1, rows):
        source = lax.rem(row - step + rows, rows)
        remote(
            send_x.at[step - 1],
            grid_x.at[col, pl.ds(pl.multiple_of(source * tokens, tokens), tokens), :],
            x_send.at[step - 1],
            x_recv.at[step - 1],
            {"row": row_peer(step)},
        ).wait_recv()
    def z_copy(direction, distance, source):
        sign = 1 - 2 * direction
        return remote(
            grid_x.at[source],
            grid_x.at[source],
            z_send.at[direction, distance - 1],
            z_recv.at[direction, distance - 1],
            {"col": col + sign * max(1, distance - 1)},
        )

    def passes(direction, distance):
        sign = 1 - 2 * direction
        home = col - min(distance - 1, 1) * sign
        target = col + max(1, distance - 1) * sign
        return (home >= 0) & (home < cols) & (target >= 0) & (target < cols)

    def arrives(direction, distance):
        home = col - distance * (1 - 2 * direction)
        return (home >= 0) & (home < cols)

    def pass_on(distance):
        for direction in range(2):

            @pl.when(passes(direction, distance))
            def start(direction=direction):
                z_copy(direction, distance, col - min(distance - 1, 1) * (1 - 2 * direction)).start()

    pass_on(1)

    def pass_sums(distance):
        for direction in range(2):

            @pl.when(arrives(direction, distance))
            def forward(direction=direction):
                scatter_pass(col - distance * (1 - 2 * direction), *part_state)

    def text_part():
        prompt_copy.wait()
        text_stats = []
        for start_row in range(0, padded_text, 16):
            count = min(16, text - start_row)
            if count <= 0:
                continue
            values = prompt_ref[start_row : start_row + count, :].astype(jnp.float32)
            center = jnp.mean(values, axis=-1, keepdims=True)
            centered = values - center
            spread = lax.rsqrt(jnp.mean(centered * centered, axis=-1, keepdims=True) + 1e-06)
            text_stats.append((center, spread))

        scale_pieces = [affine[1, :, pl.ds(start, depth)] for start in own_slices]
        shift_pieces = [affine[0, :, pl.ds(start, depth)] for start in own_slices]
        for start_row in range(0, padded_text, 16):
            count = min(16, text - start_row)
            if count <= 0:
                text_in[start_row : start_row + 16, 0 : 2 * depth] = jnp.zeros((16, 2 * depth), jnp.bfloat16)
                continue
            center, spread = text_stats[start_row // 16]
            for order, start in enumerate(own_slices):
                part = prompt_ref[start_row : start_row + count, pl.ds(start, depth)].astype(jnp.float32)
                normed = (part - center) * spread * scale_pieces[order] + shift_pieces[order]
                if count < 16:
                    normed = jnp.concatenate([normed, jnp.zeros((16 - count, depth), jnp.float32)], axis=0)
                text_in[start_row : start_row + 16, order * depth : (order + 1) * depth] = normed.astype(
                    jnp.bfloat16
                )
        text_values = text_in[:, 0 : 2 * depth]
        scatter_start(0, text_values, out_w, *text_state)

    weight_copy.wait_recv()
    scatter_start(col, grid_x[col], 0, *part_state)
    for distance in range(1, cols):
        for direction in range(2):

            @pl.when(arrives(direction, distance))
            def landed(direction=direction, distance=distance):
                z_copy(direction, distance, col - distance * (1 - 2 * direction)).wait_recv()

        if distance == 1:
            pass_on(2)
            pass_on(3)
            scatter_pass(col, *part_state)
        for direction in range(2):

            @pl.when(arrives(direction, distance))
            def multiply(direction=direction, distance=distance):
                group = col - distance * (1 - 2 * direction)
                scatter_start(group, grid_x[group], 0, *part_state)

        if distance == 1:
            text_part()
        else:
            pass_sums(distance - 1)
        if distance == 2:
            scatter_pass(0, *text_state)

    pass_sums(cols - 1)

    rounded = scatter_end(0, *text_state)
    k_buf[0:padded_text, :] = rounded[:, 0:out_w]
    v_buf[0:padded_text, :] = rounded[:, out_w:]
    for group in range(cols):
        rounded = scatter_end(group, *part_state)
        per_col = rows * tokens
        base = padded_text + group * per_col
        k_buf[base : base + per_col, :] = rounded[:, out_w : 2 * out_w]
        v_buf[base : base + per_col, :] = rounded[:, 2 * out_w :]
        for dest in range(rows):
            q_buf[dest, group * tokens : (group + 1) * tokens, :] = rounded[
                dest * tokens : (dest + 1) * tokens, 0:out_w
            ]

    at = lax.broadcasted_iota(jnp.int32, (block, block), 0)
    source = lax.broadcasted_iota(jnp.int32, (block, block), 1)
    group = source // tokens
    token = source - group * tokens
    line = token // tile_w
    place = token - line * tile_w
    target = (line * cols + group) * tile_w + place
    permute = jnp.where(at == target, 0.125, 0.0).astype(jnp.bfloat16)
    keys = k_buf[...]
    vals = v_buf[...]
    position = lax.broadcasted_iota(jnp.int32, (1, keys.shape[0]), 1)
    valid = (position >= padded_text) | (position < len_ref[0])
    head_of = lax.broadcasted_iota(jnp.int32, (1, out_w), 1) // HD
    heads = out_w // HD
    o_copies = []
    for step in list(range(1, rows)) + [0]:
        peer = row_peer(step)
        queries = jnp.dot(permute, q_buf[peer], preferred_element_type=jnp.float32)
        by_head = [jnp.where(head_of == head, queries, 0.0) for head in range(heads)]
        stacked = jnp.concatenate(by_head, axis=0).astype(jnp.bfloat16)
        scores = lax.dot_general(
            stacked, keys, (((1,), (1,)), ((), ())), preferred_element_type=jnp.float32
        )
        scores = jnp.where(valid, scores, -jnp.inf)
        weight = jnp.exp(scores - jnp.max(scores, axis=-1, keepdims=True))
        total = jnp.sum(weight, axis=-1, keepdims=True)
        mixed = jnp.dot(weight.astype(jnp.bfloat16), vals, preferred_element_type=jnp.float32) / total
        result = mixed[0:block]
        for head in range(1, heads):
            result = jnp.where(head_of == head, mixed[head * block : (head + 1) * block], result)
        result = result.astype(jnp.bfloat16)
        if step == 0:
            recv_out[row] = result
        else:
            send_out[step - 1] = result
            copy = remote(
                send_out.at[step - 1],
                recv_out.at[row],
                o_send.at[step - 1],
                o_recv.at[step - 1],
                {"row": peer},
            )
            copy.start()
            o_copies.append(copy)
    for step in range(1, rows):
        source = lax.rem(row - step + rows, rows)
        remote(
            send_out.at[step - 1],
            recv_out.at[source],
            o_send.at[step - 1],
            o_recv.at[step - 1],
            {"row": row_peer(step)},
        ).wait_recv()
    for source in range(rows):
        out_ref[:, source * out_w : (source + 1) * out_w] = recv_out[source]
    for at, (down, right) in enumerate(SIDES):

        @pl.when(within(-down, -right))
        def sent(at=at, down=down, right=right):
            halo_copy(at, down, right).wait_send()

    for direction in range(2):
        for distance in range(1, cols):

            @pl.when(passes(direction, distance))
            def passed(direction=direction, distance=distance):
                z_copy(direction, distance, col - min(distance - 1, 1) * (1 - 2 * direction)).wait_send()

    for count, state in ((1, text_state), (cols, part_state)):
        own, first, first_in, hold, second, second_in, sems = state
        for group in range(count):
            for way in range(2):
                first_copy(group, way, sems, first, first_in).wait_send()
                second_copy(group, way, sems, second, second_in).wait_send()
    for copy in mod_copies + [weight_copy] + x_copies + o_copies:
        copy.wait_send()


def on_device_fast(
    rows, cols, latents, prompt_rows, peg_weight, modulation_weight, qkv_weight, text_len, timestep
):
    frames, tile_h, tile_w, width = latents.shape[1:]
    tokens = frames * tile_h * tile_w
    parts = 8
    narrow = width // parts
    pick, shift = (jnp.asarray(table, jnp.bfloat16) for table in halo_tables(frames, tile_h, tile_w, parts))
    temb = modulation_weight.shape[0]
    activation = jax.nn.silu(time_angles(timestep[0], temb)).astype(jnp.bfloat16)
    activation = jnp.broadcast_to(activation[None, :], (16, temb))
    depth, kinds, head_width = qkv_weight.shape
    out_w = head_width // rows
    by_kind = qkv_weight.transpose(1, 0, 2)
    text = prompt_rows.shape[1]
    padded_text = -(-text // 32) * 32
    block = tokens * cols
    group_rows = tokens * rows
    bf16, f32 = jnp.bfloat16, jnp.float32
    dma = pltpu.SemaphoreType.DMA
    all_rows = padded_text + group_rows * cols
    attended = pl.pallas_call(
        functools.partial(layer_kernel, (rows, cols, text, padded_text, tile_w)),
        out_shape=jax.ShapeDtypeStruct((block, head_width), bf16),
        in_specs=[pl.BlockSpec(memory_space=pltpu.SMEM)] + [pl.BlockSpec(memory_space=space) for space in (VMEM, VMEM, pltpu.HBM, VMEM, pltpu.HBM, VMEM, pltpu.HBM, pltpu.HBM)],
        out_specs=pl.BlockSpec(memory_space=VMEM),
        scratch_shapes=[
            VMEM(shift.shape, bf16),
            VMEM((text, width), bf16),
            VMEM(modulation_weight.shape, bf16),
            VMEM((4, 16, width // 2), bf16),
            VMEM((4, 16, width // 2), bf16),
            VMEM((64, narrow), bf16),
            VMEM((64, narrow), bf16),
            VMEM((tokens, width), bf16),
            dma((3 + 3 * rows,)),
            dma((8,)),
            dma((8,)),
            VMEM((cols, 1, modulation_weight.shape[1]), f32),
            VMEM((2, 1, width), f32),
            VMEM((rows, 2 * depth, kinds * out_w), bf16),
            VMEM((max(padded_text, tokens), width), bf16),
            VMEM((rows - 1, tokens, 2 * depth), bf16),
            VMEM((cols, group_rows, 2 * depth), bf16),
            VMEM((tokens, width), bf16),
            VMEM((1, padded_text, 2 * out_w), f32),
            VMEM((1, 2, 2, padded_text // 2, 2 * out_w), bf16),
            VMEM((1, 2, 2, padded_text // 2, 2 * out_w), bf16),
            VMEM((1, 2, padded_text // 2, 2 * out_w), f32),
            VMEM((1, 2, padded_text // 2, 2 * out_w), bf16),
            VMEM((1, 2, padded_text // 2, 2 * out_w), bf16),
            VMEM((cols, group_rows, kinds * out_w), f32),
            VMEM((cols, 2, 2, group_rows // 2, kinds * out_w), bf16),
            VMEM((cols, 2, 2, group_rows // 2, kinds * out_w), bf16),
            VMEM((cols, 2, group_rows // 2, kinds * out_w), f32),
            VMEM((cols, 2, group_rows // 2, kinds * out_w), bf16),
            VMEM((cols, 2, group_rows // 2, kinds * out_w), bf16),
            VMEM((rows, block, out_w), bf16),
            VMEM((all_rows, out_w), bf16),
            VMEM((all_rows, out_w), bf16),
            VMEM((rows - 1, block, out_w), bf16),
            VMEM((rows, block, out_w), bf16),
            dma((2,)),
            dma((cols - 1,)),
            dma((cols - 1,)),
            dma((rows - 1,)),
            dma((rows - 1,)),
            dma((2, cols - 1)),
            dma((2, cols - 1)),
            dma((4, 1, 2)),
            dma((4, cols, 2)),
            dma((rows - 1,)),
            dma((rows - 1,)),
        ],
        compiler_params=pltpu.CompilerParams(
            collective_id=0, has_side_effects=True, vmem_limit_bytes=58 * 1024 * 1024
        ),
    )(text_len, latents, pick, shift, peg_weight, prompt_rows[0], activation, modulation_weight, by_kind)
    return attended.reshape(1, frames, tile_h, tile_w * cols, head_width)


def solution(mesh):
    in_specs = (
        P("item", None, "row", "col", None),
        P("item", None, None),
        P(),
        P(None, "col"),
        P(("item", "row"), None, "col"),
        P("item"),
        P("item"),
    )
    out_specs = P("item", None, "row", None, "col")
    rows, cols, items = mesh.shape["row"], mesh.shape["col"], mesh.shape["item"]

    def on_device(*blocks):
        group = blocks[4].shape[2] // rows
        if items == 2 and rows == 4 and cols == 4 and group >= 128 and group % 128 == 0 and blocks[0].shape[1:4] == (2, 4, 4):
            return on_device_fast(rows, cols, *blocks)
        return on_device_general(*blocks)

    return jax.shard_map(
        on_device, mesh=mesh, in_specs=in_specs, out_specs=out_specs, check_vma=False
    )
```
